32 devices in a mesh: dp: 8 (over z, y), mp: 4 (over x, core).
Axes of the slice: x: 2, y: 2, z: 4, core: 2. Of those that a mesh axis runs over, the one named last changes fastest.
Arguments:
- tokens: bfloat16 [16384, 768], P('dp'), may hold values from -6 to 6
- cotangent: bfloat16 [16384, 768], P('dp'), may hold values from -6 to 6
- seq_lengths: int32 [32], replicated, may hold values from 1 to 768, as said below
- seq_bin: int32 [32], replicated, may hold values from 0 to 15, as said below
- qkv_weight: bfloat16 [3, 768, 768], P(None, 'dp', 'mp'), may hold values from -0.21875 to 0.21875
- out_weight: bfloat16 [768, 768], P('mp', 'dp'), may hold values from -0.875 to 0.875
- up_weight: bfloat16 [768, 3072], P('dp', 'mp'), may hold values from -0.21875 to 0.21875
- down_weight: bfloat16 [3072, 768], P('mp', 'dp'), may hold values from -0.109375 to 0.109375
- norm_gains: float32 [2, 768], replicated, may hold values from 0.5 to 1.5
- shared_biases: float32 [4, 768], replicated, may hold values from -1.8 to 1.8
- head_biases: float32 [2, 768], P(None, 'mp'), may hold values from -1.8 to 1.8
- unit_bias: float32 [3072], P('mp'), may hold values from -0.6 to 0.6
- qkv_moment: float32 [3, 768, 768], P(None, 'dp', 'mp'), may hold values from -768 to 768
- out_moment: float32 [768, 768], P('mp', 'dp'), may hold values from -192 to 192
- up_moment: float32 [768, 3072], P('dp', 'mp'), may hold values from -128 to 128
- down_moment: float32 [3072, 768], P('mp', 'dp'), may hold values from -320 to 320
- gain_moment: float32 [2, 768], replicated, may hold values from -640 to 640
- bias_moment: float32 [4, 768], replicated, may hold values from -640 to 640
- head_moment: float32 [2, 768], P(None, 'mp'), may hold values from -640 to 640
- unit_moment: float32 [3072], P('mp'), may hold values from -128 to 128
Outputs:
- block_out: float32 [16384, 768], P('dp')
- input_grad: float32 [16384, 768], P('dp')
- qkv_moment_next: float32 [3, 768, 768], P(None, 'dp', 'mp')
- qkv_next: float32 [3, 768, 768], P(None, 'dp', 'mp')
- out_moment_next: float32 [768, 768], P('mp', 'dp')
- out_next: float32 [768, 768], P('mp', 'dp')
- up_moment_next: float32 [768, 3072], P('dp', 'mp')
- up_next: float32 [768, 3072], P('dp', 'mp')
- down_moment_next: float32 [3072, 768], P('mp', 'dp')
- down_next: float32 [3072, 768], P('mp', 'dp')
- gain_moment_next: float32 [2, 768], replicated
- gain_next: float32 [2, 768], replicated
- bias_moment_next: float32 [4, 768], replicated
- bias_next: float32 [4, 768], replicated
- head_moment_next: float32 [2, 768], P(None, 'mp')
- head_next: float32 [2, 768], P(None, 'mp')
- unit_moment_next: float32 [3072], P('mp')
- unit_next: float32 [3072], P('mp')
The draws below stay inside these ranges and needn't reach their ends.
Inputs may be any that keep to these rules, and one draw needn't show every extreme that they name: `seq_lengths`: one sequence is exactly 768 long. Sequence s lies in bin seq_bin[s]; bin b (rows b * 1024 to (b + 1) * 1024 - 1 of tokens, on index b // 2 of dp) holds exactly two sequences, packed from its first row in the order of their indices; their lengths add up to 1024 or less, and the rows after them are unused.
All inputs are finite; a program needn't handle non-finite values.
Results may differ from the reference program's by a relative error of at most 0.024.
Values may be sent and summed in bfloat16 or wider, within the bound.
No kernel may reach another device: no remote copies, remote signals or barrier semaphores. Data moves between devices by JAX's collectives and lax.ppermute only.
A program may use at most 192 MiB of HBM per device.

```python
import math
import jax
import jax.numpy as jnp
from jax import lax

D = 768
HEAD_DIM = 64
FF = 3072
SLOTS = 1024
NS_STEPS = 5
MAXLEN = 768
BINS = 16
SEQS = 32
TOKENS = 16384
N_MP = 4


def bin_layout(key):
    count = SEQS // 2
    first_key, second_key, third_key, fourth_key = jax.random.split(key, 4)
    permuted = jax.random.permutation(first_key, SEQS)
    seq_bin = (permuted // 2).astype(jnp.int32)
    shortest = max(SLOTS // 8, 1)
    first = jax.random.randint(second_key, (count,), shortest, MAXLEN + 1)
    forced = jax.random.randint(fourth_key, (), 0, count)
    first = jnp.where(jnp.arange(count) == forced, MAXLEN, first)
    room = jnp.minimum(MAXLEN, SLOTS - first)
    fraction = jax.random.randint(third_key, (count,), 0, 1 << 16)
    second = 1 + fraction * room // (1 << 16)
    inverse = jnp.argsort(permuted)
    leader = jnp.minimum(inverse[0::2], inverse[1::2])
    is_leader = jnp.arange(SEQS) == leader[seq_bin]
    lengths = jnp.where(is_leader, first[seq_bin], second[seq_bin])
    return (lengths.astype(jnp.int32), seq_bin)


def draw_seq_lengths(key, part):
    shared = bin_layout(key)
    return shared[0]


def draw_seq_bin(key, part):
    shared = bin_layout(key)
    return shared[1]


def block_levels(own_key, extent, shards, least, high):
    level = 1.0
    for position, shards_of in shards:
        steps = jax.random.uniform(jax.random.fold_in(jax.random.fold_in(own_key, 6), position), (shards_of,), jnp.float32, least / len(shards), high / len(shards))
        level = level * jnp.repeat(jnp.exp(steps), extent[position] // shards_of).reshape((-1,) + (1,) * (len(extent) - 1 - position))
    return level


def centred(rng, shape, scale, reach, pieces=(), kind=jnp.bfloat16):
    entries = scale * jax.random.normal(rng, shape, jnp.float32)
    if pieces:
        entries = entries * block_levels(rng, shape, pieces, -0.22, 0.18)
    return jnp.clip(entries, -reach, reach).astype(kind)


def setup_inputs(seed: int = 0) -> dict:
    seeds = jax.random.split(jax.random.key(seed), 21)
    return {
        "tokens": centred(seeds[0], (TOKENS, D), 1.0, 6.0, ((0, 8),)),
        "cotangent": centred(seeds[1], (TOKENS, D), 1.0, 6.0, ((0, 8),)),
        "seq_lengths": draw_seq_lengths(jax.random.fold_in(seeds[20], 71), 0),
        "seq_bin": draw_seq_bin(jax.random.fold_in(seeds[20], 71), 0),
        "qkv_weight": centred(seeds[4], (3, D, D), D ** -0.5, 0.21875, ((1, 8), (2, 4))),
        "out_weight": centred(seeds[5], (D, D), (D // 16) ** -0.5, 0.875, ((0, 4), (1, 8))),
        "up_weight": centred(seeds[6], (D, FF), D ** -0.5, 0.21875, ((0, 8), (1, 4))),
        "down_weight": centred(seeds[7], (FF, D), FF ** -0.5, 0.109375, ((0, 4), (1, 8))),
        "norm_gains": jnp.clip(1.0 + 0.1 * jax.random.normal(seeds[8], (2, D), jnp.float32), 0.5, 1.5),
        "shared_biases": centred(seeds[9], (4, D), 0.3, 1.8, (), jnp.float32),
        "head_biases": centred(seeds[10], (2, D), 0.3, 1.8, ((1, 4),), jnp.float32),
        "unit_bias": centred(seeds[11], (FF,), 0.1, 0.6, ((0, 4),), jnp.float32),
        "qkv_moment": centred(seeds[12], (3, D, D), (1.2 * TOKENS ** 0.5), 768.0, ((1, 8), (2, 4)), jnp.float32),
        "out_moment": centred(seeds[13], (D, D), (0.3 * TOKENS ** 0.5), 192.0, ((0, 4), (1, 8)), jnp.float32),
        "up_moment": centred(seeds[14], (D, FF), (0.2 * TOKENS ** 0.5), 128.0, ((0, 8), (1, 4)), jnp.float32),
        "down_moment": centred(seeds[15], (FF, D), (0.5 * TOKENS ** 0.5), 320.0, ((0, 4), (1, 8)), jnp.float32),
        "gain_moment": centred(seeds[16], (2, D), (1.0 * TOKENS ** 0.5), 640.0, (), jnp.float32),
        "bias_moment": centred(seeds[17], (4, D), (1.0 * TOKENS ** 0.5), 640.0, (), jnp.float32),
        "head_moment": centred(seeds[18], (2, D), (1.0 * TOKENS ** 0.5), 640.0, ((1, 4),), jnp.float32),
        "unit_moment": centred(seeds[19], (FF,), (0.2 * TOKENS ** 0.5), 128.0, ((0, 4),), jnp.float32),
    }


@jax.custom_vjp
def low(v):
    return lax.optimization_barrier(v.astype(jnp.bfloat16)).astype(jnp.float32)

@jax.custom_vjp
def low_back(v):
    return v

def low_keep(v):
    return (low(v), None)

def low_pass(kept, grad):
    return (grad,)

def back_keep(v):
    return (v, None)

def back_low(kept, grad):
    return (low(grad),)
low.defvjp(low_keep, low_pass)
low_back.defvjp(back_keep, back_low)
EPS = 1e-05
MOMENTUM = 0.9
NS_A = 3.4445
NS_B = -4.775
NS_C = 2.0315
RATE = 1.0
DECAY = 0.01
VECTOR_RATE = 0.1
FLOOR = -1e+30
PRECISE = lax.Precision.HIGHEST

def highest(left, right):
    return jnp.dot(left, right, precision=PRECISE, preferred_element_type=jnp.float32)

def layer_norm(rows, gain, shift):
    centre = rows - lax.optimization_barrier(jnp.mean(rows, axis=-1, keepdims=True))
    spread = lax.optimization_barrier(jnp.mean(centre * centre, axis=-1, keepdims=True))
    return centre * lax.rsqrt(spread + EPS) * gain + shift

def bin_segments(seq_lengths, seq_bin, index):
    order = jnp.arange(SEQS, dtype=jnp.int32)
    inside = seq_bin == index
    leader = jnp.min(jnp.where(inside, order, SEQS))
    first = jnp.sum(jnp.where(order == leader, seq_lengths, 0))
    total = jnp.sum(jnp.where(inside, seq_lengths, 0))
    slot = jnp.arange(SLOTS, dtype=jnp.int32)
    segment = jnp.where(slot < first, 0, jnp.where(slot < total, 1, slot + 2))
    return (segment.astype(jnp.int32), slot < total)

def split_heads(block):
    return block.reshape(block.shape[0], block.shape[1] // HEAD_DIM, HEAD_DIM)

def block_rows(rows, segment, params):
    qkv, proj, up_matrix, down_matrix, gains, shifts, head_shift, unit_shift = params
    width = D // N_MP
    units = FF // N_MP
    order = jnp.arange(SLOTS, dtype=jnp.int32)
    causal = (segment[:, None] == segment[None, :]) & (order[None, :] <= order[:, None])
    scale = HEAD_DIM ** (-0.5)
    normed = low(layer_norm(rows, gains[0], shifts[0]))
    branch = jnp.zeros((SLOTS, D), jnp.float32)
    for group in range(N_MP):
        columns = slice(group * width, (group + 1) * width)
        inner = low_back(normed)
        query = low_back(low((highest(inner, qkv[0][:, columns]) + head_shift[0][columns]) * scale))
        keys = low_back(low(highest(inner, qkv[1][:, columns])))
        values = low_back(low(highest(inner, qkv[2][:, columns]) + head_shift[1][columns]))
        scores = low_back(jnp.einsum('qhd,khd->hqk', split_heads(query), split_heads(keys), precision=PRECISE))
        scores = jnp.where(causal[None], scores, FLOOR)
        top = lax.optimization_barrier(jnp.max(scores, axis=-1, keepdims=True))
        raised = jnp.exp(scores - top)
        weights = low(raised / lax.optimization_barrier(jnp.sum(raised, axis=-1, keepdims=True)))
        mixed = jnp.einsum('hqk,khd->qhd', weights, split_heads(values), precision=PRECISE).reshape(SLOTS, width)
        mixed = low_back(low(mixed))
        branch = branch + low(highest(mixed, proj[columns, :]))
    hidden = rows + low_back(branch + shifts[2])
    normed_two = low(layer_norm(hidden, gains[1], shifts[1]))
    branch_two = jnp.zeros((SLOTS, D), jnp.float32)
    for group in range(N_MP):
        columns = slice(group * units, (group + 1) * units)
        inner = low_back(normed_two)
        before = low_back(highest(inner, up_matrix[:, columns]) + unit_shift[columns])
        active = low(jax.nn.gelu(before))
        branch_two = branch_two + low(highest(active, down_matrix[columns, :]))
    return hidden + low_back(branch_two + shifts[3])

def orthogonal(matrix):
    current = matrix / (jnp.sqrt(jnp.sum(matrix * matrix)) + 1e-07)
    for step in range(NS_STEPS):
        gram = highest(current, current.T)
        poly = NS_B * gram + NS_C * highest(gram, gram)
        current = NS_A * current + highest(poly, current)
    return current

def muon(weight, moment, grad, flip, factor):
    moment_next = MOMENTUM * moment + grad
    nesterov = grad + MOMENTUM * moment_next
    panel = nesterov.T if flip else nesterov
    orth = orthogonal(panel)
    orth = orth.T if flip else orth
    return (moment_next, weight.astype(jnp.float32) * (1.0 - RATE * DECAY) - RATE * factor * orth)

def reference(tokens, cotangent, seq_lengths, seq_bin, qkv_weight, out_weight, up_weight, down_weight, norm_gains, shared_biases, head_biases, unit_bias, qkv_moment, out_moment, up_moment, down_moment, gain_moment, bias_moment, head_moment, unit_moment):
    indices = jnp.arange(BINS, dtype=jnp.int32)
    segments, valid = jax.vmap(lambda index: bin_segments(seq_lengths, seq_bin, index))(indices)
    params = (qkv_weight.astype(jnp.float32), out_weight.astype(jnp.float32), up_weight.astype(jnp.float32), down_weight.astype(jnp.float32), norm_gains.astype(jnp.float32), shared_biases.astype(jnp.float32), head_biases.astype(jnp.float32), unit_bias.astype(jnp.float32))

    def forward(weights, rows):

        def one_bin(item):
            return block_rows(item[0], item[1], weights)
        results = lax.map(jax.checkpoint(one_bin), (rows.reshape(BINS, SLOTS, D), segments))
        return results.reshape(TOKENS, D)
    block_out, pull = jax.vjp(forward, params, tokens.astype(jnp.float32))
    masked_cotangent = cotangent.astype(jnp.float32) * valid.reshape(TOKENS, 1).astype(jnp.float32)
    grads, input_grad = pull(masked_cotangent)
    grad_qkv, grad_out, grad_up, grad_down, grad_gains, grad_biases, grad_heads, grad_units = grads
    qkv_parts = [muon(qkv_weight[t], qkv_moment[t], grad_qkv[t], False, 1.0) for t in range(3)]
    qkv_moment_next = jnp.stack([part[0] for part in qkv_parts])
    qkv_next = jnp.stack([part[1] for part in qkv_parts])
    out_moment_next, out_next = muon(out_weight, out_moment, grad_out, True, 1.0)
    up_moment_next, up_next = muon(up_weight, up_moment, grad_up, False, math.sqrt(max(1.0, FF / D)))
    down_moment_next, down_next = muon(down_weight, down_moment, grad_down, True, 1.0)
    rate = VECTOR_RATE / math.sqrt(TOKENS)

    def plain(param, moment, grad):
        moment_next = MOMENTUM * moment + grad
        return (moment_next, param - rate * moment_next)
    gain_moment_next, gain_next = plain(norm_gains, gain_moment, grad_gains)
    bias_moment_next, bias_next = plain(shared_biases, bias_moment, grad_biases)
    head_moment_next, head_next = plain(head_biases, head_moment, grad_heads)
    unit_moment_next, unit_next = plain(unit_bias, unit_moment, grad_units)
    return (block_out, input_grad, qkv_moment_next, qkv_next, out_moment_next, out_next, up_moment_next, up_next, down_moment_next, down_next, gain_moment_next, gain_next, bias_moment_next, bias_next, head_moment_next, head_next, unit_moment_next, unit_next)
```

```python
import math

import jax
import jax.numpy as jnp
from jax import lax
from jax.sharding import Mesh, PartitionSpec as P

D = 768
HEAD_DIM = 64
FF = 3072
SLOTS = 1024
NS_STEPS = 5

EPS = 1e-05
MOMENTUM = 0.9
NS_A = 3.4445
NS_B = -4.775
NS_C = 2.0315
RATE = 1.0
DECAY = 0.01
VECTOR_RATE = 0.1
FLOOR = -1e30

BF = jnp.bfloat16
F32 = jnp.float32


def swap(value, axis, distance=1):
    size = lax.axis_size(axis)
    return lax.ppermute(value, axis, [(i, i ^ distance) for i in range(size)])


def join(mine, theirs, bit, dim):
    low = jnp.where(bit, theirs, mine)
    high = jnp.where(bit, mine, theirs)
    return jnp.stack((low, high), axis=dim)


def distances(axis):
    found = []
    step = lax.axis_size(axis) // 2
    while step >= 1:
        found.append(step)
        step //= 2
    return found


def bit_of(axis, distance=1):
    return (lax.axis_index(axis) // distance) % 2 == 1


def gather_z(piece):
    lead = 0
    for distance in distances("z"):
        piece = join(piece, swap(piece, "z", distance), bit_of("z", distance), lead)
        lead += 1
    return piece.reshape(lax.axis_size("z"), *piece.shape[lead:])


def gather_rows(shard):
    half = shard.shape[0] // 2
    first = gather_z(shard[:half])
    second = gather_z(shard[half:])
    first = join(first, swap(first, "y"), bit_of("y"), 1)
    first = jnp.stack((first, swap(first, "x")))
    second = jnp.stack((second, swap(second, "x")))
    second = join(second, swap(second, "y"), bit_of("y"), 2)
    return jnp.stack((first, second), axis=3).reshape(2, -1, shard.shape[1])


def take(value, bit, dim):
    low, high = (lax.index_in_dim(value, k, dim, keepdims=False) for k in (0, 1))
    keep = jnp.where(bit, high, low)
    send = jnp.where(bit, low, high)
    return keep, send


def halve(value, axis, bit, dim, distance=1):
    keep, send = take(value, bit, dim)
    return keep.astype(F32) + swap(send.astype(BF), axis, distance).astype(F32)


def scatter_z(value):
    steps = distances("z")
    value = value.reshape(*(2 for _ in steps), *value.shape[1:])
    for k in range(len(steps) - 1, -1, -1):
        value = halve(value, "z", bit_of("z", steps[k]), k, steps[k])
    return value


def scatter_rows(grad):
    width = grad.shape[2]
    planes = lax.axis_size("z")
    parts = grad.reshape(2, planes, 2, 2, -1, width)
    first, second = parts[:, :, :, 0], parts[:, :, :, 1]
    first = first[0].astype(F32) + swap(first[1], "x").astype(F32)
    first = halve(first, "y", bit_of("y"), 1)
    second = halve(second, "y", bit_of("y"), 2)
    second = second[0] + swap(second[1].astype(BF), "x").astype(F32)
    return jnp.concatenate((scatter_z(first), scatter_z(second)), axis=0)


def fixed(value):
    return lax.optimization_barrier(value.astype(BF))


def across_cores(partial_value):
    own = fixed(partial_value)
    return own.astype(F32) + swap(own, "c").astype(F32)


def both_bins(value):
    own = fixed(value)
    half = SLOTS // 2
    core = lax.axis_index("c")
    sent = lax.dynamic_slice_in_dim(own, core * half, half, axis=0)
    got = swap(sent, "x")
    other = join(got, swap(got, "c"), bit_of("c"), 0).reshape(value.shape)
    return join(own, other, bit_of("x"), 0).reshape(-1, D).astype(F32)


def highest(left, right):
    return jnp.dot(left, right, precision=lax.Precision.HIGHEST, preferred_element_type=F32)


def layer_norm(rows, gain, shift):
    centre = rows - jnp.mean(rows, axis=-1, keepdims=True)
    spread = jnp.mean(centre * centre, axis=-1, keepdims=True)
    return centre * lax.rsqrt(spread + EPS) * gain + shift


def segments_of(seq_lengths, seq_bin, index):
    count = seq_lengths.shape[0]
    order = jnp.arange(count, dtype=jnp.int32)
    inside = seq_bin == index
    leader = jnp.min(jnp.where(inside, order, count))
    first = jnp.sum(jnp.where(order == leader, seq_lengths, 0))
    total = jnp.sum(jnp.where(inside, seq_lengths, 0))
    slot = jnp.arange(SLOTS, dtype=jnp.int32)
    segment = jnp.where(slot < first, 0, jnp.where(slot < total, 1, slot + 2))
    return (segment, slot < total)


def causal_mask(segment):
    order = jnp.arange(segment.shape[0], dtype=jnp.int32)
    return (segment[:, None] == segment[None, :]) & (order[None, :] <= order[:, None])


def split_heads(block):
    return block.reshape(block.shape[0], block.shape[1] // HEAD_DIM, HEAD_DIM)


def attend(query, keys, values, causal):
    scores = jnp.einsum(
        "qhd,khd->hqk", split_heads(query), split_heads(keys), preferred_element_type=F32
    )
    scores = jnp.where(causal[None], scores, FLOOR)
    top = jnp.max(scores, axis=-1, keepdims=True)
    raised = jnp.exp(scores - top)
    total = jnp.sum(raised, axis=-1, keepdims=True)
    weights = (raised / total).astype(BF)
    mixed = jnp.einsum("hqk,khd->qhd", weights, split_heads(values), preferred_element_type=F32)
    return (mixed.reshape(query.shape), top + jnp.log(total))


def attend_back(query, keys, values, log_total, causal, grad_mixed):
    heads_query = split_heads(query)
    heads_keys = split_heads(keys)
    heads_values = split_heads(values)
    grad_heads = split_heads(grad_mixed)
    scores = jnp.einsum("qhd,khd->hqk", heads_query, heads_keys, preferred_element_type=F32)
    weights = jnp.where(causal[None], jnp.exp(scores - log_total), 0.0)
    grad_values = jnp.einsum(
        "hqk,qhd->khd", weights.astype(BF), grad_heads, preferred_element_type=F32
    )
    grad_weights = jnp.einsum("qhd,khd->hqk", grad_heads, heads_values, preferred_element_type=F32)
    inner = jnp.sum(weights * grad_weights, axis=-1, keepdims=True)
    grad_scores = (weights * (grad_weights - inner)).astype(BF)
    grad_query = jnp.einsum("hqk,khd->qhd", grad_scores, heads_keys, preferred_element_type=F32)
    grad_keys = jnp.einsum("hqk,qhd->khd", grad_scores, heads_query, preferred_element_type=F32)
    shape = query.shape
    return (
        grad_query.reshape(shape).astype(BF),
        grad_keys.reshape(shape).astype(BF),
        grad_values.reshape(shape).astype(BF),
    )


def gram_sum(gram):
    parts = gram.reshape(2, D // 2, D)
    keep, send = take(parts, bit_of("c"), 0)
    mine = keep + swap(send, "c")
    mine = mine + swap(mine, "x")
    return join(mine, swap(mine, "c"), bit_of("c"), 0).reshape(D, D)


def newton(panel):
    gram = gram_sum(highest(panel, panel.T))
    factor = 1.0 / (jnp.sqrt(jnp.trace(gram)) + 1e-07)
    gram = gram * (factor * factor)
    eye = jnp.eye(D, dtype=F32)
    total = None
    for step in range(NS_STEPS):
        poly = NS_A * eye + NS_B * gram + NS_C * highest(gram, gram)
        total = poly if total is None else highest(poly, total)
        if step < NS_STEPS - 1:
            gram = highest(highest(poly, gram), poly)
    return highest(total, panel * factor)


def on_device(
    tokens,
    cotangent,
    seq_lengths,
    seq_bin,
    qkv_weight,
    out_weight,
    up_weight,
    down_weight,
    norm_gains,
    shared_biases,
    head_biases,
    unit_bias,
    qkv_moment,
    out_moment,
    up_moment,
    down_moment,
    gain_moment,
    bias_moment,
    head_moment,
    unit_moment,
):
    x_index = lax.axis_index("x")
    groups = lax.axis_size("z") * lax.axis_size("y")
    position = lax.axis_index("z") * lax.axis_size("y") + lax.axis_index("y")
    rows_each = qkv_weight.shape[1]
    heads_each = qkv_weight.shape[2]
    units_each = up_weight.shape[1]
    scale = HEAD_DIM ** (-0.5)

    qkv_shard = jnp.moveaxis(qkv_weight, 0, 1).reshape(rows_each, 3 * heads_each)
    qkv_full = gather_rows(qkv_shard)
    rest = gather_rows(jnp.concatenate((out_weight.T, up_weight), axis=1))
    down_full = gather_rows(down_weight.T)
    out_full = rest[:, :, :heads_each]
    up_full = rest[:, :, heads_each:]

    small = jnp.concatenate((head_biases.reshape(-1), unit_bias))
    small = jnp.stack((small, swap(small, "x")))
    query_bias = small[:, :heads_each].reshape(-1)
    value_bias = small[:, heads_each : 2 * heads_each].reshape(-1)
    units_shift = small[:, 2 * heads_each :].reshape(-1)

    start = x_index * SLOTS
    rows = lax.dynamic_slice_in_dim(tokens, start, SLOTS, axis=0)
    segment, valid = segments_of(seq_lengths, seq_bin, position * 2 + x_index)
    causal = causal_mask(segment)
    source = rows.astype(F32)
    normed = layer_norm(source, norm_gains[0], shared_biases[0]).astype(BF)
    weights_qkv = qkv_full.reshape(2, D, 3, heads_each)
    project = jnp.einsum("rd,gdtc->rtgc", normed, weights_qkv, preferred_element_type=F32)
    project = project.reshape(SLOTS, 3, 2 * heads_each)
    query = ((project[:, 0] + query_bias) * scale).astype(BF)
    keys = project[:, 1].astype(BF)
    values = (project[:, 2] + value_bias).astype(BF)
    mixed, log_total = attend(query, keys, values, causal)
    mixed = mixed.astype(BF)
    mixed_two = mixed.reshape(SLOTS, 2, heads_each)
    branch = across_cores(
        jnp.einsum("rgc,gdc->rd", mixed_two, out_full, preferred_element_type=F32)
    )
    hidden = source + (branch + shared_biases[2])
    normed_two = layer_norm(hidden, norm_gains[1], shared_biases[1]).astype(BF)
    up_cols = jnp.concatenate((up_full[0], up_full[1]), axis=1)
    down_cols = jnp.concatenate((down_full[0], down_full[1]), axis=1)
    before = jnp.dot(normed_two, up_cols, preferred_element_type=F32) + units_shift
    active = jax.nn.gelu(before).astype(BF)
    result = hidden + (
        across_cores(jnp.einsum("ru,du->rd", active, down_cols, preferred_element_type=F32))
        + shared_biases[3]
    )
    block_out = both_bins(result)

    grad_rows = lax.dynamic_slice_in_dim(cotangent, start, SLOTS, axis=0)
    grad_rows = grad_rows * valid[:, None].astype(BF)
    grad_result = grad_rows.astype(F32)
    grad_down = jnp.einsum("rd,ru->du", grad_rows, active, preferred_element_type=F32).astype(BF)
    grad_down = jnp.stack((grad_down[:, :units_each], grad_down[:, units_each:]))
    sum_down = scatter_rows(grad_down)
    grad_active = jnp.dot(grad_rows, down_cols, preferred_element_type=F32)
    grad_before = jax.vjp(jax.nn.gelu, before)[1](grad_active)[0].astype(BF)
    grad_up = jnp.einsum("rd,ru->du", normed_two, grad_before, preferred_element_type=F32).astype(BF)
    grad_up = jnp.stack((grad_up[:, :units_each], grad_up[:, units_each:]))
    sum_up = scatter_rows(grad_up)
    grad_normed_two = across_cores(
        jnp.einsum("ru,du->rd", grad_before, up_cols, preferred_element_type=F32)
    )
    grad_hidden, grad_gain_two, grad_shift_two = jax.vjp(
        layer_norm, hidden, norm_gains[1], shared_biases[1]
    )[1](grad_normed_two)
    grad_hidden = grad_hidden + grad_result
    grad_branch = grad_hidden.astype(BF)
    grad_out = jnp.einsum("rd,rgc->gdc", grad_branch, mixed_two, preferred_element_type=F32)
    grad_mixed = jnp.einsum("rd,gdc->rgc", grad_branch, out_full, preferred_element_type=F32)
    grad_mixed = grad_mixed.astype(BF).reshape(SLOTS, 2 * heads_each)
    grad_query, grad_keys, grad_values = attend_back(
        query, keys, values, log_total, causal, grad_mixed
    )
    grad_query = (grad_query.astype(F32) * scale).astype(BF)
    stacked = jnp.stack((grad_query, grad_keys, grad_values), axis=1)
    stacked = stacked.reshape(SLOTS, 3, 2, heads_each)
    grad_qkv = jnp.einsum("rd,rtgc->gdtc", normed, stacked, preferred_element_type=F32)
    grad_square = jnp.concatenate(
        (grad_qkv.astype(BF).reshape(2, D, 3 * heads_each), grad_out.astype(BF)), axis=2
    )
    sum_square = scatter_rows(grad_square)
    grad_normed = across_cores(
        jnp.einsum("rtgc,gdtc->rd", stacked, weights_qkv, preferred_element_type=F32)
    )
    grad_source, grad_gain_one, grad_shift_one = jax.vjp(
        layer_norm, source, norm_gains[0], shared_biases[0]
    )[1](grad_normed)
    input_grad = both_bins(grad_hidden + grad_source)

    def by_x(value):
        mine, theirs = value[:, 0], value[:, 1]
        return join(mine, theirs, bit_of("x"), 1)

    grad_heads = jnp.stack(
        (jnp.sum(grad_query.astype(F32), axis=0), jnp.sum(grad_values.astype(F32), axis=0))
    )
    grad_units = jnp.sum(grad_before.astype(F32), axis=0)
    vectors = (
        jnp.stack((grad_gain_one, grad_gain_two)),
        jnp.stack(
            (
                grad_shift_one,
                grad_shift_two,
                jnp.sum(grad_branch.astype(F32), axis=0),
                jnp.sum(grad_result, axis=0),
            )
        ),
        by_x(grad_heads.reshape(2, 2, heads_each)),
        by_x(grad_units.reshape(1, 2, units_each)),
    )
    sizes = [v.size for v in vectors]
    flat = lax.psum(jnp.concatenate([v.reshape(-1) for v in vectors]), ("z", "y", "x"))
    ends = [sum(sizes[: k + 1]) for k in range(4)]
    pieces = [flat[end - size : end] for end, size in zip(ends, sizes)]
    gains_sum = pieces[0].reshape(2, D)
    biases_sum = pieces[1].reshape(4, D)
    heads_sum = lax.dynamic_index_in_dim(
        pieces[2].reshape(2, 2, heads_each), x_index, 1, keepdims=False
    )
    units_sum = lax.dynamic_index_in_dim(pieces[3].reshape(2, units_each), x_index, 0, False)

    grads = (
        sum_square[:, :heads_each],
        sum_square[:, heads_each : 2 * heads_each],
        sum_square[:, 2 * heads_each : 3 * heads_each],
        sum_square[:, 3 * heads_each :],
        sum_up,
        sum_down,
    )
    moments = (
        qkv_moment[0],
        qkv_moment[1],
        qkv_moment[2],
        out_moment.T,
        up_moment,
        down_moment.T,
    )
    next_moments = [MOMENTUM * moment + grad for moment, grad in zip(moments, grads)]
    local_panels = [grad + MOMENTUM * moment for moment, grad in zip(next_moments, grads)]
    spacing = groups // 6
    width_all = units_each
    outgoing = jnp.zeros((groups, rows_each, width_all), BF)
    for number in range(6):
        shard = local_panels[number].astype(BF)
        shard = jnp.pad(shard, ((0, 0), (0, width_all - shard.shape[1])))
        outgoing = outgoing.at[number * spacing].set(shard)
    incoming = lax.all_to_all(outgoing, ("z", "y"), split_axis=0, concat_axis=0, tiled=True)
    orth = newton(incoming.reshape(groups * rows_each, width_all).astype(F32))
    back = lax.all_to_all(
        orth.astype(BF).reshape(groups, rows_each, width_all),
        ("z", "y"),
        split_axis=0,
        concat_axis=0,
        tiled=True,
    ).astype(F32)
    returned = [back[number * spacing][:, : local_panels[number].shape[1]] for number in range(6)]
    keep_share = 1.0 - RATE * DECAY
    up_factor = math.sqrt(max(1.0, FF / D))
    qkv_next = qkv_weight.astype(F32) * keep_share - RATE * jnp.stack(returned[:3])
    out_next = out_weight.astype(F32) * keep_share - RATE * returned[3].T
    up_next = up_weight.astype(F32) * keep_share - RATE * up_factor * returned[4]
    down_next = down_weight.astype(F32) * keep_share - RATE * returned[5].T
    rate_vector = VECTOR_RATE / math.sqrt(groups * tokens.shape[0])
    gain_moment_next = MOMENTUM * gain_moment + gains_sum
    bias_moment_next = MOMENTUM * bias_moment + biases_sum
    head_moment_next = MOMENTUM * head_moment + heads_sum
    unit_moment_next = MOMENTUM * unit_moment + units_sum
    gain_next = norm_gains - rate_vector * gain_moment_next
    bias_next = shared_biases - rate_vector * bias_moment_next
    head_next = head_biases - rate_vector * head_moment_next
    unit_next = unit_bias - rate_vector * unit_moment_next
    return (
        block_out,
        input_grad,
        jnp.stack(next_moments[:3]),
        qkv_next,
        next_moments[3].T,
        out_next,
        next_moments[4],
        up_next,
        next_moments[5].T,
        down_next,
        gain_moment_next,
        gain_next,
        bias_moment_next,
        bias_next,
        head_moment_next,
        head_next,
        unit_moment_next,
        unit_next,
    )


def solution(mesh):
    dp_size, mp_size = mesh.devices.shape
    split = Mesh(
        mesh.devices.reshape(dp_size // 2, 2, mp_size // 2, 2), ("z", "y", "x", "c")
    )
    dp, mp = ("z", "y"), ("x", "c")
    in_specs = (
        P(dp, None),
        P(dp, None),
        P(),
        P(),
        P(None, dp, mp),
        P(mp, dp),
        P(dp, mp),
        P(mp, dp),
        P(),
        P(),
        P(None, mp),
        P(mp),
        P(None, dp, mp),
        P(mp, dp),
        P(dp, mp),
        P(mp, dp),
        P(),
        P(),
        P(None, mp),
        P(mp),
    )
    out_specs = (
        P(dp, None),
        P(dp, None),
        P(None, dp, mp),
        P(None, dp, mp),
        P(mp, dp),
        P(mp, dp),
        P(dp, mp),
        P(dp, mp),
        P(mp, dp),
        P(mp, dp),
        P(),
        P(),
        P(),
        P(),
        P(None, mp),
        P(None, mp),
        P(mp),
        P(mp),
    )
    return jax.shard_map(
        on_device, mesh=split, in_specs=in_specs, out_specs=out_specs, check_vma=False
    )
```

```python
import math

import jax
import jax.numpy as jnp
from jax import lax
from jax.experimental import pallas as pl
from jax.experimental.pallas import tpu as pltpu
from jax.sharding import Mesh, PartitionSpec as P

D = 768
HEAD_DIM = 64
FF = 3072
SLOTS = 1024
NS_STEPS = 5

EPS = 1e-05
MOMENTUM = 0.9
NS_A = 3.4445
NS_B = -4.775
NS_C = 2.0315
RATE = 1.0
DECAY = 0.01
VECTOR_RATE = 0.1
FLOOR = -1e30
TILE = 256
ROWS = 256

BF = jnp.bfloat16
F32 = jnp.float32


def swap(value, axis, distance=1):
    size = lax.axis_size(axis)
    return lax.ppermute(value, axis, [(i, i ^ distance) for i in range(size)])


def join(mine, theirs, bit, dim):
    low = jnp.where(bit, theirs, mine)
    high = jnp.where(bit, mine, theirs)
    return jnp.stack((low, high), axis=dim)


def distances(axis):
    found = []
    step = lax.axis_size(axis) // 2
    while step >= 1:
        found.append(step)
        step //= 2
    return found


def bit_of(axis, distance=1):
    return (lax.axis_index(axis) // distance) % 2 == 1


def after(value, *others):
    return lax.optimization_barrier((value, *others))[0]


def fixed(value):
    return lax.optimization_barrier(value.astype(BF))


def gather_z(piece):
    lead = 0
    for distance in distances("z"):
        piece = join(piece, swap(piece, "z", distance), bit_of("z", distance), lead)
        lead += 1
    return piece.reshape(lax.axis_size("z"), *piece.shape[lead:])


def gather_yx(shard):
    piece = gather_z(shard)
    mine = join(piece, swap(piece, "y"), bit_of("y"), 1).reshape(-1, shard.shape[1])
    return mine, swap(mine, "x")


def gather_xy(shard):
    piece = gather_z(shard)
    other = swap(piece, "x")
    bit = bit_of("y")
    both = (join(p, swap(p, "y"), bit, 1) for p in (piece, other))
    return tuple(p.reshape(-1, shard.shape[1]) for p in both)


def take(value, bit, dim):
    low, high = (lax.index_in_dim(value, k, dim, keepdims=False) for k in (0, 1))
    keep = jnp.where(bit, high, low)
    send = jnp.where(bit, low, high)
    return keep, send


def halve(value, axis, bit, dim, distance=1, *wait):
    keep, send = take(value, bit, dim)
    got = swap(fixed(send), axis, distance)
    if wait:
        got = after(got, *wait)
    return keep.astype(F32) + got.astype(F32)


def scatter_z(value):
    steps = distances("z")
    value = value.reshape(*(2 for _ in steps), *value.shape[1:])
    for k in range(len(steps) - 1, -1, -1):
        value = halve(value, "z", bit_of("z", steps[k]), k, steps[k])
    return value


def by_rows(grad):
    return grad.reshape(lax.axis_size("z"), 2, -1, grad.shape[-1])


def all_sum(value, axes):
    for axis in axes:
        for distance in distances(axis):
            value = value + swap(value, axis, distance)
    return value


def swap_cores(own):
    half = own.shape[0] // 2
    return jnp.concatenate((swap(own[:half], "c"), swap(own[half:], "c")), axis=0)


def across_cores(partial_value):
    own = fixed(partial_value)
    return own.astype(F32) + swap_cores(own).astype(F32)


def both_bins(own):
    half = SLOTS // 2
    core = lax.axis_index("c")
    sent = lax.dynamic_slice_in_dim(own, core * half, half, axis=0)
    got = swap(sent, "x")
    other = join(got, swap(got, "c"), bit_of("c"), 0).reshape(own.shape)
    return join(own, other, bit_of("x"), 0).reshape(-1, D).astype(F32)


def layer_norm(rows, gain, shift):
    centre = rows - jnp.mean(rows, axis=-1, keepdims=True)
    spread = jnp.mean(centre * centre, axis=-1, keepdims=True)
    return centre * lax.rsqrt(spread + EPS) * gain + shift


def segments_of(seq_lengths, seq_bin, index):
    count = seq_lengths.shape[0]
    order = jnp.arange(count, dtype=jnp.int32)
    inside = seq_bin == index
    leader = jnp.min(jnp.where(inside, order, count))
    first = jnp.sum(jnp.where(order == leader, seq_lengths, 0))
    total = jnp.sum(jnp.where(inside, seq_lengths, 0))
    slot = jnp.arange(SLOTS, dtype=jnp.int32)
    segment = jnp.where(slot < first, 0, jnp.where(slot < total, 1, slot + 2))
    return (segment, slot < total)


def first_key(seq_lengths, seq_bin, index):
    segment, valid = segments_of(seq_lengths, seq_bin, index)
    slot = jnp.arange(SLOTS, dtype=jnp.int32)
    start = jnp.sum(jnp.where(segment == 0, 1, 0))
    low = jnp.where(segment == 0, 0, jnp.where(segment == 1, start, slot))
    return low, valid


def dot_nt(left, right):
    return lax.dot_general(left, right, (((1,), (1,)), ((), ())), preferred_element_type=F32)


def dot_tn(left, right):
    return lax.dot_general(left, right, (((0,), (0,)), ((), ())), preferred_element_type=F32)


def tile_mask(low, tile, keys):
    shape = (TILE, keys)
    row = lax.broadcasted_iota(jnp.int32, shape, 0) + tile * TILE
    column = lax.broadcasted_iota(jnp.int32, shape, 1)
    return (column <= row) & (column >= low)


def attend_kernel(low_ref, qkv_ref, out_ref, log_ref):
    width = out_ref.shape[1]
    for tile in range(SLOTS // TILE):
        here = slice(tile * TILE, (tile + 1) * TILE)
        keys = (tile + 1) * TILE
        mask = tile_mask(low_ref[here], tile, keys)
        for head in range(width // HEAD_DIM):
            lanes = slice(head * HEAD_DIM, (head + 1) * HEAD_DIM)
            query = qkv_ref[here, lanes]
            key = qkv_ref[:keys, width + head * HEAD_DIM : width + (head + 1) * HEAD_DIM]
            value = qkv_ref[:keys, 2 * width + head * HEAD_DIM : 2 * width + (head + 1) * HEAD_DIM]
            scores = jnp.where(mask, dot_nt(query, key), FLOOR)
            top = jnp.max(scores, axis=-1, keepdims=True)
            raised = jnp.exp(scores - top)
            total = jnp.sum(raised, axis=-1, keepdims=True)
            weights = (raised * (1.0 / total)).astype(BF)
            mixed = jnp.dot(weights, value, preferred_element_type=F32)
            out_ref[here, lanes] = mixed.astype(BF)
            log_ref[here, lanes] = jnp.broadcast_to(top + jnp.log(total), (TILE, HEAD_DIM))


def attend_back_kernel(low_ref, qkv_ref, grad_ref, log_ref, out_ref, keys_sum, values_sum):
    width = grad_ref.shape[1]
    for head in range(width // HEAD_DIM):
        lanes = slice(head * HEAD_DIM, (head + 1) * HEAD_DIM)
        key_lanes = slice(width + head * HEAD_DIM, width + (head + 1) * HEAD_DIM)
        value_lanes = slice(2 * width + head * HEAD_DIM, 2 * width + (head + 1) * HEAD_DIM)
        keys_sum[...] = jnp.zeros_like(keys_sum)
        values_sum[...] = jnp.zeros_like(values_sum)
        for tile in range(SLOTS // TILE):
            here = slice(tile * TILE, (tile + 1) * TILE)
            keys = (tile + 1) * TILE
            mask = tile_mask(low_ref[here], tile, keys)
            query = qkv_ref[here, lanes]
            key = qkv_ref[:keys, key_lanes]
            value = qkv_ref[:keys, value_lanes]
            grad = grad_ref[here, lanes]
            scores = dot_nt(query, key) - log_ref[here, head * HEAD_DIM : head * HEAD_DIM + 1]
            weights = jnp.exp(jnp.where(mask, scores, FLOOR))
            grad_weights = dot_nt(grad, value)
            product = weights * grad_weights
            inner = jnp.sum(product, axis=-1, keepdims=True)
            grad_scores = (product - weights * inner).astype(BF)
            values_sum[:keys] += dot_tn(weights.astype(BF), grad)
            keys_sum[:keys] += dot_tn(grad_scores, query)
            grad_query = jnp.dot(grad_scores, key, preferred_element_type=F32).astype(BF)
            out_ref[here, lanes] = (grad_query.astype(F32) * HEAD_DIM ** (-0.5)).astype(BF)
        out_ref[:, key_lanes] = keys_sum[...].astype(BF)
        out_ref[:, value_lanes] = values_sum[...].astype(BF)


def on_chip(kernel, shapes, scratch, flops, exps, *operands):
    moved = sum(o.size * o.dtype.itemsize for o in (*operands, *shapes))
    return pl.pallas_call(
        kernel,
        out_shape=shapes,
        in_specs=[pl.BlockSpec(memory_space=pltpu.VMEM)] * len(operands),
        out_specs=[pl.BlockSpec(memory_space=pltpu.VMEM)] * len(shapes),
        scratch_shapes=scratch,
        compiler_params=pltpu.CompilerParams(vmem_limit_bytes=50 * 2**20),
        cost_estimate=pl.CostEstimate(flops=flops, bytes_accessed=moved, transcendentals=exps),
    )(*operands)


def attend(low, qkv):
    width = qkv.shape[1] // 3
    shapes = [
        jax.ShapeDtypeStruct((SLOTS, width), BF),
        jax.ShapeDtypeStruct((SLOTS, width), F32),
    ]
    pairs = SLOTS * SLOTS * width // HEAD_DIM
    return on_chip(attend_kernel, shapes, [], 16 * pairs * HEAD_DIM, pairs, low, qkv)


def attend_back(low, qkv, grad, log_total):
    shapes = [jax.ShapeDtypeStruct(qkv.shape, BF)]
    scratch = [pltpu.VMEM((SLOTS, HEAD_DIM), F32)] * 2
    pairs = SLOTS * SLOTS * grad.shape[1] // HEAD_DIM
    return on_chip(
        attend_back_kernel, shapes, scratch, 40 * pairs * HEAD_DIM, pairs, low, qkv, grad, log_total
    )[0]


def newton_kernel(gram_ref, panel_ref, out_ref, ah, al, ph, pl_, bh, bl, qh, ql, rh, rl):
    def store(pair, here, value):
        high = value.astype(BF)
        pair[0][here] = high
        pair[1][here] = (value - high.astype(F32)).astype(BF)

    def product(left, right, here):
        total = jnp.dot(left[0][here], right[0][...], preferred_element_type=F32)
        total += jnp.dot(left[0][here], right[1][...], preferred_element_type=F32)
        return total + jnp.dot(left[1][here], right[0][...], preferred_element_type=F32)

    def tiles(body):
        @pl.loop(0, D // ROWS)
        def _(tile):
            first = pl.multiple_of(tile * ROWS, ROWS)
            body(first, pl.ds(first, ROWS))

    gram, poly, both = (ah, al), (ph, pl_), (bh, bl)
    total, spare = (qh, ql), (rh, rl)
    tiles(lambda first, here: store(gram, here, gram_ref[here]))
    for step in range(NS_STEPS):

        def make_poly(first, here):
            square = product(gram, gram, here)
            here_gram = gram[0][here].astype(F32) + gram[1][here].astype(F32)
            row = lax.broadcasted_iota(jnp.int32, (ROWS, D), 0) + first
            column = lax.broadcasted_iota(jnp.int32, (ROWS, D), 1)
            value = NS_B * here_gram + NS_C * square
            value = jnp.where(row == column, value + NS_A, value)
            store(poly, here, value)
            if step == 0:
                store(total, here, value)

        tiles(make_poly)
        if step > 0:
            tiles(lambda first, here: store(spare, here, product(poly, total, here)))
            total, spare = spare, total
        if step < NS_STEPS - 1:
            tiles(lambda first, here: store(both, here, product(poly, gram, here)))
            tiles(lambda first, here: store(gram, here, product(both, poly, here)))

    def finish(first, here):
        value = jnp.dot(total[0][here], panel_ref[...], preferred_element_type=F32)
        value += jnp.dot(total[1][here], panel_ref[...], preferred_element_type=F32)
        out_ref[here] = value

    tiles(finish)


def newton(gram, panel):
    factor = 1.0 / (jnp.sqrt(jnp.trace(gram)) + 1e-07)
    shapes = [jax.ShapeDtypeStruct(panel.shape, F32)]
    scratch = [pltpu.VMEM((D, D), BF)] * 10
    flops = 53 * 2 * D**3
    orth = on_chip(newton_kernel, shapes, scratch, flops, 0, gram * (factor * factor), panel)[0]
    return orth * factor


def gram_sum(gram):
    keep, send = take(gram.reshape(2, D // 2, D), bit_of("c"), 0)
    mine = keep + swap(send, "c")
    mine = mine + swap(mine, "x")
    return join(mine, swap(mine, "c"), bit_of("c"), 0).reshape(D, D)


def on_device(
    tokens,
    cotangent,
    seq_lengths,
    seq_bin,
    qkv_weight,
    out_weight,
    up_weight,
    down_weight,
    norm_gains,
    shared_biases,
    head_biases,
    unit_bias,
    qkv_moment,
    out_moment,
    up_moment,
    down_moment,
    gain_moment,
    bias_moment,
    head_moment,
    unit_moment,
):
    x_index = lax.axis_index("x")
    groups = lax.axis_size("z") * lax.axis_size("y")
    position = lax.axis_index("z") * lax.axis_size("y") + lax.axis_index("y")
    rows_each = qkv_weight.shape[1]
    heads_each = qkv_weight.shape[2]
    units_each = up_weight.shape[1]
    scale = HEAD_DIM ** (-0.5)

    qkv_shard = jnp.concatenate([qkv_weight[t] for t in range(3)], axis=1)
    qkv_own, qkv_next_x = gather_yx(qkv_shard)
    up_own, up_next_x = gather_yx(jnp.concatenate((up_weight, out_weight.T), axis=1))
    down = gather_xy(down_weight.T)
    qkv = (qkv_own, qkv_next_x)
    up = (up_own[:, :units_each], up_next_x[:, :units_each])
    out = (up_own[:, units_each:], up_next_x[:, units_each:])

    small = jnp.concatenate((head_biases.reshape(-1), unit_bias))
    small = (small, swap(small, "x"))
    zero = jnp.zeros((heads_each,), F32)
    scales = jnp.concatenate((jnp.full((heads_each,), scale, F32), jnp.ones((2 * heads_each,), F32)))

    def project(group):
        shift = jnp.concatenate(
            (small[group][:heads_each], zero, small[group][heads_each : 2 * heads_each])
        )
        value = jnp.dot(normed, qkv[group], preferred_element_type=F32)
        return ((value + shift) * scales).astype(BF)

    start = x_index * SLOTS
    rows = lax.dynamic_slice_in_dim(tokens, start, SLOTS, axis=0)
    low, valid = first_key(seq_lengths, seq_bin, position * 2 + x_index)
    low = low[:, None]
    source = rows.astype(F32)
    normed = layer_norm(source, norm_gains[0], shared_biases[0]).astype(BF)
    heads = [project(0)]
    mixed, logs = zip(attend(low, heads[0]))
    heads.append(after(project(1), mixed[0]))
    mixed_x, logs_x = attend(low, heads[1])
    mixed, logs = (mixed[0], mixed_x), (logs[0], logs_x)
    branch = across_cores(dot_nt(mixed[0], out[0]) + dot_nt(mixed[1], out[1]))
    hidden = source + (branch + shared_biases[2])
    normed_two = layer_norm(hidden, norm_gains[1], shared_biases[1]).astype(BF)
    before = [
        jnp.dot(normed_two, up[k], preferred_element_type=F32) + small[k][2 * heads_each :]
        for k in range(2)
    ]
    active = [jax.nn.gelu(b).astype(BF) for b in before]

    grad_rows = lax.dynamic_slice_in_dim(cotangent, start, SLOTS, axis=0)
    grad_rows = grad_rows * valid[:, None].astype(BF)
    grad_result = grad_rows.astype(F32)
    grad_before = [
        jax.vjp(jax.nn.gelu, before[k])[1](
            jnp.dot(grad_rows, down[k], preferred_element_type=F32)
        )[0].astype(BF)
        for k in range(2)
    ]
    grad_partial = fixed(dot_nt(grad_before[0], up[0]) + dot_nt(grad_before[1], up[1]))
    grad_other = swap_cores(grad_partial)
    planes = lax.axis_size("z")
    held, held_two = after(tuple(active), grad_partial), after(normed_two, grad_partial)
    grad_up = [dot_tn(held_two, grad_before[k]).astype(BF) for k in range(2)]
    grad_down = jnp.stack([by_rows(dot_tn(grad_rows, held[k]).astype(BF)) for k in range(2)])
    partial_two = fixed(dot_nt(active[0], down[0]) + dot_nt(active[1], down[1]))

    grad_normed_two = grad_partial.astype(F32) + grad_other.astype(F32)
    grad_hidden, grad_gain_two, grad_shift_two = jax.vjp(
        layer_norm, hidden, norm_gains[1], shared_biases[1]
    )[1](grad_normed_two)
    grad_hidden = grad_hidden + grad_result
    grad_branch = grad_hidden.astype(BF)
    grad_mixed = [jnp.dot(grad_branch, out[k], preferred_element_type=F32).astype(BF) for k in range(2)]
    back_x = attend_back(low, heads[1], grad_mixed[1], logs[1])
    grad_square_x = jnp.concatenate(
        (dot_tn(normed, back_x).astype(BF), dot_tn(grad_branch, mixed[1]).astype(BF)), axis=1
    )
    up_sum = grad_up[0].astype(F32) + after(swap(grad_up[1], "x"), back_x).astype(F32)
    down_sum = halve(grad_down, "y", bit_of("y"), 2, 1, back_x)
    square_got = swap(fixed(grad_square_x), "x")
    back = attend_back(low, heads[0], after(grad_mixed[0], back_x), logs[0])
    grad_square = jnp.concatenate(
        (dot_tn(normed, back).astype(BF), dot_tn(grad_branch, mixed[0]).astype(BF)), axis=1
    )
    up_sum = halve(by_rows(up_sum), "y", bit_of("y"), 1, 1, back)
    down_got = after(swap(fixed(down_sum[1]), "x"), back)
    down_sum = down_sum[0] + down_got.astype(F32)
    sum_up = scatter_z(up_sum)
    sum_down = scatter_z(down_sum)
    square = grad_square.astype(F32) + square_got.astype(F32)
    square = halve(by_rows(square), "y", bit_of("y"), 1)
    sum_square = scatter_z(square)

    grad_partial = fixed(dot_nt(back, qkv[0]) + dot_nt(back_x, qkv[1]))
    grad_normed = grad_partial.astype(F32) + swap_cores(grad_partial).astype(F32)
    grad_source, grad_gain_one, grad_shift_one = jax.vjp(
        layer_norm, source, norm_gains[0], shared_biases[0]
    )[1](grad_normed)
    result = hidden + (
        (partial_two.astype(F32) + swap_cores(partial_two).astype(F32)) + shared_biases[3]
    )
    block_out = both_bins(after(fixed(result), square))
    input_grad = both_bins(fixed(grad_hidden + grad_source))

    def by_x(mine, theirs):
        return join(mine, theirs, bit_of("x"), 1)

    grad_bias = [jnp.sum(b.astype(F32), axis=0) for b in (back, back_x)]
    grad_heads = [jnp.stack((g[:heads_each], g[2 * heads_each :])) for g in grad_bias]
    grad_units = [jnp.sum(g.astype(F32), axis=0)[None] for g in grad_before]
    vectors = (
        jnp.stack((grad_gain_one, grad_gain_two)),
        jnp.stack(
            (
                grad_shift_one,
                grad_shift_two,
                jnp.sum(grad_branch.astype(F32), axis=0),
                jnp.sum(grad_result, axis=0),
            )
        ),
        by_x(*grad_heads),
        by_x(*grad_units),
    )
    sizes = [v.size for v in vectors]
    flat = all_sum(
        jnp.concatenate([v.reshape(-1) for v in vectors]).reshape(-1, 128), ("x", "y", "z")
    ).reshape(-1)
    ends = [sum(sizes[: k + 1]) for k in range(4)]
    pieces = [flat[end - size : end] for end, size in zip(ends, sizes)]
    gains_sum = pieces[0].reshape(2, D)
    biases_sum = pieces[1].reshape(4, D)
    heads_sum = lax.dynamic_index_in_dim(
        pieces[2].reshape(2, 2, heads_each), x_index, 1, keepdims=False
    )
    units_sum = lax.dynamic_index_in_dim(pieces[3].reshape(2, units_each), x_index, 0, False)

    grads = (
        sum_square[:, :heads_each],
        sum_square[:, heads_each : 2 * heads_each],
        sum_square[:, 2 * heads_each : 3 * heads_each],
        sum_square[:, 3 * heads_each :],
        sum_up,
        sum_down,
    )
    moments = (
        qkv_moment[0],
        qkv_moment[1],
        qkv_moment[2],
        out_moment.T,
        up_moment,
        down_moment.T,
    )
    next_moments = [MOMENTUM * moment + grad for moment, grad in zip(moments, grads)]
    local_panels = [
        (grad + MOMENTUM * moment).astype(BF) for moment, grad in zip(next_moments, grads)
    ]
    spread = groups // 8
    owners = [number * spread for number in (0, 3, 4, 7, 2, 5)]

    def to_owners(width, numbers):
        outgoing = jnp.zeros((groups, rows_each, width), BF)
        for number in numbers:
            outgoing = outgoing.at[owners[number]].set(local_panels[number])
        incoming = lax.all_to_all(outgoing, ("z", "y"), split_axis=0, concat_axis=0, tiled=True)
        return incoming.reshape(groups * rows_each, width)

    wide = to_owners(units_each, (4, 5))
    wide_gram = gram_sum(dot_nt(wide, wide))
    narrow = to_owners(heads_each, (0, 1, 2, 3))
    narrow_x = swap(narrow, "x")
    pair = jnp.concatenate((narrow, narrow_x), axis=1)
    pair = jnp.concatenate((pair, swap(pair, "c")), axis=1)
    is_wide = (position == owners[4]) | (position == owners[5])
    gram = jnp.where(is_wide, wide_gram, dot_nt(pair, pair))
    narrow = jnp.pad(narrow, ((0, 0), (0, units_each - heads_each)))
    orth = newton(gram, jnp.where(is_wide, wide, narrow))
    back = lax.all_to_all(
        orth.astype(BF).reshape(groups, rows_each, units_each),
        ("z", "y"),
        split_axis=0,
        concat_axis=0,
        tiled=True,
    ).astype(F32)
    returned = [back[owners[k]][:, : local_panels[k].shape[1]] for k in range(6)]
    keep_share = 1.0 - RATE * DECAY
    up_factor = math.sqrt(max(1.0, FF / D))
    qkv_next = qkv_weight.astype(F32) * keep_share - RATE * jnp.stack(returned[:3])
    out_next = out_weight.astype(F32) * keep_share - RATE * returned[3].T
    up_next = up_weight.astype(F32) * keep_share - RATE * up_factor * returned[4]
    down_next = down_weight.astype(F32) * keep_share - RATE * returned[5].T
    rate_vector = VECTOR_RATE / math.sqrt(groups * tokens.shape[0])
    gain_moment_next = MOMENTUM * gain_moment + gains_sum
    bias_moment_next = MOMENTUM * bias_moment + biases_sum
    head_moment_next = MOMENTUM * head_moment + heads_sum
    unit_moment_next = MOMENTUM * unit_moment + units_sum
    gain_next = norm_gains - rate_vector * gain_moment_next
    bias_next = shared_biases - rate_vector * bias_moment_next
    head_next = head_biases - rate_vector * head_moment_next
    unit_next = unit_bias - rate_vector * unit_moment_next
    return (
        block_out,
        input_grad,
        jnp.stack(next_moments[:3]),
        qkv_next,
        next_moments[3].T,
        out_next,
        next_moments[4],
        up_next,
        next_moments[5].T,
        down_next,
        gain_moment_next,
        gain_next,
        bias_moment_next,
        bias_next,
        head_moment_next,
        head_next,
        unit_moment_next,
        unit_next,
    )


def solution(mesh):
    dp_size, mp_size = mesh.devices.shape
    split = Mesh(
        mesh.devices.reshape(dp_size // 2, 2, mp_size // 2, 2), ("z", "y", "x", "c")
    )
    dp, mp = ("z", "y"), ("x", "c")
    in_specs = (
        P(dp, None),
        P(dp, None),
        P(),
        P(),
        P(None, dp, mp),
        P(mp, dp),
        P(dp, mp),
        P(mp, dp),
        P(),
        P(),
        P(None, mp),
        P(mp),
        P(None, dp, mp),
        P(mp, dp),
        P(dp, mp),
        P(mp, dp),
        P(),
        P(),
        P(None, mp),
        P(mp),
    )
    out_specs = (
        P(dp, None),
        P(dp, None),
        P(None, dp, mp),
        P(None, dp, mp),
        P(mp, dp),
        P(mp, dp),
        P(dp, mp),
        P(dp, mp),
        P(mp, dp),
        P(mp, dp),
        P(),
        P(),
        P(),
        P(),
        P(None, mp),
        P(None, mp),
        P(mp),
        P(mp),
    )
    return jax.shard_map(
        on_device, mesh=split, in_specs=in_specs, out_specs=out_specs, check_vma=False
    )
```

```python
import math

import jax
import jax.numpy as jnp
from jax import lax
from jax.experimental import pallas as pl
from jax.experimental.pallas import tpu as pltpu
from jax.sharding import Mesh, PartitionSpec as P

D = 768
HEAD_DIM = 64
FF = 3072
SLOTS = 1024
NS_STEPS = 5

EPS = 1e-05
MOMENTUM = 0.9
NS_A = 3.4445
NS_B = -4.775
NS_C = 2.0315
RATE = 1.0
DECAY = 0.01
VECTOR_RATE = 0.1
FLOOR = -1e30
TILE = 256
SHIFTS = (0.0, 0.0, 0.3, 0.8, 0.8)
ROWS = 256

BF = jnp.bfloat16
F32 = jnp.float32


def swap(value, axis, distance=1):
    size = lax.axis_size(axis)
    return lax.ppermute(value, axis, [(i, i ^ distance) for i in range(size)])


def join(mine, theirs, bit, dim):
    low = jnp.where(bit, theirs, mine)
    high = jnp.where(bit, mine, theirs)
    return jnp.stack((low, high), axis=dim)


def distances(axis):
    found = []
    step = lax.axis_size(axis) // 2
    while step >= 1:
        found.append(step)
        step //= 2
    return found


def bit_of(axis, distance=1):
    return (lax.axis_index(axis) // distance) % 2 == 1


def after(value, *others):
    return lax.optimization_barrier((value, *others))[0]


def fixed(value):
    return lax.optimization_barrier(value.astype(BF))


def grow(piece, axis, distance, dim, *wait):
    got = swap(piece, axis, distance)
    if wait:
        got = after(got, *wait)
    return join(piece, got, bit_of(axis, distance), dim)


def take(value, bit, dim):
    low, high = (lax.index_in_dim(value, k, dim, keepdims=False) for k in (0, 1))
    keep = jnp.where(bit, high, low)
    send = jnp.where(bit, low, high)
    return keep, send


def halve(value, axis, dim, distance, *wait):
    keep, send = take(value, bit_of(axis, distance), dim)
    got = swap(fixed(send), axis, distance)
    if wait:
        got = after(got, *wait)
    return keep.astype(F32) + got.astype(F32)


def split_planes(value, dim):
    bits = [2 for _ in distances("z")]
    return value.reshape(*value.shape[:dim], *bits, *value.shape[dim + 1 :])


def by_rows(grad):
    return grad.reshape(lax.axis_size("z"), 2, -1, grad.shape[-1])


def all_sum(value, axes):
    for axis in axes:
        for distance in distances(axis):
            value = value + swap(value, axis, distance)
    return value


def swap_cores(own):
    half = own.shape[0] // 2
    return jnp.concatenate((swap(own[:half], "c"), swap(own[half:], "c")), axis=0)


def across_cores(partial_value):
    own = fixed(partial_value)
    return own.astype(F32) + swap_cores(own).astype(F32)


def layer_norm(rows, gain, shift):
    centre = rows - jnp.mean(rows, axis=-1, keepdims=True)
    spread = jnp.mean(centre * centre, axis=-1, keepdims=True)
    return centre * lax.rsqrt(spread + EPS) * gain + shift


def segments_of(seq_lengths, seq_bin, index):
    count = seq_lengths.shape[0]
    order = jnp.arange(count, dtype=jnp.int32)
    inside = seq_bin == index
    leader = jnp.min(jnp.where(inside, order, count))
    first = jnp.sum(jnp.where(order == leader, seq_lengths, 0))
    total = jnp.sum(jnp.where(inside, seq_lengths, 0))
    slot = jnp.arange(SLOTS, dtype=jnp.int32)
    segment = jnp.where(slot < first, 0, jnp.where(slot < total, 1, slot + 2))
    return (segment, slot < total)


def first_key(seq_lengths, seq_bin, index):
    segment, valid = segments_of(seq_lengths, seq_bin, index)
    slot = jnp.arange(SLOTS, dtype=jnp.int32)
    start = jnp.sum(jnp.where(segment == 0, 1, 0))
    low = jnp.where(segment == 0, 0, jnp.where(segment == 1, start, slot))
    return low, valid


def dot_nt(left, right):
    return lax.dot_general(left, right, (((1,), (1,)), ((), ())), preferred_element_type=F32)


def dot_tn(left, right):
    return lax.dot_general(left, right, (((0,), (0,)), ((), ())), preferred_element_type=F32)


def tile_mask(low, tile, keys):
    shape = (TILE, keys)
    row = lax.broadcasted_iota(jnp.int32, shape, 0) + tile * TILE
    column = lax.broadcasted_iota(jnp.int32, shape, 1)
    return (column <= row) & (column >= low)


def attend_kernel(low_ref, qkv_ref, out_ref, log_ref):
    width = out_ref.shape[1]
    for tile in range(SLOTS // TILE):
        here = slice(tile * TILE, (tile + 1) * TILE)
        keys = (tile + 1) * TILE
        mask = tile_mask(low_ref[here], tile, keys)
        for head in range(width // HEAD_DIM):
            lanes = slice(head * HEAD_DIM, (head + 1) * HEAD_DIM)
            query = qkv_ref[here, lanes]
            key = qkv_ref[:keys, width + head * HEAD_DIM : width + (head + 1) * HEAD_DIM]
            value = qkv_ref[:keys, 2 * width + head * HEAD_DIM : 2 * width + (head + 1) * HEAD_DIM]
            scores = jnp.where(mask, dot_nt(query, key), FLOOR)
            top = jnp.max(scores, axis=-1, keepdims=True)
            raised = jnp.exp(scores - top)
            total = jnp.sum(raised, axis=-1, keepdims=True)
            weights = (raised * (1.0 / total)).astype(BF)
            mixed = jnp.dot(weights, value, preferred_element_type=F32)
            out_ref[here, lanes] = mixed.astype(BF)
            log_ref[here, lanes] = jnp.broadcast_to(top + jnp.log(total), (TILE, HEAD_DIM))


def attend_back_kernel(low_ref, qkv_ref, grad_ref, log_ref, out_ref, keys_sum, values_sum):
    width = grad_ref.shape[1]
    for head in range(width // HEAD_DIM):
        lanes = slice(head * HEAD_DIM, (head + 1) * HEAD_DIM)
        key_lanes = slice(width + head * HEAD_DIM, width + (head + 1) * HEAD_DIM)
        value_lanes = slice(2 * width + head * HEAD_DIM, 2 * width + (head + 1) * HEAD_DIM)
        keys_sum[...] = jnp.zeros_like(keys_sum)
        values_sum[...] = jnp.zeros_like(values_sum)
        for tile in range(SLOTS // TILE):
            here = slice(tile * TILE, (tile + 1) * TILE)
            keys = (tile + 1) * TILE
            mask = tile_mask(low_ref[here], tile, keys)
            query = qkv_ref[here, lanes]
            key = qkv_ref[:keys, key_lanes]
            value = qkv_ref[:keys, value_lanes]
            grad = grad_ref[here, lanes]
            scores = dot_nt(query, key) - log_ref[here, head * HEAD_DIM : head * HEAD_DIM + 1]
            weights = jnp.exp(jnp.where(mask, scores, FLOOR))
            grad_weights = dot_nt(grad, value)
            product = weights * grad_weights
            inner = jnp.sum(product, axis=-1, keepdims=True)
            grad_scores = (product - weights * inner).astype(BF)
            values_sum[:keys] += dot_tn(weights.astype(BF), grad)
            keys_sum[:keys] += dot_tn(grad_scores, query)
            grad_query = jnp.dot(grad_scores, key, preferred_element_type=F32).astype(BF)
            out_ref[here, lanes] = (grad_query.astype(F32) * HEAD_DIM ** (-0.5)).astype(BF)
        out_ref[:, key_lanes] = keys_sum[...].astype(BF)
        out_ref[:, value_lanes] = values_sum[...].astype(BF)


def on_chip(kernel, shapes, scratch, flops, exps, *operands):
    moved = sum(o.size * o.dtype.itemsize for o in (*operands, *shapes))
    return pl.pallas_call(
        kernel,
        out_shape=shapes,
        in_specs=[pl.BlockSpec(memory_space=pltpu.VMEM)] * len(operands),
        out_specs=[pl.BlockSpec(memory_space=pltpu.VMEM)] * len(shapes),
        scratch_shapes=scratch,
        compiler_params=pltpu.CompilerParams(vmem_limit_bytes=50 * 2**20),
        cost_estimate=pl.CostEstimate(flops=flops, bytes_accessed=moved, transcendentals=exps),
    )(*operands)


def attend(low, qkv):
    width = qkv.shape[1] // 3
    shapes = [
        jax.ShapeDtypeStruct((SLOTS, width), BF),
        jax.ShapeDtypeStruct((SLOTS, width), F32),
    ]
    pairs = SLOTS * SLOTS * width // HEAD_DIM
    return on_chip(attend_kernel, shapes, [], 16 * pairs * HEAD_DIM, pairs, low, qkv)


def attend_back(low, qkv, grad, log_total):
    shapes = [jax.ShapeDtypeStruct(qkv.shape, BF)]
    scratch = [pltpu.VMEM((SLOTS, HEAD_DIM), F32)] * 2
    pairs = SLOTS * SLOTS * grad.shape[1] // HEAD_DIM
    return on_chip(
        attend_back_kernel, shapes, scratch, 40 * pairs * HEAD_DIM, pairs, low, qkv, grad, log_total
    )[0]


def newton_kernel(
    wide_ref, factor_ref, gram_ref, panel_ref, out_ref, gh, gl, rh, rl, sh, sl, vh, vl, qh, ql, th, tl
):
    factor = factor_ref[0]

    def store(pair, place, value):
        high = value.astype(BF)
        pair[0][place] = high
        if pair[1] is not None:
            pair[1][place] = (value - high.astype(F32)).astype(BF)

    def load(pair, place):
        return pair[0][place].astype(F32) + pair[1][place].astype(F32)

    def product(left, right, rows, columns, fine):
        total = jnp.dot(left[0][rows], right[0][:, columns], preferred_element_type=F32)
        if fine:
            total += jnp.dot(left[0][rows], right[1][:, columns], preferred_element_type=F32)
            total += jnp.dot(left[1][rows], right[0][:, columns], preferred_element_type=F32)
        return total

    def span(index):
        return pl.ds(pl.multiple_of(index * ROWS, ROWS), ROWS)

    def tiles(body):
        @pl.loop(0, D // ROWS)
        def _(tile):
            body(span(tile))

    def blocks(target, body):
        @pl.loop(0, D // ROWS)
        def _(i):
            @pl.loop(i, D // ROWS)
            def _(j):
                rows, columns = span(i), span(j)
                row = lax.broadcasted_iota(jnp.int32, (ROWS, ROWS), 0)
                column = lax.broadcasted_iota(jnp.int32, (ROWS, ROWS), 1)
                diagonal = (row == column) & (i == j)
                value = body(rows, columns, diagonal)
                store(target, (columns, rows), value.T)
                store(target, (rows, columns), value)

    gram, rest, poly, both = (gh, gl), (rh, rl), (sh, sl), (vh, vl)
    terms = []
    for shift in SHIFTS:
        terms.append((shift, NS_A + NS_B * shift + NS_C * shift * shift, NS_B + 2 * NS_C * shift))

    def make_poly(source, line, fine):
        def body(rows, columns, diagonal):
            square = product(source, source, rows, columns, fine)
            return line * load(source, (rows, columns)) + NS_C * square

        blocks(poly, body)

    @pl.when(wide_ref[0] == 1)
    def _():
        total, spare = (qh, ql), (th, tl)

        def start(rows):
            store(gram, rows, gram_ref[rows] * (factor * factor))

        tiles(start)
        for step, (shift, unit, line) in enumerate(terms):
            fine = step < 2
            source = gram
            if shift != 0.0:
                source = rest
                blocks(
                    rest,
                    lambda rows, columns, diagonal: load(gram, (rows, columns))
                    - jnp.where(diagonal, shift, 0.0),
                )
            make_poly(source, line, fine)
            if step == 0:
                blocks(
                    total,
                    lambda rows, columns, diagonal: load(poly, (rows, columns))
                    + jnp.where(diagonal, unit, 0.0),
                )
            else:
                blocks(
                    spare,
                    lambda rows, columns, diagonal: unit * load(total, (rows, columns))
                    + product(poly, total, rows, columns, False),
                )
                total, spare = spare, total
            if step < NS_STEPS - 1:
                blocks(
                    both,
                    lambda rows, columns, diagonal: unit * load(gram, (rows, columns))
                    + product(poly, gram, rows, columns, fine),
                )
                blocks(
                    gram,
                    lambda rows, columns, diagonal: unit * load(both, (rows, columns))
                    + product(both, poly, rows, columns, fine),
                )

        def finish(rows):
            value = jnp.dot(total[0][rows], panel_ref[...], preferred_element_type=F32)
            out_ref[rows] = (value * factor).astype(BF)

        tiles(finish)

    @pl.when(wide_ref[0] == 0)
    def _():
        total, spare = (qh, ql), (th, tl)

        def start(rows):
            store(total, rows, panel_ref[rows].astype(F32) * factor)

        tiles(start)
        for shift, unit, line in terms:

            def gram_block(rows, columns, diagonal):
                value = dot_nt(total[0][rows], total[0][columns])
                return value - jnp.where(diagonal, shift, 0.0)

            blocks(rest, gram_block)
            make_poly(rest, line, False)

            def advance(rows):
                value = jnp.dot(poly[0][rows], total[0][...], preferred_element_type=F32)
                store(spare, rows, unit * load(total, rows) + value)

            tiles(advance)
            total, spare = spare, total

        def finish(rows):
            out_ref[rows] = total[0][rows]

        tiles(finish)


def newton(is_wide, factor, gram, panel):
    shape = jax.ShapeDtypeStruct(panel.shape, BF)
    whole, scalar = (pl.BlockSpec(memory_space=m) for m in (pltpu.VMEM, pltpu.SMEM))
    return pl.pallas_call(
        newton_kernel,
        out_shape=shape,
        in_specs=[scalar, scalar, whole, whole],
        out_specs=whole,
        scratch_shapes=[pltpu.VMEM((D, D), BF)] * 12,
        compiler_params=pltpu.CompilerParams(vmem_limit_bytes=50 * 2**20),
        cost_estimate=pl.CostEstimate(
            flops=20 * 2 * D**3, bytes_accessed=5 * 2**20, transcendentals=0
        ),
    )(is_wide.astype(jnp.int32)[None], factor[None], gram, panel)


def on_device(
    tokens,
    cotangent,
    seq_lengths,
    seq_bin,
    qkv_weight,
    out_weight,
    up_weight,
    down_weight,
    norm_gains,
    shared_biases,
    head_biases,
    unit_bias,
    qkv_moment,
    out_moment,
    up_moment,
    down_moment,
    gain_moment,
    bias_moment,
    head_moment,
    unit_moment,
):
    x_index = lax.axis_index("x")
    groups = lax.axis_size("z") * lax.axis_size("y")
    position = lax.axis_index("z") * lax.axis_size("y") + lax.axis_index("y")
    rows_each = qkv_weight.shape[1]
    heads_each = qkv_weight.shape[2]
    units_each = up_weight.shape[1]
    scale = HEAD_DIM ** (-0.5)

    z_steps = distances("z")
    qkv_piece = jnp.concatenate([qkv_weight[t] for t in range(3)], axis=1)
    qkv_piece = grow(qkv_piece, "z", z_steps[0], 0)
    early = qkv_piece
    for lead, distance in enumerate(z_steps[1:]):
        qkv_piece = grow(qkv_piece, "z", distance, lead + 1)
    depth = len(z_steps)
    up_weight_now, out_weight_now, down_weight_now = lax.optimization_barrier(
        (up_weight, out_weight, down_weight, early)
    )[:3]
    up_piece = jnp.concatenate((up_weight_now, out_weight_now.T), axis=1)
    down_piece = fixed(down_weight_now.T)
    down_piece = jnp.stack((down_piece, after(swap(down_piece, "x"), qkv_piece)))
    up_piece = grow(up_piece, "z", z_steps[0], 0, qkv_piece)
    qkv_own = grow(qkv_piece, "y", 1, depth, up_piece)
    qkv_own = qkv_own.reshape(-1, qkv_own.shape[-1])
    qkv = (qkv_own, swap(qkv_own, "x"))
    for lead, distance in enumerate(z_steps[1:]):
        up_piece = grow(up_piece, "z", distance, lead + 1, qkv_own)

    small = jnp.concatenate((head_biases.reshape(-1), unit_bias))
    small = (small, swap(small, "x"))
    zero = jnp.zeros((heads_each,), F32)
    scales = jnp.concatenate((jnp.full((heads_each,), scale, F32), jnp.ones((2 * heads_each,), F32)))

    def project(group):
        shift = jnp.concatenate(
            (small[group][:heads_each], zero, small[group][heads_each : 2 * heads_each])
        )
        value = jnp.dot(normed, qkv[group], preferred_element_type=F32)
        return ((value + shift) * scales).astype(BF)

    start = x_index * SLOTS
    tokens_now, lengths_now = lax.optimization_barrier((tokens, seq_lengths, early))[:2]
    rows = lax.dynamic_slice_in_dim(tokens_now, start, SLOTS, axis=0)
    low, valid = first_key(lengths_now, seq_bin, position * 2 + x_index)
    low = low[:, None]
    source = rows.astype(F32)
    normed = layer_norm(source, norm_gains[0], shared_biases[0]).astype(BF)
    heads = [project(0)]
    for lead, distance in enumerate(z_steps):
        down_piece = grow(down_piece, "z", distance, lead + 1, *((up_piece,) if lead == 0 else (mixed,)))
        if lead == 0:
            mixed, logs = attend(low, after(heads[0], down_piece))
    up_own = grow(up_piece, "y", 1, depth, mixed).reshape(-1, up_piece.shape[-1])
    up_next_x = swap(up_own, "x")
    up = (up_own[:, :units_each], up_next_x[:, :units_each])
    out = (up_own[:, units_each:], up_next_x[:, units_each:])
    heads.append(after(project(1), mixed))
    mixed_x, logs_x = attend(low, heads[1])
    mixed, logs = (mixed, mixed_x), (logs, logs_x)
    down_full = grow(down_piece, "y", 1, depth + 1, mixed_x)
    down_full = down_full.reshape(2, -1, down_piece.shape[-1])
    down = (down_full[0], down_full[1])
    branch = across_cores(dot_nt(mixed[0], out[0]) + dot_nt(mixed[1], out[1]))
    hidden = source + (branch + shared_biases[2])
    normed_two = layer_norm(hidden, norm_gains[1], shared_biases[1]).astype(BF)
    before = [
        jnp.dot(normed_two, up[k], preferred_element_type=F32) + small[k][2 * heads_each :]
        for k in range(2)
    ]
    active = [jax.nn.gelu(b).astype(BF) for b in before]

    grad_rows = lax.dynamic_slice_in_dim(cotangent, start, SLOTS, axis=0)
    grad_rows = grad_rows * valid[:, None].astype(BF)
    grad_result = grad_rows.astype(F32)
    grad_before = [
        jax.vjp(jax.nn.gelu, before[k])[1](
            jnp.dot(grad_rows, down[k], preferred_element_type=F32)
        )[0].astype(BF)
        for k in range(2)
    ]
    grad_partial = fixed(dot_nt(grad_before[0], up[0]) + dot_nt(grad_before[1], up[1]))
    grad_other = swap_cores(grad_partial)
    planes = lax.axis_size("z")
    held, held_two = after(tuple(active), grad_partial), after(normed_two, grad_partial)
    grad_up = [dot_tn(held_two, grad_before[k]).astype(BF) for k in range(2)]
    grad_down = jnp.stack([by_rows(dot_tn(grad_rows, held[k]).astype(BF)) for k in range(2)])
    partial_two = fixed(dot_nt(active[0], down[0]) + dot_nt(active[1], down[1]))

    grad_normed_two = grad_partial.astype(F32) + grad_other.astype(F32)
    grad_hidden, grad_gain_two, grad_shift_two = jax.vjp(
        layer_norm, hidden, norm_gains[1], shared_biases[1]
    )[1](grad_normed_two)
    grad_hidden = grad_hidden + grad_result
    grad_branch = grad_hidden.astype(BF)
    grad_mixed = [jnp.dot(grad_branch, out[k], preferred_element_type=F32).astype(BF) for k in range(2)]
    back_x = attend_back(low, heads[1], grad_mixed[1], logs[1])
    grad_square_x = jnp.concatenate(
        (dot_tn(normed, back_x).astype(BF), dot_tn(grad_branch, mixed[1]).astype(BF)), axis=1
    )
    up_sum = grad_up[0].astype(F32) + after(swap(grad_up[1], "x"), back_x).astype(F32)
    down_sum = split_planes(halve(grad_down, "y", 2, 1, back_x), 1)
    grad_square_x = fixed(grad_square_x)
    square_got = swap(grad_square_x, "x")
    grad_mixed[0] = after(grad_mixed[0], grad_square_x, up_sum, down_sum)
    back = attend_back(low, heads[0], grad_mixed[0], logs[0])
    grad_square = jnp.concatenate(
        (dot_tn(normed, back).astype(BF), dot_tn(grad_branch, mixed[0]).astype(BF)), axis=1
    )
    up_sum = split_planes(halve(by_rows(up_sum), "y", 1, 1, back), 0)
    last = up_sum
    for lead in range(depth - 1, 0, -1):
        down_sum = last = halve(down_sum, "z", lead + 1, z_steps[lead], last)
    square = grad_square.astype(F32) + after(square_got, last).astype(F32)
    last = square
    for lead in range(depth - 1, 0, -1):
        up_sum = last = halve(up_sum, "z", lead, z_steps[lead], last)
    down_sum = last = halve(down_sum, "z", 1, z_steps[0], last)
    sum_up = halve(up_sum, "z", 0, z_steps[0], last)
    down_got = after(swap(fixed(down_sum[1]), "x"), sum_up)
    sum_down = down_sum[0] + down_got.astype(F32)
    square = split_planes(halve(by_rows(square), "y", 1, 1, sum_down), 0)
    square_y = square
    for lead in range(depth - 1, 0, -1):
        square = halve(square, "z", lead, z_steps[lead])

    grad_partial = fixed(dot_nt(back, qkv[0]) + dot_nt(back_x, qkv[1]))
    grad_normed = grad_partial.astype(F32) + swap_cores(grad_partial).astype(F32)
    grad_source, grad_gain_one, grad_shift_one = jax.vjp(
        layer_norm, source, norm_gains[0], shared_biases[0]
    )[1](grad_normed)
    result = hidden + (
        (partial_two.astype(F32) + swap_cores(partial_two).astype(F32)) + shared_biases[3]
    )
    def by_x(mine, theirs):
        return join(mine, theirs, bit_of("x"), 1)

    grad_bias = [jnp.sum(b.astype(F32), axis=0) for b in (back, back_x)]
    grad_heads = [jnp.stack((g[:heads_each], g[2 * heads_each :])) for g in grad_bias]
    grad_units = [jnp.sum(g.astype(F32), axis=0)[None] for g in grad_before]
    vectors = (
        jnp.stack((grad_gain_one, grad_gain_two)),
        jnp.stack(
            (
                grad_shift_one,
                grad_shift_two,
                jnp.sum(grad_branch.astype(F32), axis=0),
                jnp.sum(grad_result, axis=0),
            )
        ),
        by_x(*grad_heads),
        by_x(*grad_units),
    )
    sizes = [v.size for v in vectors]
    flat = jnp.concatenate([v.reshape(-1) for v in vectors]).reshape(-1, 128)
    moments = (
        qkv_moment[0],
        qkv_moment[1],
        qkv_moment[2],
        out_moment.T,
        up_moment,
        down_moment.T,
    )
    spread = groups // 8
    owners = [number * spread for number in (0, 3, 4, 7, 2, 5)]

    def to_owners(numbers, grads):
        nexts = [MOMENTUM * moments[k] + grad for k, grad in zip(numbers, grads)]
        panels = [(grad + MOMENTUM * m).astype(BF) for m, grad in zip(nexts, grads)]
        width = panels[0].shape[1]
        outgoing = jnp.zeros((groups, rows_each, width), BF)
        for number, panel in zip(numbers, panels):
            outgoing = outgoing.at[owners[number]].set(panel)
        incoming = lax.all_to_all(outgoing, ("z", "y"), split_axis=0, concat_axis=0, tiled=True)
        return nexts, incoming.reshape(groups * rows_each, width)

    def swap_parts(value, axis):
        half = value.shape[0] // 2
        return jnp.concatenate((swap(value[:half], axis), swap(value[half:], axis)), axis=0)

    wide_nexts, wide = to_owners((4, 5), (sum_up, sum_down))
    wide = after(wide, square)
    gram = dot_nt(wide, wide).reshape(2, D // 2, D)
    sum_square = halve(square, "z", 0, z_steps[0], gram)
    narrow_nexts, narrow = to_owners(
        (0, 1, 2, 3), [sum_square[:, k * heads_each : (k + 1) * heads_each] for k in range(4)]
    )
    keep, send = take(gram, bit_of("c"), 0)
    gram = keep + after(swap_parts(send, "c"), sum_square)
    gram_got = swap_parts(gram, "x")
    narrow = after(narrow, gram)
    pair = jnp.concatenate((narrow, swap(narrow, "x")), axis=1)
    flat = flat + after(swap(flat, "x"), narrow)
    pair = jnp.concatenate((pair, swap(pair, "c")), axis=1)
    flat = flat + after(swap(flat, "y"), pair)
    gram = gram + after(gram_got, pair, flat)
    half = SLOTS // 2
    core = lax.axis_index("c")
    finals = [fixed(after(result, gram)), fixed(after(grad_hidden + grad_source, gram))]
    got = [swap(lax.dynamic_slice_in_dim(v, core * half, half, axis=0), "x") for v in finals]
    gram = join(gram, swap_parts(gram, "c"), bit_of("c"), 0).reshape(D, D)
    is_wide = (position == owners[4]) | (position == owners[5])
    pair_values = pair.astype(F32)
    norm = jnp.where(is_wide, jnp.trace(gram), jnp.sum(pair_values * pair_values))
    factor = 1.0 / (jnp.sqrt(norm) + 1e-07)
    orth = newton(is_wide, factor, gram, jnp.where(is_wide, wide, pair))
    got, flat, back_sent = lax.optimization_barrier((got, flat, orth))
    back = lax.all_to_all(
        back_sent.reshape(groups, rows_each, units_each),
        ("z", "y"),
        split_axis=0,
        concat_axis=0,
        tiled=True,
    ).astype(F32)
    flat = all_sum(flat, ("z",)).reshape(-1)

    def both_bins(own, received):
        other = join(received, swap(received, "c"), bit_of("c"), 0).reshape(own.shape)
        return join(own, other, bit_of("x"), 0).reshape(-1, D).astype(F32)

    block_out, input_grad = (both_bins(own, r) for own, r in zip(finals, got))
    ends = [sum(sizes[: k + 1]) for k in range(4)]
    pieces = [flat[end - size : end] for end, size in zip(ends, sizes)]
    gains_sum = pieces[0].reshape(2, D)
    biases_sum = pieces[1].reshape(4, D)
    heads_sum = lax.dynamic_index_in_dim(
        pieces[2].reshape(2, 2, heads_each), x_index, 1, keepdims=False
    )
    units_sum = lax.dynamic_index_in_dim(pieces[3].reshape(2, units_each), x_index, 0, False)
    next_moments = (*narrow_nexts, *wide_nexts)
    returned = [back[owners[k]][:, : next_moments[k].shape[1]] for k in range(6)]
    keep_share = 1.0 - RATE * DECAY
    up_factor = math.sqrt(max(1.0, FF / D))
    qkv_next = qkv_weight.astype(F32) * keep_share - RATE * jnp.stack(returned[:3])
    out_next = out_weight.astype(F32) * keep_share - RATE * returned[3].T
    up_next = up_weight.astype(F32) * keep_share - RATE * up_factor * returned[4]
    down_next = down_weight.astype(F32) * keep_share - RATE * returned[5].T
    rate_vector = VECTOR_RATE / math.sqrt(groups * tokens.shape[0])
    gain_moment_next = MOMENTUM * gain_moment + gains_sum
    bias_moment_next = MOMENTUM * bias_moment + biases_sum
    head_moment_next = MOMENTUM * head_moment + heads_sum
    unit_moment_next = MOMENTUM * unit_moment + units_sum
    gain_next = norm_gains - rate_vector * gain_moment_next
    bias_next = shared_biases - rate_vector * bias_moment_next
    head_next = head_biases - rate_vector * head_moment_next
    unit_next = unit_bias - rate_vector * unit_moment_next
    return (
        block_out,
        input_grad,
        jnp.stack(next_moments[:3]),
        qkv_next,
        next_moments[3].T,
        out_next,
        next_moments[4],
        up_next,
        next_moments[5].T,
        down_next,
        gain_moment_next,
        gain_next,
        bias_moment_next,
        bias_next,
        head_moment_next,
        head_next,
        unit_moment_next,
        unit_next,
    )


def solution(mesh):
    dp_size, mp_size = mesh.devices.shape
    split = Mesh(
        mesh.devices.reshape(dp_size // 2, 2, mp_size // 2, 2), ("z", "y", "x", "c")
    )
    dp, mp = ("z", "y"), ("x", "c")
    in_specs = (
        P(dp, None),
        P(dp, None),
        P(),
        P(),
        P(None, dp, mp),
        P(mp, dp),
        P(dp, mp),
        P(mp, dp),
        P(),
        P(),
        P(None, mp),
        P(mp),
        P(None, dp, mp),
        P(mp, dp),
        P(dp, mp),
        P(mp, dp),
        P(),
        P(),
        P(None, mp),
        P(mp),
    )
    out_specs = (
        P(dp, None),
        P(dp, None),
        P(None, dp, mp),
        P(None, dp, mp),
        P(mp, dp),
        P(mp, dp),
        P(dp, mp),
        P(dp, mp),
        P(mp, dp),
        P(mp, dp),
        P(),
        P(),
        P(),
        P(),
        P(None, mp),
        P(None, mp),
        P(mp),
        P(mp),
    )
    return jax.shard_map(
        on_device, mesh=split, in_specs=in_specs, out_specs=out_specs, check_vma=False
    )
```

```python
import math

import jax
import jax.numpy as jnp
from jax import lax
from jax.experimental import pallas as pl
from jax.experimental.pallas import tpu as pltpu
from jax.sharding import Mesh, PartitionSpec as P

D = 768
HEAD_DIM = 64
FF = 3072
SLOTS = 1024
NS_STEPS = 5

EPS = 1e-05
MOMENTUM = 0.9
NS_A = 3.4445
NS_B = -4.775
NS_C = 2.0315
RATE = 1.0
DECAY = 0.01
VECTOR_RATE = 0.1
FLOOR = -1e30
TILE = 256
SHIFTS = (0.0, 0.0, 0.3, 0.8, 0.8)
ROWS = 256

BF = jnp.bfloat16
F32 = jnp.float32


def swap(value, axis, distance=1):
    size = lax.axis_size(axis)
    return lax.ppermute(value, axis, [(i, i ^ distance) for i in range(size)])


def join(mine, theirs, bit, dim):
    low = jnp.where(bit, theirs, mine)
    high = jnp.where(bit, mine, theirs)
    return jnp.stack((low, high), axis=dim)


def distances(axis):
    found = []
    step = lax.axis_size(axis) // 2
    while step >= 1:
        found.append(step)
        step //= 2
    return found


def bit_of(axis, distance=1):
    return (lax.axis_index(axis) // distance) % 2 == 1


def after(value, *others):
    return lax.optimization_barrier((value, *others))[0]


def fixed(value):
    return lax.optimization_barrier(value.astype(BF))


def fixed32(value):
    return lax.optimization_barrier(value)


def grow(piece, axis, distance, dim, *wait):
    got = swap(piece, axis, distance)
    if wait:
        got = after(got, *wait)
    return join(piece, got, bit_of(axis, distance), dim)


def take(value, bit, dim):
    low, high = (lax.index_in_dim(value, k, dim, keepdims=False) for k in (0, 1))
    keep = jnp.where(bit, high, low)
    send = jnp.where(bit, low, high)
    return keep, send


def offer(value, axis, dim, distance):
    keep, send = take(value, bit_of(axis, distance), dim)
    send = fixed(send)
    return keep, send, swap(send, axis, distance)


def settle(offered, *wait):
    keep, _, got = offered
    if wait:
        got = after(got, *wait)
    return keep.astype(F32) + got.astype(F32)


def split_planes(value, dim):
    bits = [2 for _ in distances("z")]
    return value.reshape(*value.shape[:dim], *bits, *value.shape[dim + 1 :])


def by_rows(grad):
    return grad.reshape(lax.axis_size("z"), 2, -1, grad.shape[-1])


def all_sum(value, axes):
    for axis in axes:
        for distance in distances(axis):
            value = value + swap(value, axis, distance)
    return value


def swap_cores(own):
    half = own.shape[0] // 2
    return jnp.concatenate((swap(own[:half], "c"), swap(own[half:], "c")), axis=0)


def across_cores(partial_value):
    own = fixed(partial_value)
    return own.astype(F32) + swap_cores(own).astype(F32)


def layer_norm(rows, gain, shift):
    centre = rows - jnp.mean(rows, axis=-1, keepdims=True)
    spread = jnp.mean(centre * centre, axis=-1, keepdims=True)
    return centre * lax.rsqrt(spread + EPS) * gain + shift


def segments_of(seq_lengths, seq_bin, index):
    count = seq_lengths.shape[0]
    order = jnp.arange(count, dtype=jnp.int32)
    inside = seq_bin == index
    leader = jnp.min(jnp.where(inside, order, count))
    first = jnp.sum(jnp.where(order == leader, seq_lengths, 0))
    total = jnp.sum(jnp.where(inside, seq_lengths, 0))
    slot = jnp.arange(SLOTS, dtype=jnp.int32)
    segment = jnp.where(slot < first, 0, jnp.where(slot < total, 1, slot + 2))
    return (segment, slot < total)


def first_key(seq_lengths, seq_bin, index):
    segment, valid = segments_of(seq_lengths, seq_bin, index)
    slot = jnp.arange(SLOTS, dtype=jnp.int32)
    start = jnp.sum(jnp.where(segment == 0, 1, 0))
    low = jnp.where(segment == 0, 0, jnp.where(segment == 1, start, slot))
    return low, valid


def dot_nt(left, right):
    return lax.dot_general(left, right, (((1,), (1,)), ((), ())), preferred_element_type=F32)


def dot_tn(left, right):
    return lax.dot_general(left, right, (((0,), (0,)), ((), ())), preferred_element_type=F32)


def tile_mask(low, tile, keys):
    shape = (TILE, keys)
    row = lax.broadcasted_iota(jnp.int32, shape, 0) + tile * TILE
    column = lax.broadcasted_iota(jnp.int32, shape, 1)
    return (column <= row) & (column >= low)


def attend_kernel(low_ref, qkv_ref, out_ref, log_ref):
    width = out_ref.shape[1]
    for tile in range(SLOTS // TILE):
        here = slice(tile * TILE, (tile + 1) * TILE)
        keys = (tile + 1) * TILE
        mask = tile_mask(low_ref[here], tile, keys)
        for head in range(width // HEAD_DIM):
            lanes = slice(head * HEAD_DIM, (head + 1) * HEAD_DIM)
            query = qkv_ref[here, lanes]
            key = qkv_ref[:keys, width + head * HEAD_DIM : width + (head + 1) * HEAD_DIM]
            value = qkv_ref[:keys, 2 * width + head * HEAD_DIM : 2 * width + (head + 1) * HEAD_DIM]
            scores = jnp.where(mask, dot_nt(query, key), FLOOR)
            top = jnp.max(scores, axis=-1, keepdims=True)
            raised = jnp.exp(scores - top)
            total = jnp.sum(raised, axis=-1, keepdims=True)
            weights = (raised * (1.0 / total)).astype(BF)
            mixed = jnp.dot(weights, value, preferred_element_type=F32)
            out_ref[here, lanes] = mixed.astype(BF)
            log_ref[here, lanes] = jnp.broadcast_to(top + jnp.log(total), (TILE, HEAD_DIM))


def attend_back_kernel(low_ref, qkv_ref, grad_ref, log_ref, out_ref, keys_sum, values_sum):
    width = grad_ref.shape[1]
    for head in range(width // HEAD_DIM):
        lanes = slice(head * HEAD_DIM, (head + 1) * HEAD_DIM)
        key_lanes = slice(width + head * HEAD_DIM, width + (head + 1) * HEAD_DIM)
        value_lanes = slice(2 * width + head * HEAD_DIM, 2 * width + (head + 1) * HEAD_DIM)
        keys_sum[...] = jnp.zeros_like(keys_sum)
        values_sum[...] = jnp.zeros_like(values_sum)
        for tile in range(SLOTS // TILE):
            here = slice(tile * TILE, (tile + 1) * TILE)
            keys = (tile + 1) * TILE
            mask = tile_mask(low_ref[here], tile, keys)
            query = qkv_ref[here, lanes]
            key = qkv_ref[:keys, key_lanes]
            value = qkv_ref[:keys, value_lanes]
            grad = grad_ref[here, lanes]
            scores = dot_nt(query, key) - log_ref[here, head * HEAD_DIM : head * HEAD_DIM + 1]
            weights = jnp.exp(jnp.where(mask, scores, FLOOR))
            grad_weights = dot_nt(grad, value)
            product = weights * grad_weights
            inner = jnp.sum(product, axis=-1, keepdims=True)
            grad_scores = (product - weights * inner).astype(BF)
            values_sum[:keys] += dot_tn(weights.astype(BF), grad)
            keys_sum[:keys] += dot_tn(grad_scores, query)
            grad_query = jnp.dot(grad_scores, key, preferred_element_type=F32).astype(BF)
            out_ref[here, lanes] = (grad_query.astype(F32) * HEAD_DIM ** (-0.5)).astype(BF)
        out_ref[:, key_lanes] = keys_sum[...].astype(BF)
        out_ref[:, value_lanes] = values_sum[...].astype(BF)


def on_chip(kernel, shapes, scratch, flops, exps, *operands):
    moved = sum(o.size * o.dtype.itemsize for o in (*operands, *shapes))
    return pl.pallas_call(
        kernel,
        out_shape=shapes,
        in_specs=[pl.BlockSpec(memory_space=pltpu.VMEM)] * len(operands),
        out_specs=[pl.BlockSpec(memory_space=pltpu.VMEM)] * len(shapes),
        scratch_shapes=scratch,
        compiler_params=pltpu.CompilerParams(vmem_limit_bytes=50 * 2**20),
        cost_estimate=pl.CostEstimate(flops=flops, bytes_accessed=moved, transcendentals=exps),
    )(*operands)


def attend(low, qkv):
    width = qkv.shape[1] // 3
    shapes = [
        jax.ShapeDtypeStruct((SLOTS, width), BF),
        jax.ShapeDtypeStruct((SLOTS, width), F32),
    ]
    pairs = SLOTS * SLOTS * width // HEAD_DIM
    return on_chip(attend_kernel, shapes, [], 16 * pairs * HEAD_DIM, pairs, low, qkv)


def attend_back(low, qkv, grad, log_total):
    shapes = [jax.ShapeDtypeStruct(qkv.shape, BF)]
    scratch = [pltpu.VMEM((SLOTS, HEAD_DIM), F32)] * 2
    pairs = SLOTS * SLOTS * grad.shape[1] // HEAD_DIM
    return on_chip(
        attend_back_kernel, shapes, scratch, 40 * pairs * HEAD_DIM, pairs, low, qkv, grad, log_total
    )[0]


def newton_kernel(
    wide_ref, factor_ref, terms_ref, gram_ref, panel_ref, out_ref, rest, rh, poly, ph, pl_, total, th
):
    factor = factor_ref[0]
    spans = [slice(k * ROWS, (k + 1) * ROWS) for k in range(D // ROWS)]

    def diagonal(span):
        row = lax.broadcasted_iota(jnp.int32, (ROWS, D), 0) + span.start
        column = lax.broadcasted_iota(jnp.int32, (ROWS, D), 1)
        return row == column

    def parts(value):
        high = value.astype(BF)
        return high, (value - high.astype(F32)).astype(BF)

    def times_poly(value, fine):
        high, low = parts(value)
        result = jnp.dot(high, ph[...], preferred_element_type=F32)
        if fine:
            result += jnp.dot(high, pl_[...], preferred_element_type=F32)
            result += jnp.dot(low, ph[...], preferred_element_type=F32)
        return result

    def make_poly(line):
        for span in spans:
            square = jnp.dot(rh[span], rh[...], preferred_element_type=F32)
            value = line * rest[span] + NS_C * square
            poly[span] = value
            ph[span], pl_[span] = parts(value)

    def terms(step):
        return [terms_ref[4 * step + k] for k in range(4)]

    def wide_step(step, fine, last):
        shift, unit, line, shift_next = terms(step)
        make_poly(line)
        for span in spans:
            value = unit * total[span] + times_poly(total[span], False)
            total[span] = value
            if last:
                th[span] = value.astype(BF)
        if not last:
            for span in spans:
                value = unit * rest[span] + times_poly(rest[span], fine) + shift * poly[span]
                value = jnp.where(diagonal(span), value + unit * shift, value)
                value = unit * value + times_poly(value, fine)
                value = jnp.where(diagonal(span), value - shift_next, value)
                rest[span] = value
                rh[span] = value.astype(BF)

    @pl.when(wide_ref[0] == 1)
    def _():
        for span in spans:
            value = gram_ref[span] * (factor * factor)
            rest[span] = value
            rh[span] = value.astype(BF)
            total[span] = jnp.where(diagonal(span), 1.0, 0.0)

        @pl.loop(0, 2)
        def _(step):
            wide_step(step, True, False)

        @pl.loop(2, NS_STEPS - 1)
        def _(step):
            wide_step(step, False, False)

        wide_step(NS_STEPS - 1, False, True)
        for span in spans:
            value = jnp.dot(th[span], panel_ref[...], preferred_element_type=F32)
            out_ref[span] = (value * factor).astype(BF)

    @pl.when(wide_ref[0] == 0)
    def _():
        for span in spans:
            value = panel_ref[span].astype(F32) * factor
            total[span] = value
            th[span] = value.astype(BF)

        @pl.loop(0, NS_STEPS)
        def _(step):
            shift, unit, line, _ = terms(step)
            for span in spans:
                value = dot_nt(th[span], th[...])
                value = jnp.where(diagonal(span), value - shift, value)
                rest[span] = value
                rh[span] = value.astype(BF)
            make_poly(line)
            for span in spans:
                value = jnp.dot(ph[...], th[:, span], preferred_element_type=F32)
                value = unit * total[:, span] + value
                total[:, span] = value
                th[:, span] = value.astype(BF)

        for span in spans:
            out_ref[span] = th[span]


def newton(is_wide, factor, gram, panel):
    shape = jax.ShapeDtypeStruct(panel.shape, BF)
    whole, scalar = (pl.BlockSpec(memory_space=m) for m in (pltpu.VMEM, pltpu.SMEM))
    terms = []
    for step, shift in enumerate(SHIFTS):
        unit = NS_A + NS_B * shift + NS_C * shift * shift
        following = SHIFTS[step + 1] if step + 1 < NS_STEPS else 0.0
        terms += [shift, unit, NS_B + 2 * NS_C * shift, following]
    full, half = pltpu.VMEM((D, D), F32), pltpu.VMEM((D, D), BF)
    return pl.pallas_call(
        newton_kernel,
        out_shape=shape,
        in_specs=[scalar, scalar, scalar, whole, whole],
        out_specs=whole,
        scratch_shapes=[full, half, full, half, half, full, half],
        compiler_params=pltpu.CompilerParams(vmem_limit_bytes=50 * 2**20),
        cost_estimate=pl.CostEstimate(
            flops=25 * 2 * D**3, bytes_accessed=5 * 2**20, transcendentals=0
        ),
    )(is_wide.astype(jnp.int32)[None], factor[None], jnp.array(terms, F32), gram, panel)


def on_device(
    tokens,
    cotangent,
    seq_lengths,
    seq_bin,
    qkv_weight,
    out_weight,
    up_weight,
    down_weight,
    norm_gains,
    shared_biases,
    head_biases,
    unit_bias,
    qkv_moment,
    out_moment,
    up_moment,
    down_moment,
    gain_moment,
    bias_moment,
    head_moment,
    unit_moment,
):
    x_index = lax.axis_index("x")
    groups = lax.axis_size("z") * lax.axis_size("y")
    position = lax.axis_index("z") * lax.axis_size("y") + lax.axis_index("y")
    rows_each = qkv_weight.shape[1]
    heads_each = qkv_weight.shape[2]
    units_each = up_weight.shape[1]
    scale = HEAD_DIM ** (-0.5)

    z_steps = distances("z")
    qkv_piece = jnp.concatenate([qkv_weight[t] for t in range(3)], axis=1)
    qkv_piece = grow(qkv_piece, "z", z_steps[0], 0)
    early = qkv_piece
    for lead, distance in enumerate(z_steps[1:]):
        qkv_piece = grow(qkv_piece, "z", distance, lead + 1)
    depth = len(z_steps)
    up_weight_now, out_weight_now, down_weight_now = lax.optimization_barrier(
        (up_weight, out_weight, down_weight, early)
    )[:3]
    up_piece = jnp.concatenate((up_weight_now, out_weight_now.T), axis=1)
    down_piece = fixed(down_weight_now.T)
    down_piece = jnp.stack((down_piece, after(swap(down_piece, "x"), qkv_piece)))
    up_piece = grow(up_piece, "z", z_steps[0], 0, qkv_piece)
    qkv_own = grow(qkv_piece, "y", 1, depth, up_piece, down_piece)
    qkv_own = qkv_own.reshape(-1, qkv_own.shape[-1])
    qkv = [qkv_own, swap(qkv_own, "x")]

    biases = after(jnp.concatenate((head_biases.reshape(-1), unit_bias)), early)
    small = (biases, swap(biases, "x"))
    zero = jnp.zeros((heads_each,), F32)
    scales = jnp.concatenate((jnp.full((heads_each,), scale, F32), jnp.ones((2 * heads_each,), F32)))

    def project(group):
        shift = jnp.concatenate(
            (small[group][:heads_each], zero, small[group][heads_each : 2 * heads_each])
        )
        value = jnp.dot(normed, qkv[group], preferred_element_type=F32)
        return ((value + shift) * scales).astype(BF)

    start = x_index * SLOTS
    tokens_now, lengths_now = lax.optimization_barrier((tokens, seq_lengths, early))[:2]
    rows = lax.dynamic_slice_in_dim(tokens_now, start, SLOTS, axis=0)
    low, valid = first_key(lengths_now, seq_bin, position * 2 + x_index)
    low = low[:, None]
    source = rows.astype(F32)
    normed = layer_norm(source, norm_gains[0], shared_biases[0]).astype(BF)
    heads = [project(0)]
    for lead, distance in enumerate(z_steps[1:]):
        up_piece = grow(up_piece, "z", distance, lead + 1, heads[0])
    down_piece = grow(down_piece, "z", z_steps[0], 1, up_piece)
    mixed, logs = attend(low, after(heads[0], down_piece))
    up_own = grow(up_piece, "y", 1, depth, mixed).reshape(-1, up_piece.shape[-1])
    out_own, up_own = up_own[:, units_each:], up_own[:, :units_each]
    out = (out_own, swap(out_own, "x"))
    up_own = fixed(up_own)
    up = (up_own, swap(up_own, "x"))
    for lead, distance in enumerate(z_steps[1:]):
        down_piece = grow(down_piece, "z", distance, lead + 2, up_own)
    qkv[1] = after(qkv[1], down_piece, up_own)
    heads.append(project(1))
    mixed_x, logs_x = attend(low, heads[1])
    mixed, logs = (mixed, mixed_x), (logs, logs_x)
    down_full = grow(down_piece, "y", 1, depth + 1, mixed_x)
    down_full = down_full.reshape(2, -1, down_piece.shape[-1])
    down = (down_full[0], down_full[1])
    branch = across_cores(dot_nt(mixed[0], out[0]) + dot_nt(mixed[1], out[1]))
    branch = after(branch, up[1], down_full)
    hidden = source + (branch + shared_biases[2])
    normed_two = layer_norm(hidden, norm_gains[1], shared_biases[1]).astype(BF)
    before = [
        jnp.dot(normed_two, up[k], preferred_element_type=F32) + small[k][2 * heads_each :]
        for k in range(2)
    ]
    active = [jax.nn.gelu(b).astype(BF) for b in before]

    grad_rows = lax.dynamic_slice_in_dim(cotangent, start, SLOTS, axis=0)
    grad_rows = grad_rows * valid[:, None].astype(BF)
    grad_result = grad_rows.astype(F32)
    grad_before = [
        jax.vjp(jax.nn.gelu, before[k])[1](
            jnp.dot(grad_rows, down[k], preferred_element_type=F32)
        )[0].astype(BF)
        for k in range(2)
    ]
    grad_partial = fixed(dot_nt(grad_before[0], up[0]) + dot_nt(grad_before[1], up[1]))
    grad_other = swap_cores(grad_partial)
    planes = lax.axis_size("z")
    held, held_two = after(tuple(active), grad_partial), after(normed_two, grad_partial)
    grad_down = jnp.stack([by_rows(dot_tn(grad_rows, held[k]).astype(BF)) for k in range(2)])
    down_offer = offer(grad_down, "y", 2, 1)
    grad_up = [
        dot_tn(after(held_two, down_offer[1]), grad_before[k]).astype(BF) for k in range(2)
    ]
    partial_two = fixed(dot_nt(active[0], down[0]) + dot_nt(active[1], down[1]))

    grad_normed_two = grad_partial.astype(F32) + grad_other.astype(F32)
    grad_hidden, grad_gain_two, grad_shift_two = jax.vjp(
        layer_norm, hidden, norm_gains[1], shared_biases[1]
    )[1](grad_normed_two)
    grad_hidden = grad_hidden + grad_result
    grad_branch = grad_hidden.astype(BF)
    grad_mixed = [jnp.dot(grad_branch, out[k], preferred_element_type=F32).astype(BF) for k in range(2)]
    grad_out = [dot_tn(grad_branch, mixed[k]).astype(BF) for k in range(2)]
    grad_up = [jnp.concatenate(pair, axis=1) for pair in zip(grad_up, grad_out)]
    grad_up_x = fixed(grad_up[1])
    up_got = swap(grad_up_x, "x")
    back_x = attend_back(low, heads[1], after(grad_mixed[1], grad_up_x, down_offer[1]), logs[1])
    grad_square_x = fixed(dot_tn(normed, back_x))
    square_got = swap(grad_square_x, "x")
    down_sum = split_planes(settle(down_offer, grad_square_x), 1)
    down_offer = offer(down_sum, "z", depth, z_steps[-1])
    up_sum = grad_up[0].astype(F32) + after(up_got, down_offer[1]).astype(F32)
    up_offer = offer(by_rows(up_sum), "y", 1, 1)
    grad_mixed[0] = after(grad_mixed[0], up_offer[1], down_offer[1])
    back = attend_back(low, heads[0], grad_mixed[0], logs[0])
    grad_square = dot_tn(normed, back).astype(BF)

    def next_down(lead, offered, last):
        summed = settle(offered, last)
        return offer(summed, "z", lead, z_steps[lead - 1])

    for lead in range(depth - 1, 0, -1):
        down_offer = next_down(lead, down_offer, grad_square)
    up_sum = split_planes(settle(up_offer, down_offer[1]), 0)
    up_offer = offer(up_sum, "z", depth - 1, z_steps[-1])
    square = grad_square.astype(F32) + after(square_got, up_offer[1]).astype(F32)
    square_offer = offer(by_rows(square), "y", 1, 1)
    down_sum = settle(down_offer, square_offer[1])
    down_sent = fixed(down_sum[1])
    down_got = swap(down_sent, "x")
    last = down_sent
    for lead in range(depth - 1, 0, -1):
        up_offer = offer(settle(up_offer, last), "z", lead - 1, z_steps[lead - 1])
        last = up_offer[1]
    square = split_planes(settle(square_offer, last), 0)
    square_offer = offer(square, "z", depth - 1, z_steps[-1])
    sum_down = down_sum[0] + after(down_got, square_offer[1]).astype(F32)
    sum_up = settle(up_offer, sum_down)
    sum_out, sum_up = sum_up[:, units_each:], sum_up[:, :units_each]

    grad_partial = fixed(dot_nt(back, qkv[0]) + dot_nt(back_x, qkv[1]))
    grad_normed = grad_partial.astype(F32) + swap_cores(grad_partial).astype(F32)
    grad_source, grad_gain_one, grad_shift_one = jax.vjp(
        layer_norm, source, norm_gains[0], shared_biases[0]
    )[1](grad_normed)
    result = hidden + (
        (partial_two.astype(F32) + swap_cores(partial_two).astype(F32)) + shared_biases[3]
    )
    def by_x(mine, theirs):
        return join(mine, theirs, bit_of("x"), 1)

    grad_bias = [jnp.sum(b.astype(F32), axis=0) for b in (back, back_x)]
    grad_heads = [jnp.stack((g[:heads_each], g[2 * heads_each :])) for g in grad_bias]
    grad_units = [jnp.sum(g.astype(F32), axis=0)[None] for g in grad_before]
    vectors = (
        jnp.stack((grad_gain_one, grad_gain_two)),
        jnp.stack(
            (
                grad_shift_one,
                grad_shift_two,
                jnp.sum(grad_branch.astype(F32), axis=0),
                jnp.sum(grad_result, axis=0),
            )
        ),
        by_x(*grad_heads),
        by_x(*grad_units),
    )
    sizes = [v.size for v in vectors]
    flat = jnp.concatenate([v.reshape(-1) for v in vectors]).reshape(-1, 128)
    moments = (
        qkv_moment[0],
        qkv_moment[1],
        qkv_moment[2],
        out_moment.T,
        up_moment,
        down_moment.T,
    )
    spread = groups // 8
    owners = [number * spread for number in (0, 3, 4, 7, 2, 5)]

    def to_owners(numbers, grads):
        nexts = [MOMENTUM * moments[k] + grad for k, grad in zip(numbers, grads)]
        panels = [(grad + MOMENTUM * m).astype(BF) for m, grad in zip(nexts, grads)]
        width = panels[0].shape[1]
        outgoing = jnp.zeros((groups, rows_each, width), BF)
        for number, panel in zip(numbers, panels):
            outgoing = outgoing.at[owners[number]].set(panel)
        incoming = lax.all_to_all(outgoing, ("z", "y"), split_axis=0, concat_axis=0, tiled=True)
        return nexts, incoming.reshape(groups * rows_each, width)

    def swap_parts(value, axis):
        half = value.shape[0] // 2
        return jnp.concatenate((swap(value[:half], axis), swap(value[half:], axis)), axis=0)

    wide_nexts, wide = to_owners((4, 5), (sum_up, sum_down))
    last = wide
    for lead in range(depth - 1, 0, -1):
        square_offer = offer(settle(square_offer, wide_nexts[1]), "z", lead - 1, z_steps[lead - 1])
        wide = after(wide, square_offer[1])
    gram = dot_nt(wide, wide).reshape(2, D // 2, D)
    keep, send = take(gram, bit_of("c"), 0)
    send = fixed32(send)
    gram_sent = swap_parts(send, "c")
    sum_square = settle(square_offer, send)
    narrow_grads = [sum_square[:, k * heads_each : (k + 1) * heads_each] for k in range(3)]
    narrow_nexts, narrow = to_owners((0, 1, 2, 3), (*narrow_grads, sum_out))
    gram = fixed32(keep + after(gram_sent, sum_square))
    gram_got = swap_parts(gram, "x")
    narrow = after(narrow, gram)
    pair = jnp.concatenate((narrow, swap(narrow, "x")), axis=1)
    flat = flat + after(swap(flat, "x"), narrow)
    pair = jnp.concatenate((pair, swap(pair, "c")), axis=1)
    flat = flat + after(swap(flat, "y"), pair)
    gram = gram + after(gram_got, pair, flat)
    half = SLOTS // 2
    core = lax.axis_index("c")
    finals = [fixed(after(result, gram)), fixed(after(grad_hidden + grad_source, gram))]
    got = [swap(lax.dynamic_slice_in_dim(v, core * half, half, axis=0), "x") for v in finals]
    gram = join(gram, swap_parts(gram, "c"), bit_of("c"), 0).reshape(D, D)
    is_wide = (position == owners[4]) | (position == owners[5])
    pair_values = pair.astype(F32)
    norm = jnp.where(is_wide, jnp.trace(gram), jnp.sum(pair_values * pair_values))
    factor = 1.0 / (jnp.sqrt(norm) + 1e-07)
    orth = newton(is_wide, factor, gram, jnp.where(is_wide, wide, pair))
    got, flat, back_sent = lax.optimization_barrier((got, flat, orth))
    back = lax.all_to_all(
        back_sent.reshape(groups, rows_each, units_each),
        ("z", "y"),
        split_axis=0,
        concat_axis=0,
        tiled=True,
    ).astype(F32)
    flat = all_sum(flat, ("z",)).reshape(-1)

    def both_bins(own, received):
        other = join(received, swap(received, "c"), bit_of("c"), 0).reshape(own.shape)
        return join(own, other, bit_of("x"), 0).reshape(-1, D).astype(F32)

    block_out, input_grad = (both_bins(own, r) for own, r in zip(finals, got))
    ends = [sum(sizes[: k + 1]) for k in range(4)]
    pieces = [flat[end - size : end] for end, size in zip(ends, sizes)]
    gains_sum = pieces[0].reshape(2, D)
    biases_sum = pieces[1].reshape(4, D)
    heads_sum = lax.dynamic_index_in_dim(
        pieces[2].reshape(2, 2, heads_each), x_index, 1, keepdims=False
    )
    units_sum = lax.dynamic_index_in_dim(pieces[3].reshape(2, units_each), x_index, 0, False)
    next_moments = (*narrow_nexts, *wide_nexts)
    returned = [back[owners[k]][:, : next_moments[k].shape[1]] for k in range(6)]
    keep_share = 1.0 - RATE * DECAY
    up_factor = math.sqrt(max(1.0, FF / D))
    qkv_next = qkv_weight.astype(F32) * keep_share - RATE * jnp.stack(returned[:3])
    out_next = out_weight.astype(F32) * keep_share - RATE * returned[3].T
    up_next = up_weight.astype(F32) * keep_share - RATE * up_factor * returned[4]
    down_next = down_weight.astype(F32) * keep_share - RATE * returned[5].T
    rate_vector = VECTOR_RATE / math.sqrt(groups * tokens.shape[0])
    gain_moment_next = MOMENTUM * gain_moment + gains_sum
    bias_moment_next = MOMENTUM * bias_moment + biases_sum
    head_moment_next = MOMENTUM * head_moment + heads_sum
    unit_moment_next = MOMENTUM * unit_moment + units_sum
    gain_next = norm_gains - rate_vector * gain_moment_next
    bias_next = shared_biases - rate_vector * bias_moment_next
    head_next = head_biases - rate_vector * head_moment_next
    unit_next = unit_bias - rate_vector * unit_moment_next
    return (
        block_out,
        input_grad,
        jnp.stack(next_moments[:3]),
        qkv_next,
        next_moments[3].T,
        out_next,
        next_moments[4],
        up_next,
        next_moments[5].T,
        down_next,
        gain_moment_next,
        gain_next,
        bias_moment_next,
        bias_next,
        head_moment_next,
        head_next,
        unit_moment_next,
        unit_next,
    )


def solution(mesh):
    dp_size, mp_size = mesh.devices.shape
    split = Mesh(
        mesh.devices.reshape(dp_size // 2, 2, mp_size // 2, 2), ("z", "y", "x", "c")
    )
    dp, mp = ("z", "y"), ("x", "c")
    in_specs = (
        P(dp, None),
        P(dp, None),
        P(),
        P(),
        P(None, dp, mp),
        P(mp, dp),
        P(dp, mp),
        P(mp, dp),
        P(),
        P(),
        P(None, mp),
        P(mp),
        P(None, dp, mp),
        P(mp, dp),
        P(dp, mp),
        P(mp, dp),
        P(),
        P(),
        P(None, mp),
        P(mp),
    )
    out_specs = (
        P(dp, None),
        P(dp, None),
        P(None, dp, mp),
        P(None, dp, mp),
        P(mp, dp),
        P(mp, dp),
        P(dp, mp),
        P(dp, mp),
        P(mp, dp),
        P(mp, dp),
        P(),
        P(),
        P(),
        P(),
        P(None, mp),
        P(None, mp),
        P(mp),
        P(mp),
    )
    return jax.shard_map(
        on_device, mesh=split, in_specs=in_specs, out_specs=out_specs, check_vma=False
    )
```

```python
import math

import jax
import jax.numpy as jnp
from jax import lax
from jax.experimental import pallas as pl
from jax.experimental.pallas import tpu as pltpu
from jax.sharding import Mesh, PartitionSpec as P

D = 768
HEAD_DIM = 64
FF = 3072
SLOTS = 1024
NS_STEPS = 5

EPS = 1e-05
MOMENTUM = 0.9
NS_A = 3.4445
NS_B = -4.775
NS_C = 2.0315
RATE = 1.0
DECAY = 0.01
VECTOR_RATE = 0.1
FLOOR = -1e30
TILE = 256
SHIFTS = (0.0, 0.0, 0.3, 0.8, 0.8)
ROWS = 256

BF = jnp.bfloat16
F32 = jnp.float32


def swap(value, axis, distance=1):
    size = lax.axis_size(axis)
    return lax.ppermute(value, axis, [(i, i ^ distance) for i in range(size)])


def join(mine, theirs, bit, dim):
    low = jnp.where(bit, theirs, mine)
    high = jnp.where(bit, mine, theirs)
    return jnp.stack((low, high), axis=dim)


def distances(axis):
    found = []
    step = lax.axis_size(axis) // 2
    while step >= 1:
        found.append(step)
        step //= 2
    return found


def bit_of(axis, distance=1):
    return (lax.axis_index(axis) // distance) % 2 == 1


def after(value, *others):
    return lax.optimization_barrier((value, *others))[0]


def fixed(value):
    return lax.optimization_barrier(value.astype(BF))


def fixed32(value):
    return lax.optimization_barrier(value)


def grow(piece, axis, distance, dim, *wait):
    got = swap(piece, axis, distance)
    if wait:
        got = after(got, *wait)
    return join(piece, got, bit_of(axis, distance), dim)


def take(value, bit, dim):
    low, high = (lax.index_in_dim(value, k, dim, keepdims=False) for k in (0, 1))
    keep = jnp.where(bit, high, low)
    send = jnp.where(bit, low, high)
    return keep, send


def offer(value, axis, dim, distance):
    keep, send = take(value, bit_of(axis, distance), dim)
    send = fixed(send)
    return keep, send, swap(send, axis, distance)


def settle(offered, *wait):
    keep, _, got = offered
    if wait:
        got = after(got, *wait)
    return keep.astype(F32) + got.astype(F32)


def split_planes(value, dim):
    bits = [2 for _ in distances("z")]
    return value.reshape(*value.shape[:dim], *bits, *value.shape[dim + 1 :])


def by_rows(grad):
    return grad.reshape(lax.axis_size("z"), 2, -1, grad.shape[-1])


def swap_cores(own):
    half = own.shape[0] // 2
    return jnp.concatenate((swap(own[:half], "c"), swap(own[half:], "c")), axis=0)


def across_cores(partial_value):
    own = fixed(partial_value)
    return own.astype(F32) + swap_cores(own).astype(F32)


def layer_norm(rows, gain, shift):
    centre = rows - jnp.mean(rows, axis=-1, keepdims=True)
    spread = jnp.mean(centre * centre, axis=-1, keepdims=True)
    return centre * lax.rsqrt(spread + EPS) * gain + shift


def segments_of(seq_lengths, seq_bin, index):
    count = seq_lengths.shape[0]
    order = jnp.arange(count, dtype=jnp.int32)
    inside = seq_bin == index
    leader = jnp.min(jnp.where(inside, order, count))
    first = jnp.sum(jnp.where(order == leader, seq_lengths, 0))
    total = jnp.sum(jnp.where(inside, seq_lengths, 0))
    slot = jnp.arange(SLOTS, dtype=jnp.int32)
    segment = jnp.where(slot < first, 0, jnp.where(slot < total, 1, slot + 2))
    return (segment, slot < total)


def first_key(seq_lengths, seq_bin, index):
    segment, valid = segments_of(seq_lengths, seq_bin, index)
    slot = jnp.arange(SLOTS, dtype=jnp.int32)
    start = jnp.sum(jnp.where(segment == 0, 1, 0))
    low = jnp.where(segment == 0, 0, jnp.where(segment == 1, start, slot))
    return low, valid


def dot_nt(left, right):
    return lax.dot_general(left, right, (((1,), (1,)), ((), ())), preferred_element_type=F32)


def dot_tn(left, right):
    return lax.dot_general(left, right, (((0,), (0,)), ((), ())), preferred_element_type=F32)


def tile_mask(low, tile, keys):
    shape = (TILE, keys)
    row = lax.broadcasted_iota(jnp.int32, shape, 0) + tile * TILE
    column = lax.broadcasted_iota(jnp.int32, shape, 1)
    return (column <= row) & (column >= low)


def attend_kernel(low_ref, qkv_ref, out_ref, log_ref):
    width = out_ref.shape[1]
    for tile in range(SLOTS // TILE):
        here = slice(tile * TILE, (tile + 1) * TILE)
        keys = (tile + 1) * TILE
        mask = tile_mask(low_ref[here], tile, keys)
        for head in range(width // HEAD_DIM):
            lanes = slice(head * HEAD_DIM, (head + 1) * HEAD_DIM)
            query = qkv_ref[here, lanes]
            key = qkv_ref[:keys, width + head * HEAD_DIM : width + (head + 1) * HEAD_DIM]
            value = qkv_ref[:keys, 2 * width + head * HEAD_DIM : 2 * width + (head + 1) * HEAD_DIM]
            scores = jnp.where(mask, dot_nt(query, key), FLOOR)
            top = jnp.max(scores, axis=-1, keepdims=True)
            raised = jnp.exp(scores - top)
            total = jnp.sum(raised, axis=-1, keepdims=True)
            weights = (raised * (1.0 / total)).astype(BF)
            mixed = jnp.dot(weights, value, preferred_element_type=F32)
            out_ref[here, lanes] = mixed.astype(BF)
            log_ref[here, lanes] = jnp.broadcast_to(top + jnp.log(total), (TILE, HEAD_DIM))


def attend_back_kernel(low_ref, qkv_ref, grad_ref, log_ref, out_ref, keys_sum, values_sum):
    width = grad_ref.shape[1]
    for head in range(width // HEAD_DIM):
        lanes = slice(head * HEAD_DIM, (head + 1) * HEAD_DIM)
        key_lanes = slice(width + head * HEAD_DIM, width + (head + 1) * HEAD_DIM)
        value_lanes = slice(2 * width + head * HEAD_DIM, 2 * width + (head + 1) * HEAD_DIM)
        keys_sum[...] = jnp.zeros_like(keys_sum)
        values_sum[...] = jnp.zeros_like(values_sum)
        for tile in range(SLOTS // TILE):
            here = slice(tile * TILE, (tile + 1) * TILE)
            keys = (tile + 1) * TILE
            mask = tile_mask(low_ref[here], tile, keys)
            query = qkv_ref[here, lanes]
            key = qkv_ref[:keys, key_lanes]
            value = qkv_ref[:keys, value_lanes]
            grad = grad_ref[here, lanes]
            scores = dot_nt(query, key) - log_ref[here, head * HEAD_DIM : head * HEAD_DIM + 1]
            weights = jnp.exp(jnp.where(mask, scores, FLOOR))
            grad_weights = dot_nt(grad, value)
            product = weights * grad_weights
            inner = jnp.sum(product, axis=-1, keepdims=True)
            grad_scores = (product - weights * inner).astype(BF)
            values_sum[:keys] += dot_tn(weights.astype(BF), grad)
            keys_sum[:keys] += dot_tn(grad_scores, query)
            grad_query = jnp.dot(grad_scores, key, preferred_element_type=F32).astype(BF)
            out_ref[here, lanes] = (grad_query.astype(F32) * HEAD_DIM ** (-0.5)).astype(BF)
        out_ref[:, key_lanes] = keys_sum[...].astype(BF)
        out_ref[:, value_lanes] = values_sum[...].astype(BF)


def on_chip(kernel, shapes, scratch, *operands):
    return pl.pallas_call(
        kernel,
        out_shape=shapes,
        in_specs=[pl.BlockSpec(memory_space=pltpu.VMEM)] * len(operands),
        out_specs=[pl.BlockSpec(memory_space=pltpu.VMEM)] * len(shapes),
        scratch_shapes=scratch,
        compiler_params=pltpu.CompilerParams(vmem_limit_bytes=50 * 2**20),
        cost_estimate=pl.CostEstimate(flops=0, bytes_accessed=0, transcendentals=0),
    )(*operands)


def attend(low, qkv):
    width = qkv.shape[1] // 3
    shapes = [
        jax.ShapeDtypeStruct((SLOTS, width), BF),
        jax.ShapeDtypeStruct((SLOTS, width), F32),
    ]
    return on_chip(attend_kernel, shapes, [], low, qkv)


def attend_back(low, qkv, grad, log_total):
    shapes = [jax.ShapeDtypeStruct(qkv.shape, BF)]
    scratch = [pltpu.VMEM((SLOTS, HEAD_DIM), F32)] * 2
    return on_chip(attend_back_kernel, shapes, scratch, low, qkv, grad, log_total)[0]


def newton_kernel(
    wide_ref, factor_ref, terms_ref, gram_ref, panel_ref, out_ref, rest, rh, poly, ph, pl_, total, th
):
    factor = factor_ref[0]
    spans = [slice(k * ROWS, (k + 1) * ROWS) for k in range(D // ROWS)]

    def diagonal(span):
        row = lax.broadcasted_iota(jnp.int32, (ROWS, D), 0) + span.start
        column = lax.broadcasted_iota(jnp.int32, (ROWS, D), 1)
        return row == column

    def parts(value):
        high = value.astype(BF)
        return high, (value - high.astype(F32)).astype(BF)

    def times_poly(value, fine):
        high, low = parts(value)
        result = jnp.dot(high, ph[...], preferred_element_type=F32)
        if fine:
            result += jnp.dot(high, pl_[...], preferred_element_type=F32)
            result += jnp.dot(low, ph[...], preferred_element_type=F32)
        return result

    def make_poly(line):
        for span in spans:
            square = jnp.dot(rh[span], rh[...], preferred_element_type=F32)
            value = line * rest[span] + NS_C * square
            poly[span] = value
            ph[span], pl_[span] = parts(value)

    def terms(step):
        return [terms_ref[4 * step + k] for k in range(4)]

    def wide_step(step, fine, last):
        shift, unit, line, shift_next = terms(step)
        make_poly(line)
        for span in spans:
            value = unit * total[span] + times_poly(total[span], False)
            total[span] = value
            if last:
                th[span] = value.astype(BF)
        if not last:
            for span in spans:
                value = unit * rest[span] + times_poly(rest[span], fine) + shift * poly[span]
                value = jnp.where(diagonal(span), value + unit * shift, value)
                value = unit * value + times_poly(value, fine)
                value = jnp.where(diagonal(span), value - shift_next, value)
                rest[span] = value
                rh[span] = value.astype(BF)

    @pl.when(wide_ref[0] == 1)
    def _():
        for span in spans:
            value = gram_ref[span] * (factor * factor)
            rest[span] = value
            rh[span] = value.astype(BF)
            total[span] = jnp.where(diagonal(span), 1.0, 0.0)

        @pl.loop(0, 2)
        def _(step):
            wide_step(step, True, False)

        @pl.loop(2, NS_STEPS - 1)
        def _(step):
            wide_step(step, False, False)

        wide_step(NS_STEPS - 1, False, True)
        for span in spans:
            value = jnp.dot(th[span], panel_ref[...], preferred_element_type=F32)
            out_ref[span] = (value * factor).astype(BF)

    @pl.when(wide_ref[0] == 0)
    def _():
        for span in spans:
            value = panel_ref[span].astype(F32) * factor
            total[span] = value
            th[span] = value.astype(BF)

        @pl.loop(0, NS_STEPS)
        def _(step):
            shift, unit, line, _ = terms(step)
            for span in spans:
                value = dot_nt(th[span], th[...])
                value = jnp.where(diagonal(span), value - shift, value)
                rest[span] = value
                rh[span] = value.astype(BF)
            make_poly(line)
            for span in spans:
                value = jnp.dot(ph[...], th[:, span], preferred_element_type=F32)
                value = unit * total[:, span] + value
                total[:, span] = value
                th[:, span] = value.astype(BF)

        for span in spans:
            out_ref[span] = th[span]


def newton(is_wide, factor, gram, panel):
    shape = jax.ShapeDtypeStruct(panel.shape, BF)
    whole, scalar = (pl.BlockSpec(memory_space=m) for m in (pltpu.VMEM, pltpu.SMEM))
    terms = []
    for step, shift in enumerate(SHIFTS):
        unit = NS_A + NS_B * shift + NS_C * shift * shift
        following = SHIFTS[step + 1] if step + 1 < NS_STEPS else 0.0
        terms += [shift, unit, NS_B + 2 * NS_C * shift, following]
    full, half = pltpu.VMEM((D, D), F32), pltpu.VMEM((D, D), BF)
    return pl.pallas_call(
        newton_kernel,
        out_shape=shape,
        in_specs=[scalar, scalar, scalar, whole, whole],
        out_specs=whole,
        scratch_shapes=[full, half, full, half, half, full, half],
        compiler_params=pltpu.CompilerParams(vmem_limit_bytes=50 * 2**20),
        cost_estimate=pl.CostEstimate(
            flops=25 * 2 * D**3, bytes_accessed=5 * 2**20, transcendentals=0
        ),
    )(is_wide.astype(jnp.int32)[None], factor[None], jnp.array(terms, F32), gram, panel)


def on_device(
    tokens,
    cotangent,
    seq_lengths,
    seq_bin,
    qkv_weight,
    out_weight,
    up_weight,
    down_weight,
    norm_gains,
    shared_biases,
    head_biases,
    unit_bias,
    qkv_moment,
    out_moment,
    up_moment,
    down_moment,
    gain_moment,
    bias_moment,
    head_moment,
    unit_moment,
):
    x_index = lax.axis_index("x")
    groups = lax.axis_size("z") * lax.axis_size("y")
    position = lax.axis_index("z") * lax.axis_size("y") + lax.axis_index("y")
    rows_each = qkv_weight.shape[1]
    heads_each = qkv_weight.shape[2]
    units_each = up_weight.shape[1]
    scale = HEAD_DIM ** (-0.5)

    z_steps = distances("z")
    qkv_piece = jnp.concatenate([qkv_weight[t] for t in range(3)], axis=1)
    qkv_piece = grow(qkv_piece, "z", z_steps[0], 0)
    early = qkv_piece
    for lead, distance in enumerate(z_steps[1:]):
        qkv_piece = grow(qkv_piece, "z", distance, lead + 1)
    depth = len(z_steps)
    up_weight_now, out_weight_now, down_weight_now = lax.optimization_barrier(
        (up_weight, out_weight, down_weight, early)
    )[:3]
    up_piece = jnp.concatenate((up_weight_now, out_weight_now.T), axis=1)
    down_piece = fixed(down_weight_now.T)
    down_piece = jnp.stack((down_piece, after(swap(down_piece, "x"), qkv_piece)))
    up_piece = grow(up_piece, "z", z_steps[0], 0, qkv_piece)
    qkv_own = grow(qkv_piece, "y", 1, depth, up_piece, down_piece)
    qkv_own = qkv_own.reshape(-1, qkv_own.shape[-1])
    qkv = [qkv_own, swap(qkv_own, "x")]

    biases = after(jnp.concatenate((head_biases.reshape(-1), unit_bias)), early)
    small = (biases, swap(biases, "x"))
    zero = jnp.zeros((heads_each,), F32)
    scales = jnp.concatenate((jnp.full((heads_each,), scale, F32), jnp.ones((2 * heads_each,), F32)))

    def project(group):
        shift = jnp.concatenate(
            (small[group][:heads_each], zero, small[group][heads_each : 2 * heads_each])
        )
        value = jnp.dot(normed, qkv[group], preferred_element_type=F32)
        return ((value + shift) * scales).astype(BF)

    start = x_index * SLOTS
    tokens_now, lengths_now = lax.optimization_barrier((tokens, seq_lengths, early))[:2]
    rows = lax.dynamic_slice_in_dim(tokens_now, start, SLOTS, axis=0)
    low, valid = first_key(lengths_now, seq_bin, position * 2 + x_index)
    low = low[:, None]
    source = rows.astype(F32)
    normed = layer_norm(source, norm_gains[0], shared_biases[0]).astype(BF)
    heads = [project(0)]
    for lead, distance in enumerate(z_steps[1:]):
        up_piece = grow(up_piece, "z", distance, lead + 1, heads[0])
    down_piece = grow(down_piece, "z", z_steps[0], 1, up_piece)
    mixed, logs = attend(low, after(heads[0], down_piece))
    up_own = grow(up_piece, "y", 1, depth, mixed).reshape(-1, up_piece.shape[-1])
    out_own, up_own = up_own[:, units_each:], up_own[:, :units_each]
    out = (out_own, swap(out_own, "x"))
    up_own = fixed(up_own)
    up = (up_own, swap(up_own, "x"))
    for lead, distance in enumerate(z_steps[1:]):
        down_piece = grow(down_piece, "z", distance, lead + 2, up_own)
    qkv[1] = after(qkv[1], down_piece, up_own)
    heads.append(project(1))
    mixed_x, logs_x = attend(low, heads[1])
    mixed, logs = (mixed, mixed_x), (logs, logs_x)
    down_full = grow(down_piece, "y", 1, depth + 1, mixed_x)
    down_full = down_full.reshape(2, -1, down_piece.shape[-1])
    down = (down_full[0], down_full[1])
    branch = across_cores(dot_nt(mixed[0], out[0]) + dot_nt(mixed[1], out[1]))
    branch = after(branch, up[1], down_full)
    hidden = source + (branch + shared_biases[2])
    normed_two = layer_norm(hidden, norm_gains[1], shared_biases[1]).astype(BF)
    before = [
        jnp.dot(normed_two, up[k], preferred_element_type=F32) + small[k][2 * heads_each :]
        for k in range(2)
    ]
    active = [jax.nn.gelu(b).astype(BF) for b in before]

    grad_rows = lax.dynamic_slice_in_dim(cotangent, start, SLOTS, axis=0)
    grad_rows = grad_rows * valid[:, None].astype(BF)
    grad_result = grad_rows.astype(F32)
    grad_before = [
        jax.vjp(jax.nn.gelu, before[k])[1](
            jnp.dot(grad_rows, down[k], preferred_element_type=F32)
        )[0].astype(BF)
        for k in range(2)
    ]
    grad_partial = fixed(dot_nt(grad_before[0], up[0]) + dot_nt(grad_before[1], up[1]))
    grad_other = swap_cores(grad_partial)
    planes = lax.axis_size("z")
    held, held_two = after(tuple(active), grad_partial), after(normed_two, grad_partial)
    grad_down = jnp.stack([by_rows(dot_tn(grad_rows, held[k]).astype(BF)) for k in range(2)])
    down_offer = offer(grad_down, "y", 2, 1)
    grad_up = [
        dot_tn(after(held_two, down_offer[1]), grad_before[k]).astype(BF) for k in range(2)
    ]
    partial_two = fixed(dot_nt(active[0], down[0]) + dot_nt(active[1], down[1]))

    grad_normed_two = grad_partial.astype(F32) + grad_other.astype(F32)
    grad_hidden, grad_gain_two, grad_shift_two = jax.vjp(
        layer_norm, hidden, norm_gains[1], shared_biases[1]
    )[1](grad_normed_two)
    grad_hidden = grad_hidden + grad_result
    grad_branch = grad_hidden.astype(BF)
    grad_mixed = [jnp.dot(grad_branch, out[k], preferred_element_type=F32).astype(BF) for k in range(2)]
    grad_out = [dot_tn(grad_branch, mixed[k]).astype(BF) for k in range(2)]
    grad_up = [jnp.concatenate(pair, axis=1) for pair in zip(grad_up, grad_out)]
    grad_up_x = fixed(grad_up[1])
    up_got = swap(grad_up_x, "x")
    back_x = attend_back(low, heads[1], after(grad_mixed[1], grad_up_x, down_offer[1]), logs[1])
    grad_square_x = fixed(dot_tn(normed, back_x))
    square_got = swap(grad_square_x, "x")
    down_sum = split_planes(settle(down_offer, grad_square_x), 1)
    down_offer = offer(down_sum, "z", depth, z_steps[-1])
    up_sum = grad_up[0].astype(F32) + after(up_got, down_offer[1]).astype(F32)
    up_offer = offer(by_rows(up_sum), "y", 1, 1)
    grad_mixed[0] = after(grad_mixed[0], up_offer[1], down_offer[1])
    back = attend_back(low, heads[0], grad_mixed[0], logs[0])
    grad_square = dot_tn(normed, back).astype(BF)

    def next_down(lead, offered, last):
        summed = settle(offered, last)
        return offer(summed, "z", lead, z_steps[lead - 1])

    for lead in range(depth - 1, 0, -1):
        down_offer = next_down(lead, down_offer, grad_square)
    up_sum = split_planes(settle(up_offer, down_offer[1]), 0)
    up_offer = offer(up_sum, "z", depth - 1, z_steps[-1])
    square = grad_square.astype(F32) + after(square_got, up_offer[1]).astype(F32)
    square_offer = offer(by_rows(square), "y", 1, 1)
    down_sum = settle(down_offer, square_offer[1])
    down_sent = fixed(down_sum[1])
    down_got = swap(down_sent, "x")
    last = down_sent
    for lead in range(depth - 1, 0, -1):
        up_offer = offer(settle(up_offer, last), "z", lead - 1, z_steps[lead - 1])
        last = up_offer[1]
    square = split_planes(settle(square_offer, last), 0)
    square_offer = offer(square, "z", depth - 1, z_steps[-1])
    sum_down = down_sum[0] + after(down_got, square_offer[1]).astype(F32)
    sum_up = settle(up_offer, sum_down)
    sum_out, sum_up = sum_up[:, units_each:], sum_up[:, :units_each]

    grad_partial = fixed(dot_nt(back, qkv[0]) + dot_nt(back_x, qkv[1]))
    grad_normed = grad_partial.astype(F32) + swap_cores(grad_partial).astype(F32)
    grad_source, grad_gain_one, grad_shift_one = jax.vjp(
        layer_norm, source, norm_gains[0], shared_biases[0]
    )[1](grad_normed)
    result = hidden + (
        (partial_two.astype(F32) + swap_cores(partial_two).astype(F32)) + shared_biases[3]
    )
    def by_x(mine, theirs):
        return join(mine, theirs, bit_of("x"), 1)

    grad_bias = [jnp.sum(b.astype(F32), axis=0) for b in (back, back_x)]
    grad_heads = [jnp.stack((g[:heads_each], g[2 * heads_each :])) for g in grad_bias]
    grad_units = [jnp.sum(g.astype(F32), axis=0)[None] for g in grad_before]
    vectors = (
        jnp.stack((grad_gain_one, grad_gain_two)),
        jnp.stack(
            (
                grad_shift_one,
                grad_shift_two,
                jnp.sum(grad_branch.astype(F32), axis=0),
                jnp.sum(grad_result, axis=0),
            )
        ),
        by_x(*grad_heads),
        by_x(*grad_units),
    )
    sizes = [v.size for v in vectors]
    flat = jnp.concatenate([v.reshape(-1) for v in vectors]).reshape(-1, 128)
    moments = (
        qkv_moment[0],
        qkv_moment[1],
        qkv_moment[2],
        out_moment.T,
        up_moment,
        down_moment.T,
    )
    spread = groups // 8
    owners = [number * spread for number in (0, 3, 4, 7, 2, 5)]
    planes_xy = ("z", "y")
    everywhere = ("z", "y", "x")
    chips = [owner * 2 + number % 2 for number, owner in enumerate(owners[:4])]

    def updated(numbers, grads):
        nexts = [MOMENTUM * moments[k] + grad for k, grad in zip(numbers, grads)]
        panels = [(grad + MOMENTUM * m).astype(BF) for m, grad in zip(nexts, grads)]
        return nexts, panels

    def to_wide_owners(panels):
        pieces = [jnp.where(position == owners[4], *panels)]
        for k in range(1, groups):
            pairs = [(owner ^ k, owner) for owner in owners[4:]]
            sent = jnp.where(position == owners[4] ^ k, *panels)
            pieces.append(lax.ppermute(sent, planes_xy, pairs))
        return jnp.concatenate(pieces, axis=0)

    def from_wide_owners(orth):
        blocks = orth.reshape(groups, rows_each, -1)
        found = [blocks[0], blocks[0]]
        for k in range(1, groups):
            pairs = [(owner, owner ^ k) for owner in owners[4:]]
            got = lax.ppermute(blocks[k], planes_xy, pairs)
            found = [
                jnp.where(position == owner ^ k, got, value)
                for owner, value in zip(owners[4:], found)
            ]
        return found

    def to_square_owners(panels):
        width = panels[0].shape[1]
        outgoing = jnp.zeros((2 * groups, rows_each, width), BF)
        for chip, panel in zip(chips, panels):
            outgoing = outgoing.at[chip].set(panel)
        incoming = lax.all_to_all(outgoing, everywhere, split_axis=0, concat_axis=0, tiled=True)
        incoming = incoming.reshape(groups, 2, rows_each, width)
        return jnp.moveaxis(incoming, 1, 2).reshape(groups * rows_each, 2 * width)

    def from_square_owners(orth):
        width = heads_each
        outgoing = orth[:, : 2 * width].reshape(groups, rows_each, 2, width)
        outgoing = jnp.moveaxis(outgoing, 2, 1).reshape(2 * groups, rows_each, width)
        back = lax.all_to_all(outgoing, everywhere, split_axis=0, concat_axis=0, tiled=True)
        return [back[chip] for chip in chips]

    def swap_parts(value, axis):
        half = value.shape[0] // 2
        return jnp.concatenate((swap(value[:half], axis), swap(value[half:], axis)), axis=0)

    wide_nexts, wide_panels = updated((4, 5), (sum_up, sum_down))
    wide = to_wide_owners(wide_panels)
    last = wide_nexts[1]
    for lead in range(depth - 1, 0, -1):
        square_offer = offer(settle(square_offer, last), "z", lead - 1, z_steps[lead - 1])
        last = square_offer[1]
    wide = after(wide, last)
    gram = dot_nt(wide, wide).reshape(2, D // 2, D)
    keep, send = take(gram, bit_of("c"), 0)
    send = fixed32(send)
    gram_sent = swap_parts(send, "c")
    sum_square = settle(square_offer, send)
    gram = fixed32(keep + after(gram_sent, sum_square))
    gram_got = swap_parts(gram, "x")
    narrow_grads = [sum_square[:, k * heads_each : (k + 1) * heads_each] for k in range(3)]
    narrow_nexts, narrow_panels = updated((0, 1, 2, 3), (*narrow_grads, sum_out))
    narrow = to_square_owners(narrow_panels)
    flat = flat + after(swap(flat, "x"), narrow_panels[0])
    narrow = after(narrow, gram, flat)
    pair = jnp.concatenate((narrow, swap(narrow, "c")), axis=1)
    flat = flat + after(swap(flat, "y"), pair)
    gram = gram + after(gram_got, pair, flat)
    for distance in z_steps[:-1]:
        flat = flat + after(swap(flat, "z", distance), gram)
    flat_got = swap(flat, "z", z_steps[-1])
    half = SLOTS // 2
    core = lax.axis_index("c")
    finals = [fixed(after(result, gram)), fixed(after(grad_hidden + grad_source, gram))]
    got = [swap(lax.dynamic_slice_in_dim(v, core * half, half, axis=0), "x") for v in finals]
    gram = join(gram, swap_parts(gram, "c"), bit_of("c"), 0).reshape(D, D)
    is_wide = (position == owners[4]) | (position == owners[5])
    pair_values = pair.astype(F32)
    norm = jnp.where(is_wide, jnp.trace(gram), jnp.sum(pair_values * pair_values))
    factor = 1.0 / (jnp.sqrt(norm) + 1e-07)
    orth = newton(is_wide, factor, gram, jnp.where(is_wide, wide, pair))
    got, flat_got, orth = lax.optimization_barrier((got, flat_got, orth))
    wide_back = from_wide_owners(orth)
    square_back = from_square_owners(orth)
    flat = (flat + flat_got).reshape(-1)

    def both_bins(own, received):
        other = join(received, swap(received, "c"), bit_of("c"), 0).reshape(own.shape)
        return join(own, other, bit_of("x"), 0).reshape(-1, D).astype(F32)

    block_out, input_grad = (both_bins(own, r) for own, r in zip(finals, got))
    ends = [sum(sizes[: k + 1]) for k in range(4)]
    pieces = [flat[end - size : end] for end, size in zip(ends, sizes)]
    gains_sum = pieces[0].reshape(2, D)
    biases_sum = pieces[1].reshape(4, D)
    heads_sum = lax.dynamic_index_in_dim(
        pieces[2].reshape(2, 2, heads_each), x_index, 1, keepdims=False
    )
    units_sum = lax.dynamic_index_in_dim(pieces[3].reshape(2, units_each), x_index, 0, False)
    next_moments = (*narrow_nexts, *wide_nexts)
    returned = [value.astype(F32) for value in (*square_back, *wide_back)]
    keep_share = 1.0 - RATE * DECAY
    up_factor = math.sqrt(max(1.0, FF / D))
    qkv_next = qkv_weight.astype(F32) * keep_share - RATE * jnp.stack(returned[:3])
    out_next = out_weight.astype(F32) * keep_share - RATE * returned[3].T
    up_next = up_weight.astype(F32) * keep_share - RATE * up_factor * returned[4]
    down_next = down_weight.astype(F32) * keep_share - RATE * returned[5].T
    rate_vector = VECTOR_RATE / math.sqrt(groups * tokens.shape[0])
    gain_moment_next = MOMENTUM * gain_moment + gains_sum
    bias_moment_next = MOMENTUM * bias_moment + biases_sum
    head_moment_next = MOMENTUM * head_moment + heads_sum
    unit_moment_next = MOMENTUM * unit_moment + units_sum
    gain_next = norm_gains - rate_vector * gain_moment_next
    bias_next = shared_biases - rate_vector * bias_moment_next
    head_next = head_biases - rate_vector * head_moment_next
    unit_next = unit_bias - rate_vector * unit_moment_next
    return (
        block_out,
        input_grad,
        jnp.stack(next_moments[:3]),
        qkv_next,
        next_moments[3].T,
        out_next,
        next_moments[4],
        up_next,
        next_moments[5].T,
        down_next,
        gain_moment_next,
        gain_next,
        bias_moment_next,
        bias_next,
        head_moment_next,
        head_next,
        unit_moment_next,
        unit_next,
    )


def solution(mesh):
    dp_size, mp_size = mesh.devices.shape
    split = Mesh(
        mesh.devices.reshape(dp_size // 2, 2, mp_size // 2, 2), ("z", "y", "x", "c")
    )
    dp, mp = ("z", "y"), ("x", "c")
    in_specs = (
        P(dp, None),
        P(dp, None),
        P(),
        P(),
        P(None, dp, mp),
        P(mp, dp),
        P(dp, mp),
        P(mp, dp),
        P(),
        P(),
        P(None, mp),
        P(mp),
        P(None, dp, mp),
        P(mp, dp),
        P(dp, mp),
        P(mp, dp),
        P(),
        P(),
        P(None, mp),
        P(mp),
    )
    out_specs = (
        P(dp, None),
        P(dp, None),
        P(None, dp, mp),
        P(None, dp, mp),
        P(mp, dp),
        P(mp, dp),
        P(dp, mp),
        P(dp, mp),
        P(mp, dp),
        P(mp, dp),
        P(),
        P(),
        P(),
        P(),
        P(None, mp),
        P(None, mp),
        P(mp),
        P(mp),
    )
    return jax.shard_map(
        on_device, mesh=split, in_specs=in_specs, out_specs=out_specs, check_vma=False
    )
```

```python
import math

import jax
import jax.numpy as jnp
from jax import lax
from jax.experimental import pallas as pl
from jax.experimental.pallas import tpu as pltpu
from jax.sharding import Mesh, PartitionSpec as P

D = 768
HEAD_DIM = 64
FF = 3072
SLOTS = 1024
NS_STEPS = 5

EPS = 1e-05
MOMENTUM = 0.9
NS_A = 3.4445
NS_B = -4.775
NS_C = 2.0315
RATE = 1.0
DECAY = 0.01
VECTOR_RATE = 0.1
FLOOR = -1e30
TILE = 256
SHIFTS = (0.0, 0.0, 0.3, 0.8, 0.8)
ROWS = 256

BF = jnp.bfloat16
F32 = jnp.float32


def swap(value, axis, distance=1):
    size = lax.axis_size(axis)
    return lax.ppermute(value, axis, [(i, i ^ distance) for i in range(size)])


def join(mine, theirs, bit, dim):
    low = jnp.where(bit, theirs, mine)
    high = jnp.where(bit, mine, theirs)
    return jnp.stack((low, high), axis=dim)


def distances(axis):
    found = []
    step = lax.axis_size(axis) // 2
    while step >= 1:
        found.append(step)
        step //= 2
    return found


def bit_of(axis, distance=1):
    return (lax.axis_index(axis) // distance) % 2 == 1


def after(value, *others):
    return lax.optimization_barrier((value, *others))[0]


def fixed(value):
    return lax.optimization_barrier(value.astype(BF))


def fixed32(value):
    return lax.optimization_barrier(value)


def grow(piece, axis, distance, dim, *wait):
    got = swap(piece, axis, distance)
    if wait:
        got = after(got, *wait)
    return join(piece, got, bit_of(axis, distance), dim)


def take(value, bit, dim):
    low, high = (lax.index_in_dim(value, k, dim, keepdims=False) for k in (0, 1))
    keep = jnp.where(bit, high, low)
    send = jnp.where(bit, low, high)
    return keep, send


def offer(value, axis, dim, distance):
    keep, send = take(value, bit_of(axis, distance), dim)
    send = fixed(send)
    return keep, send, swap(send, axis, distance)


def settle(offered, *wait):
    keep, _, got = offered
    if wait:
        got = after(got, *wait)
    return keep.astype(F32) + got.astype(F32)


def split_planes(value, dim):
    bits = [2 for _ in distances("z")]
    return value.reshape(*value.shape[:dim], *bits, *value.shape[dim + 1 :])


def by_rows(grad):
    return grad.reshape(lax.axis_size("z"), 2, -1, grad.shape[-1])


def swap_cores(own):
    half = own.shape[0] // 2
    return jnp.concatenate((swap(own[:half], "c"), swap(own[half:], "c")), axis=0)


def across_cores(partial_value):
    own = fixed(partial_value)
    return own.astype(F32) + swap_cores(own).astype(F32)


def layer_norm(rows, gain, shift):
    centre = rows - jnp.mean(rows, axis=-1, keepdims=True)
    spread = jnp.mean(centre * centre, axis=-1, keepdims=True)
    return centre * lax.rsqrt(spread + EPS) * gain + shift


def segments_of(seq_lengths, seq_bin, index):
    count = seq_lengths.shape[0]
    order = jnp.arange(count, dtype=jnp.int32)
    inside = seq_bin == index
    leader = jnp.min(jnp.where(inside, order, count))
    first = jnp.sum(jnp.where(order == leader, seq_lengths, 0))
    total = jnp.sum(jnp.where(inside, seq_lengths, 0))
    slot = jnp.arange(SLOTS, dtype=jnp.int32)
    segment = jnp.where(slot < first, 0, jnp.where(slot < total, 1, slot + 2))
    return (segment, slot < total)


def first_key(seq_lengths, seq_bin, index):
    segment, valid = segments_of(seq_lengths, seq_bin, index)
    slot = jnp.arange(SLOTS, dtype=jnp.int32)
    start = jnp.sum(jnp.where(segment == 0, 1, 0))
    low = jnp.where(segment == 0, 0, jnp.where(segment == 1, start, slot))
    return low, valid


def dot_nt(left, right):
    return lax.dot_general(left, right, (((1,), (1,)), ((), ())), preferred_element_type=F32)


def dot_tn(left, right):
    return lax.dot_general(left, right, (((0,), (0,)), ((), ())), preferred_element_type=F32)


def tile_mask(low, tile, keys):
    shape = (TILE, keys)
    row = lax.broadcasted_iota(jnp.int32, shape, 0) + tile * TILE
    column = lax.broadcasted_iota(jnp.int32, shape, 1)
    return (column <= row) & (column >= low)


def attend_kernel(low_ref, qkv_ref, out_ref, log_ref):
    width = out_ref.shape[1]
    for tile in range(SLOTS // TILE):
        here = slice(tile * TILE, (tile + 1) * TILE)
        keys = (tile + 1) * TILE
        mask = tile_mask(low_ref[here], tile, keys)
        for head in range(width // HEAD_DIM):
            lanes = slice(head * HEAD_DIM, (head + 1) * HEAD_DIM)
            query = qkv_ref[here, lanes]
            key = qkv_ref[:keys, width + head * HEAD_DIM : width + (head + 1) * HEAD_DIM]
            value = qkv_ref[:keys, 2 * width + head * HEAD_DIM : 2 * width + (head + 1) * HEAD_DIM]
            scores = jnp.where(mask, dot_nt(query, key), FLOOR)
            top = jnp.max(scores, axis=-1, keepdims=True)
            raised = jnp.exp(scores - top)
            total = jnp.sum(raised, axis=-1, keepdims=True)
            weights = (raised * (1.0 / total)).astype(BF)
            mixed = jnp.dot(weights, value, preferred_element_type=F32)
            out_ref[here, lanes] = mixed.astype(BF)
            log_ref[here, lanes] = jnp.broadcast_to(top + jnp.log(total), (TILE, HEAD_DIM))


def attend_back_kernel(low_ref, qkv_ref, grad_ref, log_ref, out_ref, keys_sum, values_sum):
    width = grad_ref.shape[1]
    for head in range(width // HEAD_DIM):
        lanes = slice(head * HEAD_DIM, (head + 1) * HEAD_DIM)
        key_lanes = slice(width + head * HEAD_DIM, width + (head + 1) * HEAD_DIM)
        value_lanes = slice(2 * width + head * HEAD_DIM, 2 * width + (head + 1) * HEAD_DIM)
        keys_sum[...] = jnp.zeros_like(keys_sum)
        values_sum[...] = jnp.zeros_like(values_sum)
        for tile in range(SLOTS // TILE):
            here = slice(tile * TILE, (tile + 1) * TILE)
            keys = (tile + 1) * TILE
            mask = tile_mask(low_ref[here], tile, keys)
            query = qkv_ref[here, lanes]
            key = qkv_ref[:keys, key_lanes]
            value = qkv_ref[:keys, value_lanes]
            grad = grad_ref[here, lanes]
            scores = dot_nt(query, key) - log_ref[here, head * HEAD_DIM : head * HEAD_DIM + 1]
            weights = jnp.exp(jnp.where(mask, scores, FLOOR))
            grad_weights = dot_nt(grad, value)
            product = weights * grad_weights
            inner = jnp.sum(product, axis=-1, keepdims=True)
            grad_scores = (product - weights * inner).astype(BF)
            values_sum[:keys] += dot_tn(weights.astype(BF), grad)
            keys_sum[:keys] += dot_tn(grad_scores, query)
            grad_query = jnp.dot(grad_scores, key, preferred_element_type=F32).astype(BF)
            out_ref[here, lanes] = (grad_query.astype(F32) * HEAD_DIM ** (-0.5)).astype(BF)
        out_ref[:, key_lanes] = keys_sum[...].astype(BF)
        out_ref[:, value_lanes] = values_sum[...].astype(BF)


def on_chip(kernel, shapes, scratch, *operands):
    return pl.pallas_call(
        kernel,
        out_shape=shapes,
        in_specs=[pl.BlockSpec(memory_space=pltpu.VMEM)] * len(operands),
        out_specs=[pl.BlockSpec(memory_space=pltpu.VMEM)] * len(shapes),
        scratch_shapes=scratch,
        compiler_params=pltpu.CompilerParams(vmem_limit_bytes=50 * 2**20),
        cost_estimate=pl.CostEstimate(flops=0, bytes_accessed=0, transcendentals=0),
    )(*operands)


def attend(low, qkv):
    width = qkv.shape[1] // 3
    shapes = [
        jax.ShapeDtypeStruct((SLOTS, width), BF),
        jax.ShapeDtypeStruct((SLOTS, width), F32),
    ]
    return on_chip(attend_kernel, shapes, [], low, qkv)


def attend_back(low, qkv, grad, log_total):
    shapes = [jax.ShapeDtypeStruct(qkv.shape, BF)]
    scratch = [pltpu.VMEM((SLOTS, HEAD_DIM), F32)] * 2
    return on_chip(attend_back_kernel, shapes, scratch, low, qkv, grad, log_total)[0]


def newton_kernel(
    wide_ref, factor_ref, terms_ref, gram_ref, panel_ref, out_ref, rest, rh, poly, ph, pl_, total, th
):
    factor = factor_ref[0]
    spans = [slice(k * ROWS, (k + 1) * ROWS) for k in range(D // ROWS)]

    def diagonal(span):
        row = lax.broadcasted_iota(jnp.int32, (ROWS, D), 0) + span.start
        column = lax.broadcasted_iota(jnp.int32, (ROWS, D), 1)
        return row == column

    def parts(value):
        high = value.astype(BF)
        return high, (value - high.astype(F32)).astype(BF)

    def times_poly(value, fine):
        high, low = parts(value)
        result = jnp.dot(high, ph[...], preferred_element_type=F32)
        if fine:
            result += jnp.dot(high, pl_[...], preferred_element_type=F32)
            result += jnp.dot(low, ph[...], preferred_element_type=F32)
        return result

    def make_poly(line):
        for span in spans:
            square = jnp.dot(rh[span], rh[...], preferred_element_type=F32)
            value = line * rest[span] + NS_C * square
            poly[span] = value
            ph[span], pl_[span] = parts(value)

    def terms(step):
        return [terms_ref[4 * step + k] for k in range(4)]

    def wide_step(step, fine, last):
        shift, unit, line, shift_next = terms(step)
        make_poly(line)
        for span in spans:
            value = unit * total[span] + times_poly(total[span], False)
            total[span] = value
            if last:
                th[span] = value.astype(BF)
        if not last:
            for span in spans:
                value = unit * rest[span] + times_poly(rest[span], fine) + shift * poly[span]
                value = jnp.where(diagonal(span), value + unit * shift, value)
                value = unit * value + times_poly(value, fine)
                value = jnp.where(diagonal(span), value - shift_next, value)
                rest[span] = value
                rh[span] = value.astype(BF)

    @pl.when(wide_ref[0] == 1)
    def _():
        for span in spans:
            value = gram_ref[span] * (factor * factor)
            rest[span] = value
            rh[span] = value.astype(BF)
            total[span] = jnp.where(diagonal(span), 1.0, 0.0)

        @pl.loop(0, 2)
        def _(step):
            wide_step(step, True, False)

        @pl.loop(2, NS_STEPS - 1)
        def _(step):
            wide_step(step, False, False)

        wide_step(NS_STEPS - 1, False, True)
        for span in spans:
            value = jnp.dot(th[span], panel_ref[...], preferred_element_type=F32)
            out_ref[span] = (value * factor).astype(BF)

    @pl.when(wide_ref[0] == 0)
    def _():
        for span in spans:
            value = panel_ref[span].astype(F32) * factor
            total[span] = value
            th[span] = value.astype(BF)

        @pl.loop(0, NS_STEPS)
        def _(step):
            shift, unit, line, _ = terms(step)
            for span in spans:
                value = dot_nt(th[span], th[...])
                value = jnp.where(diagonal(span), value - shift, value)
                rest[span] = value
                rh[span] = value.astype(BF)
            make_poly(line)
            for span in spans:
                value = jnp.dot(ph[...], th[:, span], preferred_element_type=F32)
                value = unit * total[:, span] + value
                total[:, span] = value
                th[:, span] = value.astype(BF)

        for span in spans:
            out_ref[span] = th[span]


def newton(is_wide, factor, gram, panel):
    shape = jax.ShapeDtypeStruct(panel.shape, BF)
    whole, scalar = (pl.BlockSpec(memory_space=m) for m in (pltpu.VMEM, pltpu.SMEM))
    terms = []
    for step, shift in enumerate(SHIFTS):
        unit = NS_A + NS_B * shift + NS_C * shift * shift
        following = SHIFTS[step + 1] if step + 1 < NS_STEPS else 0.0
        terms += [shift, unit, NS_B + 2 * NS_C * shift, following]
    full, half = pltpu.VMEM((D, D), F32), pltpu.VMEM((D, D), BF)
    return pl.pallas_call(
        newton_kernel,
        out_shape=shape,
        in_specs=[scalar, scalar, scalar, whole, whole],
        out_specs=whole,
        scratch_shapes=[full, half, full, half, half, full, half],
        compiler_params=pltpu.CompilerParams(vmem_limit_bytes=50 * 2**20),
        cost_estimate=pl.CostEstimate(
            flops=25 * 2 * D**3, bytes_accessed=5 * 2**20, transcendentals=0
        ),
    )(is_wide.astype(jnp.int32)[None], factor[None], jnp.array(terms, F32), gram, panel)


def on_device(
    tokens,
    cotangent,
    seq_lengths,
    seq_bin,
    qkv_weight,
    out_weight,
    up_weight,
    down_weight,
    norm_gains,
    shared_biases,
    head_biases,
    unit_bias,
    qkv_moment,
    out_moment,
    up_moment,
    down_moment,
    gain_moment,
    bias_moment,
    head_moment,
    unit_moment,
):
    x_index = lax.axis_index("x")
    groups = lax.axis_size("z") * lax.axis_size("y")
    position = lax.axis_index("z") * lax.axis_size("y") + lax.axis_index("y")
    rows_each = qkv_weight.shape[1]
    heads_each = qkv_weight.shape[2]
    units_each = up_weight.shape[1]
    scale = HEAD_DIM ** (-0.5)

    z_steps = distances("z")
    qkv_piece = jnp.concatenate([qkv_weight[t] for t in range(3)], axis=1)
    qkv_piece = grow(qkv_piece, "z", z_steps[0], 0)
    early = qkv_piece
    for lead, distance in enumerate(z_steps[1:]):
        qkv_piece = grow(qkv_piece, "z", distance, lead + 1)
    depth = len(z_steps)
    up_weight_now, out_weight_now, down_weight_now = lax.optimization_barrier(
        (up_weight, out_weight, down_weight, early)
    )[:3]
    up_piece = jnp.concatenate((up_weight_now, out_weight_now.T), axis=1)
    down_piece = fixed(down_weight_now.T)
    down_piece = jnp.stack((down_piece, after(swap(down_piece, "x"), qkv_piece)))
    up_piece = grow(up_piece, "z", z_steps[0], 0, qkv_piece)
    qkv_own = grow(qkv_piece, "y", 1, depth, up_piece, down_piece)
    qkv_own = qkv_own.reshape(-1, qkv_own.shape[-1])
    qkv = [qkv_own, swap(qkv_own, "x")]

    biases = after(jnp.concatenate((head_biases.reshape(-1), unit_bias)), early)
    small = (biases, swap(biases, "x"))
    zero = jnp.zeros((heads_each,), F32)
    scales = jnp.concatenate((jnp.full((heads_each,), scale, F32), jnp.ones((2 * heads_each,), F32)))

    def project(group):
        shift = jnp.concatenate(
            (small[group][:heads_each], zero, small[group][heads_each : 2 * heads_each])
        )
        value = jnp.dot(normed, qkv[group], preferred_element_type=F32)
        return ((value + shift) * scales).astype(BF)

    start = x_index * SLOTS
    tokens_now, lengths_now = lax.optimization_barrier((tokens, seq_lengths, early))[:2]
    rows = lax.dynamic_slice_in_dim(tokens_now, start, SLOTS, axis=0)
    low, valid = first_key(lengths_now, seq_bin, position * 2 + x_index)
    low = low[:, None]
    source = rows.astype(F32)
    normed = layer_norm(source, norm_gains[0], shared_biases[0]).astype(BF)
    heads = [project(0)]
    for lead, distance in enumerate(z_steps[1:]):
        up_piece = grow(up_piece, "z", distance, lead + 1, heads[0], low)
    mixed, logs = attend(low, after(heads[0], up_piece))
    qkv[1] = after(qkv[1], mixed)
    up_own = grow(up_piece, "y", 1, depth, qkv[1]).reshape(-1, up_piece.shape[-1])
    out_own, up_own = up_own[:, units_each:], up_own[:, :units_each]
    up_own = fixed(up_own)
    up_got = swap(up_own, "x")
    out_own = fixed(out_own)
    out_got = swap(out_own, "x")
    down_piece = grow(down_piece, "z", z_steps[0], 1, up_own)
    qkv[1] = after(qkv[1], down_piece, up_own, out_own)
    heads.append(project(1))
    mixed_x, logs_x = attend(low, heads[1])
    out_got, mixed_x = after((out_got, mixed_x), mixed_x)
    out = (out_own, out_got)
    up = (up_own, after(up_got, mixed_x))
    for lead, distance in enumerate(z_steps[1:]):
        down_piece = grow(down_piece, "z", distance, lead + 2, mixed_x)
    down_full = grow(down_piece, "y", 1, depth + 1)
    down_full = down_full.reshape(2, -1, down_piece.shape[-1])
    down = (down_full[0], down_full[1])
    mixed, logs = (mixed, after(mixed_x, up[1], down_piece)), (logs, logs_x)
    branch = across_cores(dot_nt(mixed[0], out[0]) + dot_nt(mixed[1], out[1]))
    hidden = source + (branch + shared_biases[2])
    normed_two = layer_norm(hidden, norm_gains[1], shared_biases[1]).astype(BF)
    before = [
        jnp.dot(normed_two, up[k], preferred_element_type=F32) + small[k][2 * heads_each :]
        for k in range(2)
    ]
    active = [jax.nn.gelu(b).astype(BF) for b in before]

    grad_rows = lax.dynamic_slice_in_dim(cotangent, start, SLOTS, axis=0)
    grad_rows = grad_rows * valid[:, None].astype(BF)
    grad_result = grad_rows.astype(F32)
    grad_before = [
        jax.vjp(jax.nn.gelu, before[k])[1](
            jnp.dot(grad_rows, down[k], preferred_element_type=F32)
        )[0].astype(BF)
        for k in range(2)
    ]
    grad_partial = fixed(dot_nt(grad_before[0], up[0]) + dot_nt(grad_before[1], up[1]))
    grad_other = swap_cores(grad_partial)
    planes = lax.axis_size("z")
    held, held_two = after(tuple(active), grad_partial), after(normed_two, grad_partial)
    grad_down = jnp.stack([by_rows(dot_tn(grad_rows, held[k]).astype(BF)) for k in range(2)])
    down_offer = offer(grad_down, "y", 2, 1)
    grad_up = [
        dot_tn(after(held_two, down_offer[1]), grad_before[k]).astype(BF) for k in range(2)
    ]
    partial_two = fixed(dot_nt(active[0], down[0]) + dot_nt(active[1], down[1]))

    grad_normed_two = grad_partial.astype(F32) + grad_other.astype(F32)
    grad_hidden, grad_gain_two, grad_shift_two = jax.vjp(
        layer_norm, hidden, norm_gains[1], shared_biases[1]
    )[1](grad_normed_two)
    grad_hidden = grad_hidden + grad_result
    grad_branch = grad_hidden.astype(BF)
    grad_mixed = [jnp.dot(grad_branch, out[k], preferred_element_type=F32).astype(BF) for k in range(2)]
    grad_out = [dot_tn(grad_branch, mixed[k]).astype(BF) for k in range(2)]
    grad_up = [jnp.concatenate(pair, axis=1) for pair in zip(grad_up, grad_out)]
    grad_up_x = fixed(grad_up[1])
    up_got = swap(grad_up_x, "x")
    back_x = attend_back(low, heads[1], after(grad_mixed[1], grad_up_x, down_offer[1]), logs[1])
    up_got = after(up_got, back_x)
    up_sum = by_rows(grad_up[0]).astype(F32) + by_rows(up_got).astype(F32)
    down_sum = split_planes(settle(down_offer, back_x), 1)
    up_offer = offer(up_sum, "y", 1, 1)
    down_offer = offer(down_sum, "z", depth, z_steps[-1])
    back_x = after(back_x, up_offer[1], down_offer[1])
    grad_square_x = fixed(dot_tn(normed, back_x))
    square_got = swap(grad_square_x, "x")
    grad_mixed[0] = after(grad_mixed[0], grad_square_x)
    back = attend_back(low, heads[0], grad_mixed[0], logs[0])

    def next_down(lead, offered, last):
        summed = settle(offered, last)
        return offer(summed, "z", lead, z_steps[lead - 1])

    up_sum = split_planes(settle(up_offer, back), 0)
    up_offer = offer(up_sum, "z", depth - 1, z_steps[-1])
    for lead in range(depth - 1, 0, -1):
        down_offer = next_down(lead, down_offer, up_offer[1])
    back = after(back, up_offer[1], down_offer[1])
    grad_square = dot_tn(normed, back).astype(BF)
    square_got = after(square_got, grad_square)
    square = by_rows(grad_square).astype(F32) + by_rows(square_got).astype(F32)
    square_offer = offer(square, "y", 1, 1)
    down_sum = settle(down_offer, square_offer[1])
    down_sent = fixed(down_sum[1])
    down_got = swap(down_sent, "x")
    last = down_sent
    for lead in range(depth - 1, 0, -1):
        up_offer = offer(settle(up_offer, last), "z", lead - 1, z_steps[lead - 1])
        last = up_offer[1]
    square = split_planes(settle(square_offer, last), 0)
    square_offer = offer(square, "z", depth - 1, z_steps[-1])
    sum_down = down_sum[0] + after(down_got, square_offer[1]).astype(F32)
    sum_up = settle(up_offer, sum_down)
    sum_out, sum_up = sum_up[:, units_each:], sum_up[:, :units_each]

    grad_partial = fixed(dot_nt(back, qkv[0]) + dot_nt(back_x, qkv[1]))
    grad_normed = grad_partial.astype(F32) + swap_cores(grad_partial).astype(F32)
    grad_source, grad_gain_one, grad_shift_one = jax.vjp(
        layer_norm, source, norm_gains[0], shared_biases[0]
    )[1](grad_normed)
    result = hidden + (
        (partial_two.astype(F32) + swap_cores(partial_two).astype(F32)) + shared_biases[3]
    )
    def by_x(mine, theirs):
        return join(mine, theirs, bit_of("x"), 1)

    grad_bias = [jnp.sum(b.astype(F32), axis=0) for b in (back, back_x)]
    grad_heads = [jnp.stack((g[:heads_each], g[2 * heads_each :])) for g in grad_bias]
    grad_units = [jnp.sum(g.astype(F32), axis=0)[None] for g in grad_before]
    vectors = (
        jnp.stack((grad_gain_one, grad_gain_two)),
        jnp.stack(
            (
                grad_shift_one,
                grad_shift_two,
                jnp.sum(grad_branch.astype(F32), axis=0),
                jnp.sum(grad_result, axis=0),
            )
        ),
        by_x(*grad_heads),
        by_x(*grad_units),
    )
    sizes = [v.size for v in vectors]
    flat = jnp.concatenate([v.reshape(-1) for v in vectors]).reshape(-1, 128)
    moments = (
        qkv_moment[0],
        qkv_moment[1],
        qkv_moment[2],
        out_moment.T,
        up_moment,
        down_moment.T,
    )
    spread = groups // 8
    owners = [number * spread for number in (0, 3, 4, 7, 2, 5)]

    def to_owners(numbers, grads):
        nexts = [MOMENTUM * moments[k] + grad for k, grad in zip(numbers, grads)]
        panels = [(grad + MOMENTUM * m).astype(BF) for m, grad in zip(nexts, grads)]
        width = panels[0].shape[1]
        outgoing = jnp.zeros((groups, rows_each, width), BF)
        for number, panel in zip(numbers, panels):
            outgoing = outgoing.at[owners[number]].set(panel)
        incoming = lax.all_to_all(outgoing, ("z", "y"), split_axis=0, concat_axis=0, tiled=True)
        return nexts, incoming.reshape(groups * rows_each, width)

    def swap_parts(value, axis):
        half = value.shape[0] // 2
        return jnp.concatenate((swap(value[:half], axis), swap(value[half:], axis)), axis=0)

    wide_nexts, wide = to_owners((4, 5), (sum_up, sum_down))
    last = wide
    for lead in range(depth - 1, 0, -1):
        square_offer = offer(settle(square_offer, wide_nexts[1]), "z", lead - 1, z_steps[lead - 1])
        wide = after(wide, square_offer[1])
    gram = dot_nt(wide, wide).reshape(2, D // 2, D)
    keep, send = take(gram, bit_of("c"), 0)
    send = fixed32(send)
    gram_sent = swap_parts(send, "c")
    sum_square = settle(square_offer, send)
    narrow_grads = [sum_square[:, k * heads_each : (k + 1) * heads_each] for k in range(3)]
    narrow_nexts, narrow = to_owners((0, 1, 2, 3), (*narrow_grads, sum_out))
    gram = fixed32(keep + after(gram_sent, sum_square))
    gram_got = swap_parts(gram, "x")
    narrow = after(narrow, gram)
    pair = jnp.concatenate((narrow, swap(narrow, "x")), axis=1)
    flat = flat + after(swap(flat, "x"), narrow)
    pair = jnp.concatenate((pair, swap(pair, "c")), axis=1)
    flat = flat + after(swap(flat, "y"), pair)
    gram = gram + after(gram_got, pair, flat)
    for distance in z_steps[:-1]:
        flat = flat + after(swap(flat, "z", distance), gram)
    flat_got = swap(flat, "z", z_steps[-1])
    half = SLOTS // 2
    core = lax.axis_index("c")
    finals = [fixed(after(result, gram)), fixed(after(grad_hidden + grad_source, gram))]
    got = [swap(lax.dynamic_slice_in_dim(v, core * half, half, axis=0), "x") for v in finals]
    gram = join(gram, swap_parts(gram, "c"), bit_of("c"), 0).reshape(D, D)
    is_wide = (position == owners[4]) | (position == owners[5])
    pair_values = pair.astype(F32)
    norm = jnp.where(is_wide, jnp.trace(gram), jnp.sum(pair_values * pair_values))
    factor = 1.0 / (jnp.sqrt(norm) + 1e-07)
    orth = newton(is_wide, factor, gram, jnp.where(is_wide, wide, pair))
    got, flat_got, back_sent = lax.optimization_barrier((got, flat_got, orth))
    back = lax.all_to_all(
        back_sent.reshape(groups, rows_each, units_each),
        ("z", "y"),
        split_axis=0,
        concat_axis=0,
        tiled=True,
    ).astype(F32)
    flat = (flat + flat_got).reshape(-1)

    def both_bins(own, received):
        other = join(received, swap(received, "c"), bit_of("c"), 0).reshape(own.shape)
        return join(own, other, bit_of("x"), 0).reshape(-1, D).astype(F32)

    block_out, input_grad = (both_bins(own, r) for own, r in zip(finals, got))
    ends = [sum(sizes[: k + 1]) for k in range(4)]
    pieces = [flat[end - size : end] for end, size in zip(ends, sizes)]
    gains_sum = pieces[0].reshape(2, D)
    biases_sum = pieces[1].reshape(4, D)
    heads_sum = lax.dynamic_index_in_dim(
        pieces[2].reshape(2, 2, heads_each), x_index, 1, keepdims=False
    )
    units_sum = lax.dynamic_index_in_dim(pieces[3].reshape(2, units_each), x_index, 0, False)
    next_moments = (*narrow_nexts, *wide_nexts)
    returned = [back[owners[k]][:, : next_moments[k].shape[1]] for k in range(6)]
    keep_share = 1.0 - RATE * DECAY
    up_factor = math.sqrt(max(1.0, FF / D))
    qkv_next = qkv_weight.astype(F32) * keep_share - RATE * jnp.stack(returned[:3])
    out_next = out_weight.astype(F32) * keep_share - RATE * returned[3].T
    up_next = up_weight.astype(F32) * keep_share - RATE * up_factor * returned[4]
    down_next = down_weight.astype(F32) * keep_share - RATE * returned[5].T
    rate_vector = VECTOR_RATE / math.sqrt(groups * tokens.shape[0])
    gain_moment_next = MOMENTUM * gain_moment + gains_sum
    bias_moment_next = MOMENTUM * bias_moment + biases_sum
    head_moment_next = MOMENTUM * head_moment + heads_sum
    unit_moment_next = MOMENTUM * unit_moment + units_sum
    gain_next = norm_gains - rate_vector * gain_moment_next
    bias_next = shared_biases - rate_vector * bias_moment_next
    head_next = head_biases - rate_vector * head_moment_next
    unit_next = unit_bias - rate_vector * unit_moment_next
    return (
        block_out,
        input_grad,
        jnp.stack(next_moments[:3]),
        qkv_next,
        next_moments[3].T,
        out_next,
        next_moments[4],
        up_next,
        next_moments[5].T,
        down_next,
        gain_moment_next,
        gain_next,
        bias_moment_next,
        bias_next,
        head_moment_next,
        head_next,
        unit_moment_next,
        unit_next,
    )


def solution(mesh):
    dp_size, mp_size = mesh.devices.shape
    split = Mesh(
        mesh.devices.reshape(dp_size // 2, 2, mp_size // 2, 2), ("z", "y", "x", "c")
    )
    dp, mp = ("z", "y"), ("x", "c")
    in_specs = (
        P(dp, None),
        P(dp, None),
        P(),
        P(),
        P(None, dp, mp),
        P(mp, dp),
        P(dp, mp),
        P(mp, dp),
        P(),
        P(),
        P(None, mp),
        P(mp),
        P(None, dp, mp),
        P(mp, dp),
        P(dp, mp),
        P(mp, dp),
        P(),
        P(),
        P(None, mp),
        P(mp),
    )
    out_specs = (
        P(dp, None),
        P(dp, None),
        P(None, dp, mp),
        P(None, dp, mp),
        P(mp, dp),
        P(mp, dp),
        P(dp, mp),
        P(dp, mp),
        P(mp, dp),
        P(mp, dp),
        P(),
        P(),
        P(),
        P(),
        P(None, mp),
        P(None, mp),
        P(mp),
        P(mp),
    )
    return jax.shard_map(
        on_device, mesh=split, in_specs=in_specs, out_specs=out_specs, check_vma=False
    )
```

```python
import math

import jax
import jax.numpy as jnp
from jax import lax
from jax.experimental import pallas as pl
from jax.experimental.pallas import tpu as pltpu
from jax.sharding import Mesh, PartitionSpec as P

D = 768
HEAD_DIM = 64
FF = 3072
SLOTS = 1024
NS_STEPS = 5

EPS = 1e-05
MOMENTUM = 0.9
NS_A = 3.4445
NS_B = -4.775
NS_C = 2.0315
RATE = 1.0
DECAY = 0.01
VECTOR_RATE = 0.1
FLOOR = -1e30
TILE = 256
SHIFTS = (0.0, 0.0, 0.3, 0.8, 0.8)
ROWS = 256

BF = jnp.bfloat16
F32 = jnp.float32


def swap(value, axis, distance=1):
    size = lax.axis_size(axis)
    return lax.ppermute(value, axis, [(i, i ^ distance) for i in range(size)])


def join(mine, theirs, bit, dim):
    low = jnp.where(bit, theirs, mine)
    high = jnp.where(bit, mine, theirs)
    return jnp.stack((low, high), axis=dim)


def distances(axis):
    found = []
    step = lax.axis_size(axis) // 2
    while step >= 1:
        found.append(step)
        step //= 2
    return found


def bit_of(axis, distance=1):
    return (lax.axis_index(axis) // distance) % 2 == 1


def after(value, *others):
    return lax.optimization_barrier((value, *others))[0]


def fixed(value):
    return lax.optimization_barrier(value.astype(BF))


def fixed32(value):
    return lax.optimization_barrier(value)


def grow(piece, axis, distance, dim, *wait):
    got = swap(piece, axis, distance)
    if wait:
        got = after(got, *wait)
    return join(piece, got, bit_of(axis, distance), dim)


def take(value, bit, dim):
    low, high = (lax.index_in_dim(value, k, dim, keepdims=False) for k in (0, 1))
    keep = jnp.where(bit, high, low)
    send = jnp.where(bit, low, high)
    return keep, send


def offer(value, axis, dim, distance):
    keep, send = take(value, bit_of(axis, distance), dim)
    send = fixed(send)
    return keep, send, swap(send, axis, distance)


def settle(offered, *wait):
    keep, _, got = offered
    if wait:
        got = after(got, *wait)
    return keep.astype(F32) + got.astype(F32)


def split_planes(value, dim):
    bits = [2 for _ in distances("z")]
    return value.reshape(*value.shape[:dim], *bits, *value.shape[dim + 1 :])


def by_rows(grad):
    return grad.reshape(lax.axis_size("z"), 2, -1, grad.shape[-1])


def swap_cores(own):
    half = own.shape[0] // 2
    return jnp.concatenate((swap(own[:half], "c"), swap(own[half:], "c")), axis=0)


def across_cores(partial_value):
    own = fixed(partial_value)
    return own.astype(F32) + swap_cores(own).astype(F32)


def layer_norm(rows, gain, shift):
    centre = rows - jnp.mean(rows, axis=-1, keepdims=True)
    spread = jnp.mean(centre * centre, axis=-1, keepdims=True)
    return centre * lax.rsqrt(spread + EPS) * gain + shift


def segments_of(seq_lengths, seq_bin, index):
    count = seq_lengths.shape[0]
    order = jnp.arange(count, dtype=jnp.int32)
    inside = seq_bin == index
    leader = jnp.min(jnp.where(inside, order, count))
    first = jnp.sum(jnp.where(order == leader, seq_lengths, 0))
    total = jnp.sum(jnp.where(inside, seq_lengths, 0))
    slot = jnp.arange(SLOTS, dtype=jnp.int32)
    segment = jnp.where(slot < first, 0, jnp.where(slot < total, 1, slot + 2))
    return (segment, slot < total)


def first_key(seq_lengths, seq_bin, index):
    segment, valid = segments_of(seq_lengths, seq_bin, index)
    slot = jnp.arange(SLOTS, dtype=jnp.int32)
    start = jnp.sum(jnp.where(segment == 0, 1, 0))
    low = jnp.where(segment == 0, 0, jnp.where(segment == 1, start, slot))
    return low, valid


def dot_nt(left, right):
    return lax.dot_general(left, right, (((1,), (1,)), ((), ())), preferred_element_type=F32)


def dot_tn(left, right):
    return lax.dot_general(left, right, (((0,), (0,)), ((), ())), preferred_element_type=F32)


def tile_mask(low, tile, keys):
    shape = (TILE, keys)
    row = lax.broadcasted_iota(jnp.int32, shape, 0) + tile * TILE
    column = lax.broadcasted_iota(jnp.int32, shape, 1)
    return (column <= row) & (column >= low)


def attend_kernel(low_ref, qkv_ref, out_ref, log_ref):
    width = out_ref.shape[1]
    for tile in range(SLOTS // TILE):
        here = slice(tile * TILE, (tile + 1) * TILE)
        keys = (tile + 1) * TILE
        mask = tile_mask(low_ref[here], tile, keys)
        for head in range(width // HEAD_DIM):
            lanes = slice(head * HEAD_DIM, (head + 1) * HEAD_DIM)
            query = qkv_ref[here, lanes]
            key = qkv_ref[:keys, width + head * HEAD_DIM : width + (head + 1) * HEAD_DIM]
            value = qkv_ref[:keys, 2 * width + head * HEAD_DIM : 2 * width + (head + 1) * HEAD_DIM]
            scores = jnp.where(mask, dot_nt(query, key), FLOOR)
            top = jnp.max(scores, axis=-1, keepdims=True)
            raised = jnp.exp(scores - top)
            total = jnp.sum(raised, axis=-1, keepdims=True)
            weights = (raised * (1.0 / total)).astype(BF)
            mixed = jnp.dot(weights, value, preferred_element_type=F32)
            out_ref[here, lanes] = mixed.astype(BF)
            log_ref[here, lanes] = jnp.broadcast_to(top + jnp.log(total), (TILE, HEAD_DIM))


def attend_back_kernel(low_ref, qkv_ref, grad_ref, log_ref, out_ref, keys_sum, values_sum):
    width = grad_ref.shape[1]
    for head in range(width // HEAD_DIM):
        lanes = slice(head * HEAD_DIM, (head + 1) * HEAD_DIM)
        key_lanes = slice(width + head * HEAD_DIM, width + (head + 1) * HEAD_DIM)
        value_lanes = slice(2 * width + head * HEAD_DIM, 2 * width + (head + 1) * HEAD_DIM)
        keys_sum[...] = jnp.zeros_like(keys_sum)
        values_sum[...] = jnp.zeros_like(values_sum)
        for tile in range(SLOTS // TILE):
            here = slice(tile * TILE, (tile + 1) * TILE)
            keys = (tile + 1) * TILE
            mask = tile_mask(low_ref[here], tile, keys)
            query = qkv_ref[here, lanes]
            key = qkv_ref[:keys, key_lanes]
            value = qkv_ref[:keys, value_lanes]
            grad = grad_ref[here, lanes]
            scores = dot_nt(query, key) - log_ref[here, head * HEAD_DIM : head * HEAD_DIM + 1]
            weights = jnp.exp(jnp.where(mask, scores, FLOOR))
            grad_weights = dot_nt(grad, value)
            product = weights * grad_weights
            inner = jnp.sum(product, axis=-1, keepdims=True)
            grad_scores = (product - weights * inner).astype(BF)
            values_sum[:keys] += dot_tn(weights.astype(BF), grad)
            keys_sum[:keys] += dot_tn(grad_scores, query)
            grad_query = jnp.dot(grad_scores, key, preferred_element_type=F32).astype(BF)
            out_ref[here, lanes] = (grad_query.astype(F32) * HEAD_DIM ** (-0.5)).astype(BF)
        out_ref[:, key_lanes] = keys_sum[...].astype(BF)
        out_ref[:, value_lanes] = values_sum[...].astype(BF)


def on_chip(kernel, shapes, scratch, *operands):
    return pl.pallas_call(
        kernel,
        out_shape=shapes,
        in_specs=[pl.BlockSpec(memory_space=pltpu.VMEM)] * len(operands),
        out_specs=[pl.BlockSpec(memory_space=pltpu.VMEM)] * len(shapes),
        scratch_shapes=scratch,
        compiler_params=pltpu.CompilerParams(vmem_limit_bytes=50 * 2**20),
        cost_estimate=pl.CostEstimate(flops=0, bytes_accessed=0, transcendentals=0),
    )(*operands)


def attend(low, qkv):
    width = qkv.shape[1] // 3
    shapes = [
        jax.ShapeDtypeStruct((SLOTS, width), BF),
        jax.ShapeDtypeStruct((SLOTS, width), F32),
    ]
    return on_chip(attend_kernel, shapes, [], low, qkv)


def attend_back(low, qkv, grad, log_total):
    shapes = [jax.ShapeDtypeStruct(qkv.shape, BF)]
    scratch = [pltpu.VMEM((SLOTS, HEAD_DIM), F32)] * 2
    return on_chip(attend_back_kernel, shapes, scratch, low, qkv, grad, log_total)[0]


def newton_kernel(
    wide_ref, factor_ref, terms_ref, gram_ref, panel_ref, out_ref, rest, rh, poly, ph, pl_, total, th
):
    factor = factor_ref[0]
    spans = [slice(k * ROWS, (k + 1) * ROWS) for k in range(D // ROWS)]

    def diagonal(span):
        row = lax.broadcasted_iota(jnp.int32, (ROWS, D), 0) + span.start
        column = lax.broadcasted_iota(jnp.int32, (ROWS, D), 1)
        return row == column

    def parts(value):
        high = value.astype(BF)
        return high, (value - high.astype(F32)).astype(BF)

    def times_poly(value, fine):
        high, low = parts(value)
        result = jnp.dot(high, ph[...], preferred_element_type=F32)
        if fine:
            result += jnp.dot(high, pl_[...], preferred_element_type=F32)
            result += jnp.dot(low, ph[...], preferred_element_type=F32)
        return result

    def make_poly(line):
        for span in spans:
            square = jnp.dot(rh[span], rh[...], preferred_element_type=F32)
            value = line * rest[span] + NS_C * square
            poly[span] = value
            ph[span], pl_[span] = parts(value)

    def terms(step):
        return [terms_ref[4 * step + k] for k in range(4)]

    def wide_step(step, fine, last):
        shift, unit, line, shift_next = terms(step)
        make_poly(line)
        for span in spans:
            value = unit * total[span] + times_poly(total[span], False)
            total[span] = value
            if last:
                th[span] = value.astype(BF)
        if not last:
            for span in spans:
                value = unit * rest[span] + times_poly(rest[span], fine) + shift * poly[span]
                value = jnp.where(diagonal(span), value + unit * shift, value)
                value = unit * value + times_poly(value, fine)
                value = jnp.where(diagonal(span), value - shift_next, value)
                rest[span] = value
                rh[span] = value.astype(BF)

    @pl.when(wide_ref[0] == 1)
    def _():
        for span in spans:
            value = gram_ref[span] * (factor * factor)
            rest[span] = value
            rh[span] = value.astype(BF)
            total[span] = jnp.where(diagonal(span), 1.0, 0.0)

        @pl.loop(0, 2)
        def _(step):
            wide_step(step, True, False)

        @pl.loop(2, NS_STEPS - 1)
        def _(step):
            wide_step(step, False, False)

        wide_step(NS_STEPS - 1, False, True)
        for span in spans:
            value = jnp.dot(th[span], panel_ref[...], preferred_element_type=F32)
            out_ref[span] = (value * factor).astype(BF)

    @pl.when(wide_ref[0] == 0)
    def _():
        for span in spans:
            value = panel_ref[span].astype(F32) * factor
            total[span] = value
            th[span] = value.astype(BF)

        @pl.loop(0, NS_STEPS)
        def _(step):
            shift, unit, line, _ = terms(step)
            for span in spans:
                value = dot_nt(th[span], th[...])
                value = jnp.where(diagonal(span), value - shift, value)
                rest[span] = value
                rh[span] = value.astype(BF)
            make_poly(line)
            for span in spans:
                value = jnp.dot(ph[...], th[:, span], preferred_element_type=F32)
                value = unit * total[:, span] + value
                total[:, span] = value
                th[:, span] = value.astype(BF)

        for span in spans:
            out_ref[span] = th[span]


def newton(is_wide, factor, gram, panel):
    shape = jax.ShapeDtypeStruct(panel.shape, BF)
    whole, scalar = (pl.BlockSpec(memory_space=m) for m in (pltpu.VMEM, pltpu.SMEM))
    terms = []
    for step, shift in enumerate(SHIFTS):
        unit = NS_A + NS_B * shift + NS_C * shift * shift
        following = SHIFTS[step + 1] if step + 1 < NS_STEPS else 0.0
        terms += [shift, unit, NS_B + 2 * NS_C * shift, following]
    full, half = pltpu.VMEM((D, D), F32), pltpu.VMEM((D, D), BF)
    return pl.pallas_call(
        newton_kernel,
        out_shape=shape,
        in_specs=[scalar, scalar, scalar, whole, whole],
        out_specs=whole,
        scratch_shapes=[full, half, full, half, half, full, half],
        compiler_params=pltpu.CompilerParams(vmem_limit_bytes=50 * 2**20),
        cost_estimate=pl.CostEstimate(
            flops=25 * 2 * D**3, bytes_accessed=5 * 2**20, transcendentals=0
        ),
    )(is_wide.astype(jnp.int32)[None], factor[None], jnp.array(terms, F32), gram, panel)


def on_device(
    tokens,
    cotangent,
    seq_lengths,
    seq_bin,
    qkv_weight,
    out_weight,
    up_weight,
    down_weight,
    norm_gains,
    shared_biases,
    head_biases,
    unit_bias,
    qkv_moment,
    out_moment,
    up_moment,
    down_moment,
    gain_moment,
    bias_moment,
    head_moment,
    unit_moment,
):
    x_index = lax.axis_index("x")
    groups = lax.axis_size("z") * lax.axis_size("y")
    position = lax.axis_index("z") * lax.axis_size("y") + lax.axis_index("y")
    rows_each = qkv_weight.shape[1]
    heads_each = qkv_weight.shape[2]
    units_each = up_weight.shape[1]
    scale = HEAD_DIM ** (-0.5)

    z_steps = distances("z")
    qkv_piece = jnp.concatenate([*(qkv_weight[t] for t in range(3)), out_weight.T], axis=1)
    qkv_piece = grow(qkv_piece, "z", z_steps[0], 0)
    early = qkv_piece
    for lead, distance in enumerate(z_steps[1:]):
        qkv_piece = grow(qkv_piece, "z", distance, lead + 1)
    depth = len(z_steps)
    up_piece, down_weight_now = lax.optimization_barrier((up_weight, down_weight, early))[:2]
    down_piece = fixed(down_weight_now.T)
    down_piece = jnp.stack((down_piece, after(swap(down_piece, "x"), qkv_piece)))
    up_piece = grow(up_piece, "z", z_steps[0], 0, qkv_piece)
    qkv_own = grow(qkv_piece, "y", 1, depth, up_piece, down_piece)
    qkv_own = qkv_own.reshape(-1, qkv_own.shape[-1])
    inputs = 3 * heads_each
    qkv = [qkv_own[:, :inputs], None]
    out_own = fixed(qkv_own[:, inputs:])
    qkv_got = swap(qkv_own, "x")

    biases = after(jnp.concatenate((head_biases.reshape(-1), unit_bias)), early)
    small = (biases, swap(biases, "x"))
    zero = jnp.zeros((heads_each,), F32)
    scales = jnp.concatenate((jnp.full((heads_each,), scale, F32), jnp.ones((2 * heads_each,), F32)))

    def project(group):
        shift = jnp.concatenate(
            (small[group][:heads_each], zero, small[group][heads_each : 2 * heads_each])
        )
        value = jnp.dot(normed, qkv[group], preferred_element_type=F32)
        return ((value + shift) * scales).astype(BF)

    start = x_index * SLOTS
    tokens_now, lengths_now = lax.optimization_barrier((tokens, seq_lengths, early))[:2]
    rows = lax.dynamic_slice_in_dim(tokens_now, start, SLOTS, axis=0)
    low, valid = first_key(lengths_now, seq_bin, position * 2 + x_index)
    low = low[:, None]
    source = rows.astype(F32)
    normed = layer_norm(source, norm_gains[0], shared_biases[0]).astype(BF)
    heads = [project(0)]
    for lead, distance in enumerate(z_steps[1:]):
        up_piece = grow(up_piece, "z", distance, lead + 1, heads[0], low)
    mixed, logs = attend(low, after(heads[0], up_piece))
    qkv_got = after(qkv_got, mixed)
    up_own = grow(up_piece, "y", 1, depth, qkv_got).reshape(-1, up_piece.shape[-1])
    up_own = fixed(up_own)
    up_got = swap(up_own, "x")
    down_piece = grow(down_piece, "z", z_steps[0], 1, up_own)
    qkv_got = after(qkv_got, down_piece, up_own)
    qkv[1] = qkv_got[:, :inputs]
    out = (out_own, fixed(qkv_got[:, inputs:]))
    heads.append(project(1))
    mixed_x, logs_x = attend(low, heads[1])
    up = (up_own, after(up_got, mixed_x))
    for lead, distance in enumerate(z_steps[1:]):
        down_piece = grow(down_piece, "z", distance, lead + 2, mixed_x)
    down_full = grow(down_piece, "y", 1, depth + 1)
    down_full = down_full.reshape(2, -1, down_piece.shape[-1])
    down = (down_full[0], down_full[1])
    mixed, logs = (mixed, after(mixed_x, down_piece)), (logs, logs_x)
    branch = across_cores(dot_nt(mixed[0], out[0]) + dot_nt(mixed[1], out[1]))
    branch = after(branch, up[1])
    hidden = source + (branch + shared_biases[2])
    normed_two = layer_norm(hidden, norm_gains[1], shared_biases[1]).astype(BF)
    before = [
        jnp.dot(normed_two, up[k], preferred_element_type=F32) + small[k][2 * heads_each :]
        for k in range(2)
    ]
    active = [jax.nn.gelu(b).astype(BF) for b in before]

    grad_rows = lax.dynamic_slice_in_dim(cotangent, start, SLOTS, axis=0)
    grad_rows = grad_rows * valid[:, None].astype(BF)
    grad_result = grad_rows.astype(F32)
    grad_before = [
        jax.vjp(jax.nn.gelu, before[k])[1](
            jnp.dot(grad_rows, down[k], preferred_element_type=F32)
        )[0].astype(BF)
        for k in range(2)
    ]
    grad_partial = fixed(dot_nt(grad_before[0], up[0]) + dot_nt(grad_before[1], up[1]))
    grad_other = swap_cores(grad_partial)
    planes = lax.axis_size("z")
    held, held_two = after(tuple(active), grad_partial), after(normed_two, grad_partial)
    grad_down = jnp.stack([by_rows(dot_tn(grad_rows, held[k]).astype(BF)) for k in range(2)])
    down_offer = offer(grad_down, "y", 2, 1)
    grad_up = [
        dot_tn(after(held_two, down_offer[1]), grad_before[k]).astype(BF) for k in range(2)
    ]
    partial_two = fixed(dot_nt(active[0], down[0]) + dot_nt(active[1], down[1]))

    grad_normed_two = grad_partial.astype(F32) + grad_other.astype(F32)
    grad_hidden, grad_gain_two, grad_shift_two = jax.vjp(
        layer_norm, hidden, norm_gains[1], shared_biases[1]
    )[1](grad_normed_two)
    grad_hidden = grad_hidden + grad_result
    grad_branch = grad_hidden.astype(BF)
    grad_mixed = [jnp.dot(grad_branch, out[k], preferred_element_type=F32).astype(BF) for k in range(2)]
    grad_out = [dot_tn(grad_branch, mixed[k]).astype(BF) for k in range(2)]
    grad_up = [jnp.concatenate(pair, axis=1) for pair in zip(grad_up, grad_out)]
    grad_up_x = fixed(grad_up[1])
    up_got = swap(grad_up_x, "x")
    back_x = attend_back(low, heads[1], after(grad_mixed[1], grad_up_x, down_offer[1]), logs[1])
    up_got = after(up_got, back_x)
    up_sum = by_rows(grad_up[0]).astype(F32) + by_rows(up_got).astype(F32)
    down_sum = split_planes(settle(down_offer, back_x), 1)
    up_offer = offer(up_sum, "y", 1, 1)
    down_offer = offer(down_sum, "z", depth, z_steps[-1])
    back_x = after(back_x, up_offer[1], down_offer[1])
    grad_square_x = fixed(dot_tn(normed, back_x))
    square_got = swap(grad_square_x, "x")
    grad_mixed[0] = after(grad_mixed[0], grad_square_x)
    back = attend_back(low, heads[0], grad_mixed[0], logs[0])

    def next_down(lead, offered, last):
        summed = settle(offered, last)
        return offer(summed, "z", lead, z_steps[lead - 1])

    up_sum = split_planes(settle(up_offer, back), 0)
    up_offer = offer(up_sum, "z", depth - 1, z_steps[-1])
    for lead in range(depth - 1, 0, -1):
        down_offer = next_down(lead, down_offer, up_offer[1])
    back = after(back, up_offer[1], down_offer[1])
    grad_square = dot_tn(normed, back).astype(BF)
    square_got = after(square_got, grad_square)
    square = by_rows(grad_square).astype(F32) + by_rows(square_got).astype(F32)
    square_offer = offer(square, "y", 1, 1)
    down_sum = settle(down_offer, square_offer[1])
    down_sent = fixed(down_sum[1])
    down_got = swap(down_sent, "x")
    last = down_sent
    for lead in range(depth - 1, 0, -1):
        up_offer = offer(settle(up_offer, last), "z", lead - 1, z_steps[lead - 1])
        last = up_offer[1]
    square = split_planes(settle(square_offer, last), 0)
    square_offer = offer(square, "z", depth - 1, z_steps[-1])
    sum_down = down_sum[0] + after(down_got, square_offer[1]).astype(F32)
    sum_up = settle(up_offer, sum_down)
    sum_out, sum_up = sum_up[:, units_each:], sum_up[:, :units_each]

    grad_partial = fixed(dot_nt(back, qkv[0]) + dot_nt(back_x, qkv[1]))
    grad_normed = grad_partial.astype(F32) + swap_cores(grad_partial).astype(F32)
    grad_source, grad_gain_one, grad_shift_one = jax.vjp(
        layer_norm, source, norm_gains[0], shared_biases[0]
    )[1](grad_normed)
    result = hidden + (
        (partial_two.astype(F32) + swap_cores(partial_two).astype(F32)) + shared_biases[3]
    )
    def by_x(mine, theirs):
        return join(mine, theirs, bit_of("x"), 1)

    grad_bias = [jnp.sum(b.astype(F32), axis=0) for b in (back, back_x)]
    grad_heads = [jnp.stack((g[:heads_each], g[2 * heads_each :])) for g in grad_bias]
    grad_units = [jnp.sum(g.astype(F32), axis=0)[None] for g in grad_before]
    vectors = (
        jnp.stack((grad_gain_one, grad_gain_two)),
        jnp.stack(
            (
                grad_shift_one,
                grad_shift_two,
                jnp.sum(grad_branch.astype(F32), axis=0),
                jnp.sum(grad_result, axis=0),
            )
        ),
        by_x(*grad_heads),
        by_x(*grad_units),
    )
    sizes = [v.size for v in vectors]
    flat = jnp.concatenate([v.reshape(-1) for v in vectors]).reshape(-1, 128)
    moments = (
        qkv_moment[0],
        qkv_moment[1],
        qkv_moment[2],
        out_moment.T,
        up_moment,
        down_moment.T,
    )
    spread = groups // 8
    owners = [number * spread for number in (0, 3, 4, 7, 2, 5)]

    def to_owners(numbers, grads):
        nexts = [MOMENTUM * moments[k] + grad for k, grad in zip(numbers, grads)]
        panels = [(grad + MOMENTUM * m).astype(BF) for m, grad in zip(nexts, grads)]
        width = panels[0].shape[1]
        outgoing = jnp.zeros((groups, rows_each, width), BF)
        for number, panel in zip(numbers, panels):
            outgoing = outgoing.at[owners[number]].set(panel)
        incoming = lax.all_to_all(outgoing, ("z", "y"), split_axis=0, concat_axis=0, tiled=True)
        return nexts, incoming.reshape(groups * rows_each, width)

    def swap_parts(value, axis):
        half = value.shape[0] // 2
        return jnp.concatenate((swap(value[:half], axis), swap(value[half:], axis)), axis=0)

    wide_nexts, wide = to_owners((4, 5), (sum_up, sum_down))
    gram = dot_nt(wide, wide).reshape(2, D // 2, D)
    keep, send = take(gram, bit_of("c"), 0)
    send = fixed32(send)
    gram_sent = swap_parts(send, "c")
    last = send
    for lead in range(depth - 1, 0, -1):
        square_offer = offer(settle(square_offer, last), "z", lead - 1, z_steps[lead - 1])
        last = square_offer[1]
    gram = fixed32(keep + after(gram_sent, last))
    gram_got = swap_parts(gram, "x")
    sum_square = settle(square_offer, gram)
    narrow_grads = [sum_square[:, k * heads_each : (k + 1) * heads_each] for k in range(3)]
    narrow_nexts, narrow = to_owners((0, 1, 2, 3), (*narrow_grads, sum_out))
    gram = fixed32(gram + after(gram_got, narrow_nexts[0]))
    gram_back = swap_parts(gram, "c")
    narrow = after(narrow, gram)
    pair = jnp.concatenate((narrow, swap(narrow, "x")), axis=1)
    gram = join(gram, after(gram_back, narrow), bit_of("c"), 0).reshape(D, D)
    flat = flat + after(swap(flat, "x"), narrow)
    pair = fixed32(jnp.concatenate((pair, swap(pair, "c")), axis=1))
    flat = flat + after(swap(flat, "y"), pair)
    for distance in z_steps[:-1]:
        flat = flat + swap(flat, "z", distance)
    flat_got = swap(flat, "z", z_steps[-1])
    half = SLOTS // 2
    core = lax.axis_index("c")
    finals = [fixed(after(result, pair)), fixed(after(grad_hidden + grad_source, pair))]
    got = [swap(lax.dynamic_slice_in_dim(v, core * half, half, axis=0), "x") for v in finals]
    is_wide = (position == owners[4]) | (position == owners[5])
    pair_values = pair.astype(F32)
    norm = jnp.where(is_wide, jnp.trace(gram), jnp.sum(pair_values * pair_values))
    factor = 1.0 / (jnp.sqrt(norm) + 1e-07)
    orth = newton(is_wide, factor, gram, jnp.where(is_wide, wide, pair))
    got, flat, flat_got, back_sent = lax.optimization_barrier((got, flat, flat_got, orth))
    back = lax.all_to_all(
        back_sent.reshape(groups, rows_each, units_each),
        ("z", "y"),
        split_axis=0,
        concat_axis=0,
        tiled=True,
    ).astype(F32)
    flat = (flat + flat_got).reshape(-1)

    def both_bins(own, received):
        other = join(received, swap(received, "c"), bit_of("c"), 0).reshape(own.shape)
        return join(own, other, bit_of("x"), 0).reshape(-1, D).astype(F32)

    block_out, input_grad = (both_bins(own, r) for own, r in zip(finals, got))
    ends = [sum(sizes[: k + 1]) for k in range(4)]
    pieces = [flat[end - size : end] for end, size in zip(ends, sizes)]
    gains_sum = pieces[0].reshape(2, D)
    biases_sum = pieces[1].reshape(4, D)
    heads_sum = lax.dynamic_index_in_dim(
        pieces[2].reshape(2, 2, heads_each), x_index, 1, keepdims=False
    )
    units_sum = lax.dynamic_index_in_dim(pieces[3].reshape(2, units_each), x_index, 0, False)
    next_moments = (*narrow_nexts, *wide_nexts)
    returned = [back[owners[k]][:, : next_moments[k].shape[1]] for k in range(6)]
    keep_share = 1.0 - RATE * DECAY
    up_factor = math.sqrt(max(1.0, FF / D))
    qkv_next = qkv_weight.astype(F32) * keep_share - RATE * jnp.stack(returned[:3])
    out_next = out_weight.astype(F32) * keep_share - RATE * returned[3].T
    up_next = up_weight.astype(F32) * keep_share - RATE * up_factor * returned[4]
    down_next = down_weight.astype(F32) * keep_share - RATE * returned[5].T
    rate_vector = VECTOR_RATE / math.sqrt(groups * tokens.shape[0])
    gain_moment_next = MOMENTUM * gain_moment + gains_sum
    bias_moment_next = MOMENTUM * bias_moment + biases_sum
    head_moment_next = MOMENTUM * head_moment + heads_sum
    unit_moment_next = MOMENTUM * unit_moment + units_sum
    gain_next = norm_gains - rate_vector * gain_moment_next
    bias_next = shared_biases - rate_vector * bias_moment_next
    head_next = head_biases - rate_vector * head_moment_next
    unit_next = unit_bias - rate_vector * unit_moment_next
    return (
        block_out,
        input_grad,
        jnp.stack(next_moments[:3]),
        qkv_next,
        next_moments[3].T,
        out_next,
        next_moments[4],
        up_next,
        next_moments[5].T,
        down_next,
        gain_moment_next,
        gain_next,
        bias_moment_next,
        bias_next,
        head_moment_next,
        head_next,
        unit_moment_next,
        unit_next,
    )


def solution(mesh):
    dp_size, mp_size = mesh.devices.shape
    split = Mesh(
        mesh.devices.reshape(dp_size // 2, 2, mp_size // 2, 2), ("z", "y", "x", "c")
    )
    dp, mp = ("z", "y"), ("x", "c")
    in_specs = (
        P(dp, None),
        P(dp, None),
        P(),
        P(),
        P(None, dp, mp),
        P(mp, dp),
        P(dp, mp),
        P(mp, dp),
        P(),
        P(),
        P(None, mp),
        P(mp),
        P(None, dp, mp),
        P(mp, dp),
        P(dp, mp),
        P(mp, dp),
        P(),
        P(),
        P(None, mp),
        P(mp),
    )
    out_specs = (
        P(dp, None),
        P(dp, None),
        P(None, dp, mp),
        P(None, dp, mp),
        P(mp, dp),
        P(mp, dp),
        P(dp, mp),
        P(dp, mp),
        P(mp, dp),
        P(mp, dp),
        P(),
        P(),
        P(),
        P(),
        P(None, mp),
        P(None, mp),
        P(mp),
        P(mp),
    )
    return jax.shard_map(
        on_device, mesh=split, in_specs=in_specs, out_specs=out_specs, check_vma=False
    )
```
